32 devices in a mesh: dp: 4 (over y, core), fsdp: 8 (over z, x).
Axes of the slice: x: 2, y: 2, z: 4, core: 2. Of those that a mesh axis runs over, the one named last changes fastest.
Arguments:
- tokens: bfloat16 [33024, 1024], P(('dp', 'fsdp')), may hold values from -6 to 6
- frame_ids: int32 [33024], P(('dp', 'fsdp')), may hold values from 0 to 3, as said below
- pad_mask: int32 [33024], P(('dp', 'fsdp')), may hold values from 0 to 1, as said below
- episode_offsets: int32 [32, 3], P(('dp', 'fsdp')), may hold values from 0 to 4, as said below
- ln1_gain: bfloat16 [1024], P(('dp', 'fsdp')), may hold values from 0.5 to 1.5
- ln1_bias: bfloat16 [1024], P(('dp', 'fsdp')), may hold values from -4 to 4
- w_qkv: bfloat16 [1024, 3072], P(('dp', 'fsdp')), may hold values from -0.1875 to 0.1875
- b_qkv: bfloat16 [3, 1024], P(None, ('dp', 'fsdp')), may hold values from -4 to 4
- w_out: bfloat16 [1024, 1024], P(('dp', 'fsdp')), may hold values from -0.75 to 0.75
- b_out: bfloat16 [1024], P(('dp', 'fsdp')), may hold values from -4 to 4
- ln2_gain: bfloat16 [1024], P(('dp', 'fsdp')), may hold values from 0.5 to 1.5
- ln2_bias: bfloat16 [1024], P(('dp', 'fsdp')), may hold values from -4 to 4
- w_up: bfloat16 [1024, 4096], P(('dp', 'fsdp')), may hold values from -0.1875 to 0.1875
- b_up: bfloat16 [4096], P(('dp', 'fsdp')), may hold values from -4 to 4
- w_down: bfloat16 [4096, 1024], P(('dp', 'fsdp')), may hold values from -0.09375 to 0.09375
- b_down: bfloat16 [1024], P(('dp', 'fsdp')), may hold values from -4 to 4
- cotangent: bfloat16 [33024, 1024], P(('dp', 'fsdp')), may hold values from -6 to 6
Outputs:
- output: bfloat16 [33024, 1024], P(('dp', 'fsdp'))
- grad_tokens: float32 [33024, 1024], P(('dp', 'fsdp'))
- grad_ln1_gain: float32 [1024], P(('dp', 'fsdp'))
- grad_ln1_bias: float32 [1024], P(('dp', 'fsdp'))
- grad_w_qkv: float32 [1024, 3072], P(('dp', 'fsdp'))
- grad_b_qkv: float32 [3, 1024], P(None, ('dp', 'fsdp'))
- grad_w_out: float32 [1024, 1024], P(('dp', 'fsdp'))
- grad_b_out: float32 [1024], P(('dp', 'fsdp'))
- grad_ln2_gain: float32 [1024], P(('dp', 'fsdp'))
- grad_ln2_bias: float32 [1024], P(('dp', 'fsdp'))
- grad_w_up: float32 [1024, 4096], P(('dp', 'fsdp'))
- grad_b_up: float32 [4096], P(('dp', 'fsdp'))
- grad_w_down: float32 [4096, 1024], P(('dp', 'fsdp'))
- grad_b_down: float32 [1024], P(('dp', 'fsdp'))
The draws below stay inside these ranges and needn't reach their ends.
Inputs may be any that keep to these rules, and one draw needn't show every extreme that they name: `episode_offsets`: row r holds 0, the frames of the first episode of device r (1 or more), and the frames used by its one or two episodes (at most 4); in every draw some device holds one episode of 4 frames; lengths are heavy-tailed toward short episodes. `frame_ids`: equal over the 258 rows of a frame; counts frames from the start of the frame's episode, and on padding frames from the end of the used ones. `pad_mask`: 1 exactly on the rows of the used frames given by episode_offsets.
All inputs are finite; a program needn't handle non-finite values.
Results may differ from the reference program's by a relative error of at most 0.0073.
Values may be sent and summed in bfloat16 or wider, within the bound.
No kernel may reach another device: no remote copies, remote signals or barrier semaphores. Data moves between devices by JAX's collectives and lax.ppermute only.
A program may use at most 384 MiB of HBM per device.

```python
import math
import jax
import jax.numpy as jnp
from jax import lax

D = 1024
HEAD = 64
FF = 4096
GRID = 16
FRAME_ROWS = 258
FR_DEV = 4
TOK_DEV = 1032
MEMBERS = 32
TOKENS = 33024


def episode_plan(key):
    base_key = jax.random.fold_in(key, 11)
    first_key, second_key, third_key, fourth_key = jax.random.split(base_key, 4)
    first_draw = jax.random.randint(first_key, (MEMBERS,), 1, FR_DEV + 1)
    second_draw = jax.random.randint(second_key, (MEMBERS,), 1, FR_DEV + 1)
    first_len = jnp.minimum(first_draw, second_draw)
    longest = jax.random.randint(third_key, (), 0, MEMBERS)
    members_index = jnp.arange(MEMBERS, dtype=jnp.int32)
    first_len = jnp.where(members_index == longest, FR_DEV, first_len).astype(jnp.int32)
    room_left = FR_DEV - first_len
    second_len = jax.random.randint(fourth_key, (MEMBERS,), 0, room_left + 1).astype(jnp.int32)
    return (first_len, second_len)


def frame_layout(key):
    first_len, second_len = episode_plan(key)
    used_len = (first_len + second_len)[:, None]
    frame_index = jnp.arange(FR_DEV, dtype=jnp.int32)[None, :]
    first_col = first_len[:, None]
    frame_time = jnp.where(frame_index < first_col, frame_index, jnp.where(frame_index < used_len, frame_index - first_col, frame_index - used_len))
    frame_live = (frame_index < used_len).astype(jnp.int32)
    return (frame_time.astype(jnp.int32), frame_live)


def draw_episode_offsets(key, part):
    first_len, second_len = episode_plan(key)
    zeros_col = jnp.zeros((MEMBERS,), jnp.int32)
    return jnp.stack([zeros_col, first_len, first_len + second_len], axis=1).astype(jnp.int32)


def draw_frame_ids(key, part):
    frame_time, frame_live = frame_layout(key)
    return jnp.repeat(frame_time, FRAME_ROWS, axis=1).reshape(TOKENS).astype(jnp.int32)


def draw_pad_mask(key, part):
    frame_time, frame_live = frame_layout(key)
    return jnp.repeat(frame_live, FRAME_ROWS, axis=1).reshape(TOKENS).astype(jnp.int32)


def block_levels(key, shape, cuts, least, high):
    factor_of, own = 1.0, jax.random.fold_in(key, 6)
    for axis_at, blocks in cuts:
        draws = jnp.exp(jax.random.uniform(jax.random.fold_in(own, axis_at), (blocks,), jnp.float32, least / len(cuts), high / len(cuts)))
        factor_of = factor_of * jnp.repeat(draws, shape[axis_at] // blocks).reshape([-1 if axis == axis_at else 1 for axis in range(len(shape))])
    return factor_of


def bell_draw(rng, extent, spread, limit, cuts=(), kind=jnp.bfloat16):
    factor_of = block_levels(rng, extent, cuts, -0.22, 0.18) if cuts else 1.0
    entries = jax.random.normal(rng, extent, jnp.float32) * spread * factor_of
    return jnp.minimum(jnp.maximum(entries, -limit), limit).astype(kind)


def setup_inputs(seed: int = 0) -> dict:
    arg_keys = jax.random.split(jax.random.key(seed), 18)
    tokens = bell_draw(arg_keys[0], (TOKENS, D), 1.0, 6.0, ((0, 32),))
    frame_ids = draw_frame_ids(jax.random.fold_in(arg_keys[17], 71), 0)
    pad_mask = draw_pad_mask(jax.random.fold_in(arg_keys[17], 71), 0)
    episode_offsets = draw_episode_offsets(jax.random.fold_in(arg_keys[17], 71), 0)
    ln1_gain = jnp.clip(1.0 + 0.1 * jax.random.normal(arg_keys[4], (D,), jnp.float32), 0.5, 1.5).astype(jnp.bfloat16)
    ln1_bias = bell_draw(arg_keys[5], (D,), 0.3, 4.0, ((0, 32),))
    w_qkv = bell_draw(arg_keys[6], (D, 3 * D), D ** -0.5, 0.1875, ((0, 32),))
    b_qkv = bell_draw(arg_keys[7], (3, D), 0.3, 4.0, ((1, 32),))
    w_out = bell_draw(arg_keys[8], (D, D), (D // 16) ** -0.5, 0.75, ((0, 32),))
    b_out = bell_draw(arg_keys[9], (D,), 0.3, 4.0, ((0, 32),))
    ln2_gain = jnp.clip(1.0 + 0.1 * jax.random.normal(arg_keys[10], (D,), jnp.float32), 0.5, 1.5).astype(jnp.bfloat16)
    ln2_bias = bell_draw(arg_keys[11], (D,), 0.3, 4.0, ((0, 32),))
    w_up = bell_draw(arg_keys[12], (D, FF), D ** -0.5, 0.1875, ((0, 32),))
    b_up = bell_draw(arg_keys[13], (FF,), 0.3, 4.0, ((0, 32),))
    w_down = bell_draw(arg_keys[14], (FF, D), FF ** -0.5, 0.09375, ((0, 32),))
    b_down = bell_draw(arg_keys[15], (D,), 0.3, 4.0, ((0, 32),))
    cotangent = bell_draw(arg_keys[16], (TOKENS, D), 1.0, 6.0, ((0, 32),))
    return dict(tokens=tokens, frame_ids=frame_ids, pad_mask=pad_mask, episode_offsets=episode_offsets, ln1_gain=ln1_gain, ln1_bias=ln1_bias, w_qkv=w_qkv, b_qkv=b_qkv, w_out=w_out, b_out=b_out, ln2_gain=ln2_gain, ln2_bias=ln2_bias, w_up=w_up, b_up=b_up, w_down=w_down, b_down=b_down, cotangent=cotangent)


eps_norm = 1e-06
part_sizes = (24, 20, 20)
masked_value = -1e+30

@jax.custom_vjp
def low(v):
    return lax.optimization_barrier(v.astype(jnp.bfloat16)).astype(jnp.float32)

@jax.custom_vjp
def low_back(v):
    return v

def low_keep(v):
    return (low(v), None)

def low_pass(kept, grad):
    return (grad,)

def back_keep(v):
    return (v, None)

def back_low(kept, grad):
    return (low(grad),)
low.defvjp(low_keep, low_pass)
low_back.defvjp(back_keep, back_low)

def rope_tables(frame_ids, rows_count):
    row_index = jnp.arange(rows_count, dtype=jnp.int32) % FRAME_ROWS
    patch_index = jnp.maximum(row_index - 2, 0)
    height = jnp.where(row_index >= 2, patch_index // GRID, 0)
    breadth = jnp.where(row_index >= 2, patch_index % GRID, 0)
    cosine_parts = []
    sine_parts = []
    for position, part_size in zip((frame_ids, height, breadth), part_sizes):
        half_size = part_size // 2
        frequency = 10000.0 ** (-jnp.arange(half_size).astype(jnp.float32) / half_size)
        angles = position.astype(jnp.float32)[:, None] * frequency[None, :]
        cosine_parts.append(jnp.cos(angles))
        sine_parts.append(jnp.sin(angles))
    return (jnp.concatenate(cosine_parts, 1)[:, None, :], jnp.concatenate(sine_parts, 1)[:, None, :])

def rotate(vectors, cosine, sine_table):
    pieces = []
    offset_at = 0
    slot_at = 0
    for part_size in part_sizes:
        half_size = part_size // 2
        first_half = vectors[..., offset_at:offset_at + half_size]
        second_half = vectors[..., offset_at + half_size:offset_at + part_size]
        cosine_part = cosine[..., slot_at:slot_at + half_size]
        sine_part = sine_table[..., slot_at:slot_at + half_size]
        pieces.append(first_half * cosine_part - second_half * sine_part)
        pieces.append(second_half * cosine_part + first_half * sine_part)
        offset_at = offset_at + part_size
        slot_at = slot_at + half_size
    return jnp.concatenate(pieces, axis=-1)

def normalize(values, gain, bias_add):
    center = values - lax.optimization_barrier(jnp.mean(values, axis=-1, keepdims=True))
    scale_inv = lax.rsqrt(lax.optimization_barrier(jnp.mean(center * center, axis=-1, keepdims=True)) + eps_norm)
    unit_rows = center * scale_inv
    return (unit_rows * gain + bias_add, unit_rows, scale_inv)

def visibility(frame_ids, pad_mask, offset_row, query_lo, query_hi, key_hi):
    frame_of = jnp.arange(key_hi, dtype=jnp.int32) // FRAME_ROWS
    episode = (frame_of >= offset_row[1]).astype(jnp.int32) + (frame_of >= offset_row[2]).astype(jnp.int32)
    same_episode = episode[query_lo:query_hi][:, None] == episode[None, :]
    earlier = frame_ids[None, :key_hi] <= frame_ids[query_lo:query_hi][:, None]
    rows_query = jnp.arange(query_lo, query_hi, dtype=jnp.int32)
    rows_key = jnp.arange(key_hi, dtype=jnp.int32)
    live = (pad_mask[None, :key_hi] > 0) | (rows_query[:, None] == rows_key[None, :])
    return same_episode & earlier & live

def block_forward(params, values, frame_ids, pad_mask, offset_row):
    ln1_gain, ln1_bias, w_qkv, b_qkv, w_out, b_out, ln2_gain, ln2_bias, w_up, b_up, w_down, b_down = params
    highest = lax.Precision.HIGHEST
    rows_count = values.shape[0]
    width = w_qkv.shape[0]
    heads_count = width // HEAD
    normed_one = low(normalize(values, ln1_gain, ln1_bias)[0])
    mixed = low_back(jnp.dot(normed_one, w_qkv, precision=highest) + b_qkv.reshape(3 * width))
    cosine, sine_table = rope_tables(frame_ids, rows_count)
    query = low(rotate(mixed[:, :width].reshape(rows_count, heads_count, HEAD), cosine, sine_table))
    key_rows = low(rotate(mixed[:, width:2 * width].reshape(rows_count, heads_count, HEAD), cosine, sine_table))
    value_rows = low(mixed[:, 2 * width:].reshape(rows_count, heads_count, HEAD))
    score_scale = 1.0 / math.sqrt(HEAD)
    scores = low_back(jnp.einsum('qhd,khd->hqk', query, key_rows, precision=highest) * score_scale)
    allowed = visibility(frame_ids, pad_mask, offset_row, 0, rows_count, rows_count)
    scores = jnp.where(allowed[None], scores, masked_value)
    top_score = lax.optimization_barrier(jnp.max(scores, axis=-1, keepdims=True))
    exponent = jnp.exp(scores - top_score)
    probability = low(exponent / lax.optimization_barrier(jnp.sum(exponent, axis=-1, keepdims=True)))
    attended = jnp.einsum('hqk,khd->qhd', probability, value_rows, precision=highest).reshape(rows_count, width)
    attended = low(low_back(attended))
    branch = low_back(jnp.dot(attended, w_out, precision=highest) + b_out)
    middle = values + branch
    normed_two = low(normalize(middle, ln2_gain, ln2_bias)[0])
    upward = low_back(jnp.dot(normed_two, w_up, precision=highest) + b_up)
    activated = low(jax.nn.gelu(upward, approximate=False))
    down_rows = low_back(jnp.dot(activated, w_down, precision=highest) + b_down)
    return middle + down_rows

def reference(tokens, frame_ids, pad_mask, episode_offsets, ln1_gain, ln1_bias, w_qkv, b_qkv, w_out, b_out, ln2_gain, ln2_bias, w_up, b_up, w_down, b_down, cotangent):
    params = tuple((item.astype(jnp.float32) for item in (ln1_gain, ln1_bias, w_qkv, b_qkv, w_out, b_out, ln2_gain, ln2_bias, w_up, b_up, w_down, b_down)))
    values = tokens.astype(jnp.float32).reshape(MEMBERS, TOK_DEV, D)
    frames_all = frame_ids.reshape(MEMBERS, TOK_DEV)
    masks_all = pad_mask.reshape(MEMBERS, TOK_DEV)

    def forward(params_in, values_in):

        def one_block(items):
            return block_forward(params_in, items[0], items[1], items[2], items[3])
        return lax.map(jax.checkpoint(one_block), (values_in, frames_all, masks_all, episode_offsets))
    outputs, pullback = jax.vjp(forward, params, values)
    grads_params, grad_values = pullback(cotangent.astype(jnp.float32).reshape(MEMBERS, TOK_DEV, D))
    output = outputs.reshape(TOKENS, D).astype(jnp.bfloat16)
    grad_tokens = grad_values.reshape(TOKENS, D)
    return (output, grad_tokens, grads_params[0], grads_params[1], grads_params[2], grads_params[3], grads_params[4], grads_params[5], grads_params[6], grads_params[7], grads_params[8], grads_params[9], grads_params[10], grads_params[11])
```

```python
import functools
import math

import jax
import jax.numpy as jnp
import numpy as np
from jax import lax
from jax.experimental import pallas as pl
from jax.experimental.pallas import tpu as pltpu
from jax.sharding import PartitionSpec as P

HEAD = 64
GRID = 16
FRAME_ROWS = 258
FRAMES = 4
PATCH = GRID * GRID
EXTRA = 16
FEW = 8
BODY = FRAMES * PATCH
ROWS = BODY + EXTRA
eps_norm = 1e-06
part_sizes = (24, 20, 20)
masked_value = -1e30
inv_sqrt_two = 1.0 / math.sqrt(2.0)
inv_sqrt_tau = 1.0 / math.sqrt(2.0 * math.pi)
f32 = jnp.float32
bf16 = jnp.bfloat16
vmem_most = 60 * 1024 * 1024


def log2(n):
    return n.bit_length() - 1


def swap(value, bit, sizes):
    count = sizes[0] * sizes[1]
    pairs = [(i, i ^ (1 << bit)) for i in range(count)]
    return lax.ppermute(value, ("dp", "fsdp"), pairs)


def bit_orders(sizes):
    inner, outer = log2(sizes[1]), log2(sizes[0])
    core = inner
    line = list(range(1, inner))
    cross = [0]
    other = list(range(inner + 1, inner + outer))
    return core, line + cross + other, line + other + cross


def gather_pieces(shard, order, core, sizes):
    held = shard[None]
    rel = [0]
    for bit in order[:-1]:
        held = jnp.concatenate([held, swap(held, bit, sizes)], axis=0)
        rel = rel + [p | (1 << bit) for p in rel]
    last = order[-1]
    pieces = [(held, rel), (swap(held, last, sizes), [p | (1 << last) for p in rel])]
    pieces += [(swap(v, core, sizes), [p | (1 << core) for p in q]) for v, q in pieces]
    return pieces


def assemble_kernel(rels, rows, me_ref, *refs):
    pieces, out, sem = refs[: len(rels)], refs[len(rels)], refs[len(rels) + 1]
    me = me_ref[0]
    copies = []
    for piece, rel in zip(pieces, rels):
        for at, p in enumerate(rel):
            owner = lax.bitwise_xor(me, p)
            start = pl.multiple_of(owner * rows, rows)
            copies.append(pltpu.make_async_copy(piece.at[at], out.at[pl.ds(start, rows)], sem))
    for copy in copies:
        copy.start()
    pltpu.make_async_copy(out, out, sem).wait()


def assemble(pieces, me):
    rels = [q for _, q in pieces]
    count = sum(len(q) for q in rels)
    _, rows, cols = pieces[0][0].shape
    return pl.pallas_call(
        functools.partial(assemble_kernel, rels, rows),
        out_shape=jax.ShapeDtypeStruct((count * rows, cols), pieces[0][0].dtype),
        in_specs=[pl.BlockSpec(memory_space=pltpu.SMEM)]
        + [pl.BlockSpec(memory_space=pl.ANY)] * len(pieces),
        scratch_shapes=[pltpu.SemaphoreType.DMA],
        compiler_params=pltpu.CompilerParams(vmem_limit_bytes=vmem_most),
        cost_estimate=pl.CostEstimate(
            flops=0, bytes_accessed=4 * count * rows * cols, transcendentals=0
        ),
    )(me, *[v for v, _ in pieces])


def split_kernel(rels, rows, me_ref, whole, *refs):
    outs, sem = refs[: len(rels)], refs[len(rels)]
    me = me_ref[0]
    copies = []
    for piece, rel in zip(outs, rels):
        for at, p in enumerate(rel):
            owner = lax.bitwise_xor(me, p)
            start = pl.multiple_of(owner * rows, rows)
            copies.append(pltpu.make_async_copy(whole.at[pl.ds(start, rows)], piece.at[at], sem))
    for copy in copies:
        copy.start()
    pltpu.make_async_copy(whole, whole, sem).wait()


def relatives(order, core):
    rel = [0]
    for bit in order:
        rel = rel + [p | (1 << bit) for p in rel]
    return rel, [p | (1 << core) for p in rel]


def split(whole, order, core, me):
    own, other = relatives(order, core)
    rows = whole.shape[0] // (2 * len(own))
    return pl.pallas_call(
        functools.partial(split_kernel, (own, other), rows),
        out_shape=(jax.ShapeDtypeStruct((len(own), rows, whole.shape[1]), whole.dtype),) * 2,
        in_specs=[
            pl.BlockSpec(memory_space=pltpu.SMEM),
            pl.BlockSpec(memory_space=pltpu.VMEM),
        ],
        out_specs=(pl.BlockSpec(memory_space=pl.ANY),) * 2,
        scratch_shapes=[pltpu.SemaphoreType.DMA],
        compiler_params=pltpu.CompilerParams(vmem_limit_bytes=vmem_most),
        cost_estimate=pl.CostEstimate(flops=0, bytes_accessed=4 * whole.size, transcendentals=0),
    )(me, whole)


def reduce_pieces(own, other, order, core, sizes):
    kind = own.dtype
    taken = swap(other, core, sizes)
    kept = own
    for bit in reversed(order):
        half = kept.shape[0] // 2
        total = kept.astype(f32) + taken.astype(f32)
        sent = total[half:].astype(kind)
        kept = total[:half].astype(kind)
        taken = swap(sent, bit, sizes)
    return (kept.astype(f32) + taken.astype(f32))[0]


def gather_small(parts):
    flat = jnp.concatenate([v.reshape(-1) for v in parts])
    lines = -(-flat.size // (16 * 128)) * 16
    flat = jnp.pad(flat, (0, lines * 128 - flat.size)).reshape(lines, 128)
    whole = lax.all_gather(flat, ("dp", "fsdp"), axis=0, tiled=True).reshape(-1, lines * 128)
    found, at = [], 0
    for v in parts:
        block = whole[:, at : at + v.size]
        if v.ndim == 2:
            block = block.reshape(-1, v.shape[0], v.shape[1]).swapaxes(0, 1)
            found.append(block.reshape(v.shape[0], -1))
        else:
            found.append(block.reshape(-1))
        at = at + v.size
    return found


def reduce_small(parts, order, core, sizes, me):
    count = sizes[0] * sizes[1]
    rows = [
        v.reshape(count, -1)
        if v.ndim == 1
        else v.reshape(v.shape[0], count, -1).swapaxes(0, 1).reshape(count, -1)
        for v in parts
    ]
    flat = jnp.concatenate(rows, axis=1)
    own, other = relatives(order, core)
    index = lax.bitwise_xor(jnp.asarray(own + other, jnp.int32), me[0])
    mixed = jnp.take(flat, index, axis=0)
    total = reduce_pieces(
        mixed[: len(own), None], mixed[len(own) :, None], order, core, sizes
    )[0]
    found, at = [], 0
    for v, row in zip(parts, rows):
        block = total[at : at + row.shape[1]]
        found.append(block if v.ndim == 1 else block.reshape(v.shape[0], -1))
        at = at + row.shape[1]
    return found


def dot_t(a, b):
    return lax.dot_general(a, b, (((1,), (1,)), ((), ())), preferred_element_type=f32)


def dot_n(a, b):
    return lax.dot_general(a, b, (((1,), (0,)), ((), ())), preferred_element_type=f32)


def dot_tl(a, b):
    return lax.dot_general(a, b, (((0,), (0,)), ((), ())), preferred_element_type=f32)


def head_lanes(a, rows):
    lane = lax.broadcasted_iota(jnp.int32, (rows, 2 * HEAD), 1)
    return (lane >= HEAD) if a else (lane < HEAD)


def keep_head(x, a):
    return jnp.where(head_lanes(a, x.shape[0]), x, jnp.zeros_like(x))


def stack_heads(x):
    return jnp.concatenate([keep_head(x, 0), keep_head(x, 1)], axis=0)


def join_heads(x):
    return jnp.where(head_lanes(0, FEW), x[:FEW], x[FEW:])


def few_rows(x):
    return jnp.concatenate([x, jnp.zeros_like(x)], axis=0)


def hide_few(s, first, last):
    row = lax.broadcasted_iota(jnp.int32, (EXTRA, s.shape[1]), 0)
    frame = lax.shift_right_logical(row, 1)
    seen = (frame >= first) & (frame <= last)
    count = s.shape[0] - EXTRA
    return jnp.concatenate([s[:count], jnp.where(seen, s[count:], masked_value)], axis=0)


def seen_rows(ref, lo, n):
    return jnp.concatenate([ref[pl.ds(lo, n * PATCH), :], ref[BODY:ROWS, :]], axis=0)


def seen_lanes(ref, a, lo, n):
    return jnp.concatenate(
        [ref[a * HEAD : (a + 1) * HEAD, pl.ds(lo, n * PATCH)], ref[a * HEAD : (a + 1) * HEAD, BODY:ROWS]],
        axis=1,
    )


def attend_kernel(seen_ref, q_ref, k_ref, v_ref, hide_ref, out_ref, lse_ref, few_ref, vt):
    f = pl.program_id(1)

    @pl.when(f == 0)
    def _():
        vt[...] = v_ref[...].T
        qs = stack_heads(q_ref[BODY:ROWS, :].astype(f32)[:FEW]).astype(bf16)
        s = dot_t(k_ref[...], qs) + hide_ref[...]
        top = jnp.max(s, axis=0, keepdims=True)
        p = jnp.exp(s - top)
        total = jnp.sum(p, axis=0, keepdims=True)
        o = dot_tl((p / total).astype(bf16), v_ref[...])
        out_ref[BODY:ROWS, :] = few_rows(join_heads(o)).astype(bf16)
        few_ref[0] = top + jnp.log(total)

    row = pl.multiple_of(f * PATCH, PATCH)
    seen = seen_ref[f]

    @pl.when(seen == 0)
    def _():
        out_ref[pl.ds(row, PATCH), :] = v_ref[pl.ds(row, PATCH), :]
        lse_ref[0, :, pl.ds(row, PATCH)] = jnp.zeros((2, PATCH), f32)

    for n in range(1, FRAMES + 1):

        @pl.when(seen == n)
        def _(n=n):
            first = f - (n - 1)
            lo = pl.multiple_of(first * PATCH, PATCH)
            keys = seen_rows(k_ref, lo, n)
            q = q_ref[pl.ds(row, PATCH), :]
            outs, sums = [], []
            for a in range(2):
                s = hide_few(dot_t(keys, keep_head(q, a)), first, f)
                top = jnp.max(s, axis=0, keepdims=True)
                p = jnp.exp(s - top)
                total = jnp.sum(p, axis=0, keepdims=True)
                o = dot_n(seen_lanes(vt, a, lo, n), p.astype(bf16))
                outs.append(o / total)
                sums.append(top + jnp.log(total))
            out_ref[pl.ds(row, PATCH), :] = jnp.concatenate(outs, axis=0).T.astype(bf16)
            lse_ref[0, :, pl.ds(row, PATCH)] = jnp.concatenate(sums, axis=0)


def attend(seen, qkv, hide):
    width = qkv.shape[1] // 3
    pairs = width // (2 * HEAD)
    lanes = 2 * HEAD
    return pl.pallas_call(
        attend_kernel,
        grid_spec=pltpu.PrefetchScalarGridSpec(
            num_scalar_prefetch=1,
            grid=(pairs, FRAMES),
            in_specs=[
                pl.BlockSpec((ROWS, lanes), lambda h, f, s: (0, h)),
                pl.BlockSpec((ROWS, lanes), lambda h, f, s: (0, pairs + h)),
                pl.BlockSpec((ROWS, lanes), lambda h, f, s: (0, 2 * pairs + h)),
                pl.BlockSpec((ROWS, 2 * FEW), lambda h, f, s: (0, 0)),
            ],
            out_specs=[
                pl.BlockSpec((ROWS, lanes), lambda h, f, s: (0, h)),
                pl.BlockSpec((1, 2, BODY), lambda h, f, s: (h, 0, 0)),
                pl.BlockSpec((1, 1, 2 * FEW), lambda h, f, s: (h, 0, 0)),
            ],
            scratch_shapes=[pltpu.VMEM((lanes, ROWS), bf16)],
        ),
        out_shape=(
            jax.ShapeDtypeStruct((ROWS, width), bf16),
            jax.ShapeDtypeStruct((pairs, 2, BODY), f32),
            jax.ShapeDtypeStruct((pairs, 1, 2 * FEW), f32),
        ),
        compiler_params=pltpu.CompilerParams(vmem_limit_bytes=vmem_most),
        cost_estimate=pl.CostEstimate(
            flops=ROWS * ROWS * width * 4, bytes_accessed=8 * ROWS * width, transcendentals=0
        ),
    )(seen, qkv, qkv, qkv, hide)


def unturn(x, cosine, sine, partner):
    return x * cosine - dot_n(x.astype(bf16), partner) * sine


def attend_back_kernel(
    scale, seen_ref, q_ref, k_ref, v_ref, o_ref, g_ref, lse_ref, few_ref, hide_ref, cos_ref, sin_ref,
    part_ref, out_ref, kt, dq, dk, dv,
):
    f = pl.program_id(1)
    ones = jnp.where(
        (lax.broadcasted_iota(jnp.int32, (8, 2 * HEAD), 1) >= HEAD).astype(jnp.int32)
        == lax.broadcasted_iota(jnp.int32, (8, 2 * HEAD), 0),
        1.0,
        0.0,
    ).astype(bf16)

    @pl.when(f == 0)
    def _():
        kt[...] = k_ref[...].T
        qs = stack_heads(q_ref[BODY:ROWS, :].astype(f32)[:FEW]).astype(bf16)
        gs = stack_heads(g_ref[BODY:ROWS, :].astype(f32)[:FEW])
        os = stack_heads(o_ref[BODY:ROWS, :].astype(f32)[:FEW])
        p = jnp.exp(dot_t(k_ref[...], qs) + hide_ref[...] - few_ref[0])
        gp = dot_t(v_ref[...], gs.astype(bf16))
        delta = jnp.sum(gp * p, axis=0, keepdims=True)
        ds = (p * (gp - delta)).astype(bf16)
        dv[...] = dot_n(p.astype(bf16), gs.astype(bf16))
        dk[...] = dot_n(ds, qs)
        dq[BODY:ROWS, :] = few_rows(join_heads(dot_tl(ds, k_ref[...])))

    row = pl.multiple_of(f * PATCH, PATCH)
    seen = seen_ref[f]

    @pl.when(seen == 0)
    def _():
        dv[pl.ds(row, PATCH), :] += g_ref[pl.ds(row, PATCH), :].astype(f32)
        dq[pl.ds(row, PATCH), :] = jnp.zeros((PATCH, 2 * HEAD), f32)

    for n in range(1, FRAMES + 1):

        @pl.when(seen == n)
        def _(n=n):
            first = f - (n - 1)
            lo = pl.multiple_of(first * PATCH, PATCH)
            keys = seen_rows(k_ref, lo, n)
            values = seen_rows(v_ref, lo, n)
            q = q_ref[pl.ds(row, PATCH), :]
            g = g_ref[pl.ds(row, PATCH), :]
            product = g.astype(f32) * o_ref[pl.ds(row, PATCH), :].astype(f32)
            upper = product.astype(bf16)
            lower = (product - upper.astype(f32)).astype(bf16)
            deltas = dot_t(ones, upper) + dot_t(ones, lower)
            back, add_k, add_v = [], None, None
            for a in range(2):
                qm, gm = keep_head(q, a), keep_head(g, a)
                s = hide_few(dot_t(keys, qm), first, f)
                p = jnp.exp(s - lse_ref[0, a : a + 1, pl.ds(row, PATCH)])
                gp = dot_t(values, gm)
                ds = (p * (gp - deltas[a : a + 1])).astype(bf16)
                more_v, more_k = dot_n(p.astype(bf16), gm), dot_n(ds, qm)
                add_v = more_v if add_v is None else add_v + more_v
                add_k = more_k if add_k is None else add_k + more_k
                back.append(dot_n(seen_lanes(kt, a, lo, n), ds))
            dq[pl.ds(row, PATCH), :] = jnp.concatenate(back, axis=0).T
            count = n * PATCH
            dk[pl.ds(lo, count), :] += add_k[:count]
            dk[BODY:ROWS, :] += add_k[count:]
            dv[pl.ds(lo, count), :] += add_v[:count]
            dv[BODY:ROWS, :] += add_v[count:]

    @pl.when(f == FRAMES - 1)
    def _():
        partner = part_ref[...]
        out_ref[0] = unturn(dq[...] * scale, cos_ref[...], sin_ref[...], partner).astype(bf16)
        out_ref[1] = unturn(dk[...], cos_ref[...], sin_ref[...], partner).astype(bf16)
        out_ref[2] = dv[...].astype(bf16)


def attend_back(seen, qkv, attended, grad, lse, few, hide, cosine, sine, partner, pair_lo, pair_hi):
    width = qkv.shape[1] // 3
    pairs = width // (2 * HEAD)
    lanes = 2 * HEAD
    at = pair_lo

    def whole(h, f, s):
        return (0, 0)

    return pl.pallas_call(
        functools.partial(attend_back_kernel, 1.0 / math.sqrt(HEAD)),
        grid_spec=pltpu.PrefetchScalarGridSpec(
            num_scalar_prefetch=1,
            grid=(pair_hi - pair_lo, FRAMES),
            in_specs=[
                pl.BlockSpec((ROWS, lanes), lambda h, f, s: (0, at + h)),
                pl.BlockSpec((ROWS, lanes), lambda h, f, s: (0, at + pairs + h)),
                pl.BlockSpec((ROWS, lanes), lambda h, f, s: (0, at + 2 * pairs + h)),
                pl.BlockSpec((ROWS, lanes), lambda h, f, s: (0, at + h)),
                pl.BlockSpec((ROWS, lanes), lambda h, f, s: (0, at + h)),
                pl.BlockSpec((1, 2, BODY), lambda h, f, s: (at + h, 0, 0)),
                pl.BlockSpec((1, 1, 2 * FEW), lambda h, f, s: (at + h, 0, 0)),
                pl.BlockSpec((ROWS, 2 * FEW), whole),
                pl.BlockSpec((ROWS, lanes), whole),
                pl.BlockSpec((ROWS, lanes), whole),
                pl.BlockSpec((lanes, lanes), whole),
            ],
            out_specs=pl.BlockSpec((3, ROWS, lanes), lambda h, f, s: (0, 0, h)),
            scratch_shapes=[
                pltpu.VMEM((lanes, ROWS), bf16),
                pltpu.VMEM((ROWS, lanes), f32),
                pltpu.VMEM((ROWS, lanes), f32),
                pltpu.VMEM((ROWS, lanes), f32),
            ],
        ),
        out_shape=jax.ShapeDtypeStruct((3, ROWS, (pair_hi - pair_lo) * lanes), bf16),
        compiler_params=pltpu.CompilerParams(vmem_limit_bytes=vmem_most),
        cost_estimate=pl.CostEstimate(
            flops=ROWS * ROWS * width * 10, bytes_accessed=16 * ROWS * width, transcendentals=0
        ),
    )(seen, qkv, qkv, qkv, attended, grad, lse, few, hide, cosine, sine, partner)


def project_kernel(scale, x_ref, w_ref, b_ref, cos_ref, sin_ref, part_ref, out_ref):
    j = pl.program_id(0)
    third = pl.num_programs(0) // 3
    lanes = 2 * HEAD
    w = w_ref[...]
    mixed = dot_n(x_ref[...], w) + b_ref[...]

    @pl.when(j < 2 * third)
    def _():
        bias = jnp.broadcast_to(b_ref[...], (8, w.shape[1]))
        by = jnp.where(j < third, scale, 1.0)
        for h in range(w.shape[1] // lanes):
            at = slice(h * lanes, (h + 1) * lanes)
            turned = dot_n(w[:, at], part_ref[...]).astype(bf16)
            moved = dot_n(bias[:, at].astype(bf16), part_ref[...])[:1]
            other = dot_n(x_ref[...], turned) + moved
            out_ref[:, at] = ((mixed[:, at] * cos_ref[...] + other * sin_ref[...]) * by).astype(bf16)

    @pl.when(j >= 2 * third)
    def _():
        out_ref[...] = mixed.astype(bf16)


def project(x, w, bias, cosine, sine, partner):
    rows, width = x.shape
    cols = 256
    lanes = 2 * HEAD

    def whole(j):
        return (0, 0)

    return pl.pallas_call(
        functools.partial(project_kernel, 1.0 / math.sqrt(HEAD)),
        grid=(w.shape[1] // cols,),
        in_specs=[
            pl.BlockSpec((rows, width), whole),
            pl.BlockSpec((width, cols), lambda j: (0, j)),
            pl.BlockSpec((1, cols), lambda j: (0, j)),
            pl.BlockSpec((rows, lanes), whole),
            pl.BlockSpec((rows, lanes), whole),
            pl.BlockSpec((lanes, lanes), whole),
        ],
        out_specs=pl.BlockSpec((rows, cols), lambda j: (0, j)),
        out_shape=jax.ShapeDtypeStruct((rows, w.shape[1]), bf16),
        compiler_params=pltpu.CompilerParams(vmem_limit_bytes=vmem_most),
        cost_estimate=pl.CostEstimate(
            flops=3 * rows * w.size, bytes_accessed=2 * (x.size + w.size + 3 * x.size), transcendentals=0
        ),
    )(x, w, bias, cosine, sine, partner)


def turn_tables(frame_ids, rows_of):
    index = jnp.asarray(rows_of, jnp.int32)
    time = frame_ids[jnp.asarray([f * FRAME_ROWS for f in range(FRAMES)])]
    patch = jnp.maximum(index % FRAME_ROWS - 2, 0)
    height = patch // GRID
    breadth = patch % GRID
    time = jnp.repeat(time, PATCH)
    time = jnp.concatenate([time, jnp.repeat(time[::PATCH], 2), jnp.zeros((EXTRA - FEW,), jnp.int32)])
    cosine, sine = [], []
    for position, part in zip((time, height, breadth), part_sizes):
        half = part // 2
        frequency = 10000.0 ** (-jnp.arange(half).astype(f32) / half)
        angles = position.astype(f32)[:, None] * frequency[None, :]
        cosine += [jnp.cos(angles)] * 2
        sine += [-jnp.sin(angles), jnp.sin(angles)]
    return jnp.concatenate(cosine * 2, axis=1), jnp.concatenate(sine * 2, axis=1)


def partner_matrix():
    lanes = 2 * HEAD
    matrix = np.zeros((lanes, lanes), np.float32)
    for head in range(2):
        at = head * HEAD
        for part in part_sizes:
            for i in range(part // 2):
                matrix[at + i, at + i + part // 2] = 1.0
                matrix[at + i + part // 2, at + i] = 1.0
            at += part
    return jnp.asarray(matrix, bf16)


def seen_frames(offset_row):
    frame = jnp.arange(FRAMES, dtype=jnp.int32)
    start = jnp.where(frame >= offset_row[1], offset_row[1], 0)
    return jnp.where(frame < offset_row[2], frame - start + 1, 0)


def hidden_few(seen):
    frame_of = np.concatenate([np.repeat(np.arange(FRAMES), PATCH), np.repeat(np.arange(FRAMES), 2), np.full(EXTRA - FEW, FRAMES)])
    own = np.zeros((ROWS, FEW), bool)
    own[BODY + np.arange(FEW), np.arange(FEW)] = True
    frame = jnp.asarray(frame_of, jnp.int32)[:, None]
    query = jnp.arange(FEW, dtype=jnp.int32)[None, :] // 2
    count = jnp.repeat(seen, 2)[None, :]
    allowed = ((frame <= query) & (frame > query - count)) | jnp.asarray(own)
    return jnp.tile(jnp.where(allowed, 0.0, masked_value), (1, 2))


def row_order():
    patches = [f * FRAME_ROWS + 2 + j for f in range(FRAMES) for j in range(PATCH)]
    first = [f * FRAME_ROWS + j for f in range(FRAMES) for j in range(2)]
    return np.array(patches + first + [0] * (EXTRA - FEW))


def place(p, order, core):
    own, other = relatives(order, core)
    return (1, other.index(p)) if p in other else (0, own.index(p))


def find_piece(rels, p):
    for c, rel in enumerate(rels):
        if p in rel:
            return c, rel.index(p)
    raise ValueError(p)


def feed_kernel(
    up_rels, down_rels, up_order, down_order, core, me_ref, x_ref, g_ref, bias_ref, shift_ref, mid_ref, *refs
):
    n_up, n_down = len(up_rels), len(down_rels)
    up_refs, refs = refs[:n_up], refs[n_up:]
    down_refs, refs = refs[:n_down], refs[n_down:]
    out_ref, gx_ref, gb_ref = refs[:3]
    du_refs, dd_refs = refs[3:5], refs[5:7]
    wu, wd, su, sd, acc, xt, act, gup, in_sem, out_sem, mid_sem = refs[7:]
    count = sum(len(q) for q in up_rels)
    blocks = FEED_BLOCKS
    each = count // blocks
    shift = each.bit_length() - 1
    i = pl.program_id(0)
    me = me_ref[0]
    width = x_ref.shape[1]
    cols = wu.shape[2]
    rows = width // count
    part = cols // each
    slot = lax.rem(i, 2)

    def group(j):
        return lax.bitwise_xor(lax.shift_right_logical(me, shift), j)

    def fetch(j, to):
        at = pl.multiple_of(group(j) * cols, cols)
        for p in range(count):
            c, n = find_piece(up_rels, p)
            start = pl.multiple_of(lax.bitwise_xor(me, p) * rows, rows)
            pltpu.make_async_copy(
                up_refs[c].at[n, :, pl.ds(at, cols)], wu.at[to, pl.ds(start, rows), :], in_sem.at[0, to]
            ).start()
        for k in range(blocks):

            @pl.when(j == k)
            def _():
                for p in range(each):
                    c, n = find_piece(down_rels, (k << shift) | p)
                    start = pl.multiple_of(lax.bitwise_xor(me & (each - 1), p) * part, part)
                    pltpu.make_async_copy(
                        down_refs[c].at[n], wd.at[to, pl.ds(start, part), :], in_sem.at[1, to]
                    ).start()

    middle = pltpu.make_async_copy(mid_ref, acc, mid_sem)

    @pl.when(i == 0)
    def _():
        fetch(i, slot)
        middle.start()
        xt[...] = x_ref[...].T
        gx_ref[...] = jnp.zeros_like(gx_ref)

    @pl.when(i + 1 < blocks)
    def _():
        fetch(i + 1, 1 - slot)

    pltpu.make_async_copy(wu.at[slot], wu.at[slot], in_sem.at[0, slot]).wait()
    pltpu.make_async_copy(wd.at[slot], wd.at[slot], in_sem.at[1, slot]).wait()
    half = cols // 2
    for h in range(2):
        at = slice(h * half, (h + 1) * half)
        u = dot_n(x_ref[...], wu[slot, :, at]) + bias_ref[:, at]
        ga = dot_t(g_ref[...], wd[slot, at, :])
        e = jnp.exp(u * u * -0.5)
        d = 1.0 + jnp.abs(u) * (0.3275911 * inv_sqrt_two)
        t = pl.reciprocal(d, approx=True)
        t = t * (2.0 - d * t)
        poly = t * (0.127414796 + t * (-0.142248368 + t * (0.7107068705 + t * (-0.7265760135 + t * 0.5307027145))))
        tail = poly * e
        phi = jnp.where(u >= 0.0, 1.0 - tail, tail)
        act[:, at] = (u * phi).astype(bf16)
        gu = (ga * (phi + u * (e * inv_sqrt_tau))).astype(bf16)
        gup[:, at] = gu
        gb_ref[:, at] = jnp.sum(gu.astype(f32), axis=0, keepdims=True)

    @pl.when(i == 0)
    def _():
        middle.wait()

    acc[...] += dot_n(act[...], wd[slot])
    gx_ref[...] += dot_t(gup[...], wu[slot])

    @pl.when(i >= 2)
    def _():
        pltpu.make_async_copy(su.at[slot], su.at[slot], out_sem.at[0, slot]).wait()
        pltpu.make_async_copy(sd.at[slot], sd.at[slot], out_sem.at[1, slot]).wait()

    sd[slot] = dot_tl(act[...], g_ref[...]).astype(bf16)
    su[slot] = dot_n(xt[...], gup[...]).astype(bf16)
    at = pl.multiple_of(group(i) * cols, cols)
    for p in range(count):
        c, n = place(p, up_order, core)
        start = pl.multiple_of(lax.bitwise_xor(me, p) * rows, rows)
        pltpu.make_async_copy(
            su.at[slot, pl.ds(start, rows), :], du_refs[c].at[n, :, pl.ds(at, cols)], out_sem.at[0, slot]
        ).start()
    for k in range(blocks):

        @pl.when(i == k)
        def _():
            for p in range(each):
                c, n = place((k << shift) | p, down_order, core)
                start = pl.multiple_of(lax.bitwise_xor(me & (each - 1), p) * part, part)
                pltpu.make_async_copy(
                    sd.at[slot, pl.ds(start, part), :], dd_refs[c].at[n], out_sem.at[1, slot]
                ).start()

    @pl.when(i == blocks - 1)
    def _():
        out_ref[...] = (acc[...] + shift_ref[...]).astype(bf16)
        for s in range(2):
            pltpu.make_async_copy(su.at[s], su.at[s], out_sem.at[0, s]).wait()
            pltpu.make_async_copy(sd.at[s], sd.at[s], out_sem.at[1, s]).wait()


FEED_BLOCKS = 8


def feed(x, grad, middle, bias, shift, up_pieces, down_pieces, up_order, down_order, core, me):
    up_rels = [q for _, q in up_pieces]
    down_rels = [q for _, q in down_pieces]
    count = sum(len(q) for q in up_rels)
    tokens, width = x.shape
    hidden = bias.shape[1]
    cols = hidden // FEED_BLOCKS
    shift_by = (count // FEED_BLOCKS).bit_length() - 1

    def block(i, me_ref):
        return (0, lax.bitwise_xor(lax.shift_right_logical(me_ref[0], shift_by), i))

    def whole(i, me_ref):
        return (0, 0)

    once = pl.Buffered(1)
    anywhere = pl.BlockSpec(memory_space=pl.ANY)
    return pl.pallas_call(
        functools.partial(feed_kernel, up_rels, down_rels, up_order, down_order, core),
        grid_spec=pltpu.PrefetchScalarGridSpec(
            num_scalar_prefetch=1,
            grid=(FEED_BLOCKS,),
            in_specs=[
                pl.BlockSpec((tokens, width), whole, pipeline_mode=once),
                pl.BlockSpec((tokens, width), whole, pipeline_mode=once),
                pl.BlockSpec((1, cols), block),
                pl.BlockSpec((1, width), whole),
                anywhere,
            ]
            + [anywhere] * (len(up_pieces) + len(down_pieces)),
            out_specs=[
                pl.BlockSpec((tokens, width), whole, pipeline_mode=once),
                pl.BlockSpec((tokens, width), whole, pipeline_mode=once),
                pl.BlockSpec((1, cols), block),
            ]
            + [anywhere] * 4,
            scratch_shapes=[
                pltpu.VMEM((2, width, cols), bf16),
                pltpu.VMEM((2, cols, width), bf16),
                pltpu.VMEM((2, width, cols), bf16),
                pltpu.VMEM((2, cols, width), bf16),
                pltpu.VMEM((tokens, width), f32),
                pltpu.VMEM((width, tokens), bf16),
                pltpu.VMEM((tokens, cols), bf16),
                pltpu.VMEM((tokens, cols), bf16),
                pltpu.SemaphoreType.DMA((2, 2)),
                pltpu.SemaphoreType.DMA((2, 2)),
                pltpu.SemaphoreType.DMA,
            ],
        ),
        out_shape=[
            jax.ShapeDtypeStruct((tokens, width), bf16),
            jax.ShapeDtypeStruct((tokens, width), f32),
            jax.ShapeDtypeStruct((1, hidden), f32),
        ]
        + [jax.ShapeDtypeStruct((count // 2, width // count, hidden), bf16)] * 2
        + [jax.ShapeDtypeStruct((count // 2, hidden // count, width), bf16)] * 2,
        compiler_params=pltpu.CompilerParams(vmem_limit_bytes=vmem_most),
        cost_estimate=pl.CostEstimate(
            flops=12 * tokens * width * hidden,
            bytes_accessed=8 * width * hidden + 16 * tokens * width,
            transcendentals=0,
        ),
    )(me, x, grad, bias, shift, middle, *[v for v, _ in up_pieces], *[v for v, _ in down_pieces])


def normalize(values, gain, bias_add):
    center = values - jnp.mean(values, axis=-1, keepdims=True)
    scale_inv = lax.rsqrt(jnp.mean(center * center, axis=-1, keepdims=True) + eps_norm)
    unit_rows = center * scale_inv
    return (unit_rows * gain + bias_add, unit_rows, scale_inv)


def norm_back(grad_out, unit_rows, scale_inv, gain):
    scaled = grad_out * gain
    mean_grad = jnp.mean(scaled, axis=-1, keepdims=True)
    mean_cross = jnp.mean(scaled * unit_rows, axis=-1, keepdims=True)
    return scale_inv * (scaled - mean_grad - unit_rows * mean_cross)


def sort_rows(x):
    frames = x.reshape(FRAMES, FRAME_ROWS, -1)
    few = frames[:, :2].reshape(FEW, -1)
    return jnp.concatenate([frames[:, 2:].reshape(BODY, -1), few, jnp.zeros_like(few)], axis=0)


def unsort_rows(x):
    patches = x[:BODY].reshape(FRAMES, PATCH, -1)
    few = x[BODY : BODY + FEW].reshape(FRAMES, 2, -1)
    return jnp.concatenate([few, patches], axis=1).reshape(FRAMES * FRAME_ROWS, -1)


def body(
    sizes,
    tokens,
    frame_ids,
    pad_mask,
    episode_offsets,
    ln1_gain,
    ln1_bias,
    w_qkv,
    b_qkv,
    w_out,
    b_out,
    ln2_gain,
    ln2_bias,
    w_up,
    b_up,
    w_down,
    b_down,
    cotangent,
):
    width = tokens.shape[1]
    me = (lax.axis_index("dp") * sizes[1] + lax.axis_index("fsdp")).astype(jnp.int32)[None]
    core, order_a, order_b = bit_orders(sizes)
    pieces_q = gather_pieces(w_qkv[:, : 2 * width], order_a, core, sizes)
    pieces_v = gather_pieces(
        jnp.concatenate([w_qkv[:, 2 * width :], w_out], axis=1), order_b, core, sizes
    )
    w_up, w_down, *_ = lax.optimization_barrier((w_up, w_down, pieces_q[0][0], pieces_v[0][0]))
    pieces_up = gather_pieces(w_up, order_a, core, sizes)
    pieces_down = gather_pieces(w_down, order_b, core, sizes)
    gain_one, bias_one, qkv_rows, out_bias, gain_two, bias_two, up_bias, down_bias = [
        v.astype(f32)
        for v in gather_small(
            [ln1_gain, ln1_bias, b_qkv, b_out, ln2_gain, ln2_bias, b_up, b_down]
        )
    ]
    seen = seen_frames(episode_offsets[0])
    hide = hidden_few(seen)
    cosine, sine = turn_tables(frame_ids, row_order())
    partner = partner_matrix()
    values_in = sort_rows(tokens).astype(f32)
    cot = sort_rows(cotangent)
    normed_one, unit_one, inv_one = normalize(values_in, gain_one, bias_one)
    normed_one = normed_one.astype(bf16)
    qk_matrix = assemble(pieces_q, me)
    vo_matrix = assemble(pieces_v, me)
    qkv_matrix = jnp.concatenate([qk_matrix, vo_matrix[:, :width]], axis=1)
    out_matrix = vo_matrix[:, width:]
    qkv = project(normed_one, qkv_matrix, qkv_rows.reshape(1, 3 * width), cosine, sine, partner)
    attended, lse, few = attend(seen, qkv, hide)
    middle = values_in + jnp.dot(attended, out_matrix, preferred_element_type=f32) + out_bias
    normed_two, unit_two, inv_two = normalize(middle, gain_two, bias_two)
    normed_two = normed_two.astype(bf16)
    result, grad_normed_two, grad_b_up_local, up_own, up_other, down_own, down_other = feed(
        normed_two,
        cot,
        middle,
        up_bias[None],
        down_bias[None],
        pieces_up,
        pieces_down,
        order_a,
        order_b,
        core,
        me,
    )
    output = unsort_rows(result)
    grad_b_down_local = jnp.sum(cot.astype(f32), axis=0)
    grad_gain_two = jnp.sum(grad_normed_two * unit_two, axis=0)
    grad_bias_two = jnp.sum(grad_normed_two, axis=0)
    sum_up = reduce_pieces(up_own, up_other, order_a, core, sizes)
    sum_down = reduce_pieces(down_own, down_other, order_b, core, sizes)
    small_feed = reduce_small(
        [grad_gain_two, grad_bias_two, grad_b_up_local[0], grad_b_down_local],
        order_a,
        core,
        sizes,
        me,
    )
    grad_middle = cot.astype(f32) + norm_back(grad_normed_two, unit_two, inv_two, gain_two)
    grad_branch = grad_middle.astype(bf16)
    grad_b_out_local = jnp.sum(grad_branch.astype(f32), axis=0)
    grad_w_out_local = dot_tl(attended, grad_branch)
    grad_attended = dot_t(grad_branch, out_matrix).astype(bf16)
    pairs = width // (2 * HEAD)
    grad_mixed = attend_back(
        seen, qkv, attended, grad_attended, lse, few, hide, cosine, sine, partner, 0, pairs
    )
    grad_b_qkv_local = jnp.sum(grad_mixed.astype(f32), axis=1)
    grad_w_parts = [dot_tl(normed_one, grad_mixed[i]).astype(bf16) for i in range(3)]
    grad_normed_one = (
        dot_t(grad_mixed[0], qk_matrix[:, :width])
        + dot_t(grad_mixed[1], qk_matrix[:, width:])
        + dot_t(grad_mixed[2], vo_matrix[:, :width])
    )
    grad_gain_one = jnp.sum(grad_normed_one * unit_one, axis=0)
    grad_bias_one = jnp.sum(grad_normed_one, axis=0)
    grad_qk = jnp.concatenate(grad_w_parts[:2], axis=1)
    sum_q = reduce_pieces(*split(grad_qk, order_a, core, me), order_a, core, sizes)
    grad_vo = jnp.concatenate([grad_w_parts[2], grad_w_out_local.astype(bf16)], axis=1)
    sum_v = reduce_pieces(*split(grad_vo, order_b, core, me), order_b, core, sizes)
    small_attn = reduce_small(
        [grad_gain_one, grad_bias_one, grad_b_qkv_local, grad_b_out_local],
        order_b,
        core,
        sizes,
        me,
    )
    grad_tokens = unsort_rows(
        grad_middle + norm_back(grad_normed_one, unit_one, inv_one, gain_one)
    )
    return (
        output,
        grad_tokens,
        small_attn[0],
        small_attn[1],
        jnp.concatenate([sum_q, sum_v[:, :width]], axis=1),
        small_attn[2],
        sum_v[:, width:],
        small_attn[3],
        small_feed[0],
        small_feed[1],
        sum_up,
        small_feed[2],
        sum_down,
        small_feed[3],
    )


def solution(mesh):
    placed = (
        P(("dp", "fsdp"), None),
        P(("dp", "fsdp")),
        P(("dp", "fsdp")),
        P(("dp", "fsdp"), None),
        P(("dp", "fsdp")),
        P(("dp", "fsdp")),
        P(("dp", "fsdp"), None),
        P(None, ("dp", "fsdp")),
        P(("dp", "fsdp"), None),
        P(("dp", "fsdp")),
        P(("dp", "fsdp")),
        P(("dp", "fsdp")),
        P(("dp", "fsdp"), None),
        P(("dp", "fsdp")),
        P(("dp", "fsdp"), None),
        P(("dp", "fsdp")),
        P(("dp", "fsdp"), None),
    )
    sizes = (mesh.shape["dp"], mesh.shape["fsdp"])
    return jax.shard_map(
        functools.partial(body, sizes),
        mesh=mesh,
        in_specs=placed,
        out_specs=(
            P(("dp", "fsdp"), None),
            P(("dp", "fsdp"), None),
            P(("dp", "fsdp")),
            P(("dp", "fsdp")),
            P(("dp", "fsdp"), None),
            P(None, ("dp", "fsdp")),
            P(("dp", "fsdp"), None),
            P(("dp", "fsdp")),
            P(("dp", "fsdp")),
            P(("dp", "fsdp")),
            P(("dp", "fsdp"), None),
            P(("dp", "fsdp")),
            P(("dp", "fsdp"), None),
            P(("dp", "fsdp")),
        ),
        check_vma=False,
    )
```

```python
import functools
import math

import jax
import jax.numpy as jnp
import numpy as np
from jax import lax
from jax.experimental import pallas as pl
from jax.experimental.pallas import tpu as pltpu
from jax.sharding import PartitionSpec as P

HEAD = 64
GRID = 16
FRAME_ROWS = 258
FRAMES = 4
PATCH = GRID * GRID
EXTRA = 16
FEW = 8
BODY = FRAMES * PATCH
ROWS = BODY + EXTRA
eps_norm = 1e-06
part_sizes = (24, 20, 20)
masked_value = -1e30
inv_sqrt_two = 1.0 / math.sqrt(2.0)
inv_sqrt_tau = 1.0 / math.sqrt(2.0 * math.pi)
f32 = jnp.float32
bf16 = jnp.bfloat16
vmem_most = 60 * 1024 * 1024


def cost(micros):
    return pl.CostEstimate(flops=int(micros * 1e9), bytes_accessed=0, transcendentals=0)


def log2(n):
    return n.bit_length() - 1


def swap(value, mask, sizes):
    count = sizes[0] * sizes[1]
    return lax.ppermute(value, ("dp", "fsdp"), [(i, i ^ mask) for i in range(count)])


def bit_orders(sizes):
    inner, outer = log2(sizes[1]), log2(sizes[0])
    line = list(range(1, inner))
    cross = [0]
    other = list(range(inner + 1, inner + outer))
    return inner, line, (cross + other, other + cross)


def spread(bits):
    rel = [0]
    for bit in bits:
        rel = rel + [p | (1 << bit) for p in rel]
    return rel


def gather_line(shard, line, sizes):
    rel = spread(line)
    held = [shard[None]] + [swap(shard[None], p, sizes) for p in rel[1:]]
    half = len(rel) // 2
    return [
        [(jnp.concatenate(held[at : at + half], axis=0), rel[at : at + half])]
        for at in (0, half)
    ]


def gather_doubling(shard, line, sizes):
    held, rel = shard[None], [0]
    for bit in line[:-1]:
        held = jnp.concatenate([held, swap(held, 1 << bit, sizes)], axis=0)
        rel = rel + [p | (1 << bit) for p in rel]
    return [[(held, rel)], moved([(held, rel)], line[-1], sizes)]


def moved(pieces, bit, sizes):
    return [(swap(v, 1 << bit, sizes), [p | (1 << bit) for p in q]) for v, q in pieces]


def relatives(line, orders, core):
    low, top = line[:-1], 1 << line[-1]
    rel = spread(low + orders[0]) + [p | top for p in spread(low + orders[1])]
    return rel, [p | (1 << core) for p in rel]


def reduce_start(own, taken, orders, sizes, small=None):
    half = own.shape[0] // 2
    found = []
    for at, order in zip((0, half), orders):
        kept, came = own[at : at + half], taken[at : at + half]
        quarter = half // 2
        pieces = []
        for low in (0, quarter):
            total = kept[low : low + quarter].astype(f32) + came[low : low + quarter].astype(f32)
            if small is not None:
                total = jnp.concatenate([total, small[at + low : at + low + quarter]], axis=2)
            pieces.append(total.astype(own.dtype))
        held, sent = pieces
        found.append((held, swap(sent, 1 << order[-1], sizes), sent))
    return found


def reduce_step(kept, taken, mask, sizes):
    kind = kept.dtype
    half = kept.shape[0] // 2
    sent = (kept[half:].astype(f32) + taken[half:].astype(f32)).astype(kind)
    held = (kept[:half].astype(f32) + taken[:half].astype(f32)).astype(kind)
    return held, swap(sent, mask, sizes), sent


def reduce_next(groups, orders, step, sizes):
    return [
        reduce_step(*group, 1 << order[-1 - step], sizes) for group, order in zip(groups, orders)
    ]


def after_pieces(pieces, *others):
    return [(after(v, *others), q) for v, q in pieces]


def line_parts(groups):
    return [
        kept[n].astype(f32) + taken[n].astype(f32)
        for kept, taken in groups
        for n in range(kept.shape[0])
    ]


def reduce_line(parts, line, sizes):
    total = parts[0]
    for part, p in zip(parts[1:], spread(line)[1:]):
        total = total + swap(part, p, sizes).astype(f32)
    return total


def after_kernel(*refs):
    del refs


def after(value, *others):
    anywhere = pl.BlockSpec(memory_space=pl.ANY)
    return pl.pallas_call(
        after_kernel,
        out_shape=jax.ShapeDtypeStruct(value.shape, value.dtype),
        in_specs=[anywhere] * (1 + len(others)),
        out_specs=anywhere,
        input_output_aliases={0: 0},
        cost_estimate=cost(0),
    )(value, *others)


def assemble_kernel(rels, parts, me_ref, *refs):
    pieces, refs = refs[: len(rels)], refs[len(rels) :]
    outs, sems = refs[: len(parts)], refs[-1]
    me = me_ref[0]
    for k, (top, height, left, cols) in enumerate(parts):
        for piece, rel in zip(pieces, rels):
            for at, p in enumerate(rel):
                start = pl.multiple_of(lax.bitwise_xor(me, p) * height, height)
                pltpu.make_async_copy(
                    piece.at[at, pl.ds(top, height), pl.ds(left, cols)],
                    outs[k].at[pl.ds(start, height)],
                    sems.at[k],
                ).start()
    for k, out in enumerate(outs):
        pltpu.make_async_copy(out, out, sems.at[k]).wait()


def assemble(pieces, me, parts):
    rels = [q for _, q in pieces]
    count = sum(len(q) for q in rels)
    total = sum(h * c for _, h, _, c in parts)
    return pl.pallas_call(
        functools.partial(assemble_kernel, rels, parts),
        out_shape=[jax.ShapeDtypeStruct((count * h, c), bf16) for _, h, _, c in parts],
        in_specs=[pl.BlockSpec(memory_space=pltpu.SMEM)]
        + [pl.BlockSpec(memory_space=pl.ANY)] * len(pieces),
        scratch_shapes=[pltpu.SemaphoreType.DMA((len(parts),))],
        compiler_params=pltpu.CompilerParams(vmem_limit_bytes=vmem_most),
        cost_estimate=cost(1.5),
    )(me, *[v for v, _ in pieces])


def pack_small(parts, rows):
    def fill(blocks):
        blocks = [jnp.pad(v, ((0, 0), (0, 128 - v.shape[1]))) for v in blocks]
        used = sum(v.shape[0] for v in blocks)
        return jnp.concatenate(blocks + [jnp.zeros((rows - used, 128), bf16)], axis=0)

    flat = fill([v[None] for v in parts if v.ndim == 1])
    return jnp.concatenate([flat] + [fill([v]) for v in parts if v.ndim == 2], axis=1)


def unpack_small(whole, rows, parts):
    whole = whole.reshape(-1, rows, whole.shape[1]).astype(f32)
    found, at, left = [], 0, 128
    for v in parts:
        size = v.shape[-1]
        if v.ndim == 2:
            block = whole[:, : v.shape[0], left : left + size].swapaxes(0, 1)
            found.append(block.reshape(v.shape[0], -1))
            left += 128
        else:
            found.append(whole[:, at, :size].reshape(-1))
            at += 1
    return found


def small_units(parts, rows, where, me):
    count = sum(len(q) for q in where)
    blocks = [
        v.reshape(count, -1)
        if v.ndim == 1
        else v.reshape(v.shape[0], count, -1).swapaxes(0, 1).reshape(count, -1)
        for v in parts
    ]
    flat = jnp.concatenate(blocks, axis=1)
    flat = jnp.pad(flat, ((0, 0), (0, rows * 128 - flat.shape[1]))).reshape(count, rows, 128)
    index = lax.bitwise_xor(jnp.asarray(where[0] + where[1], jnp.int32), me[0])
    mixed = jnp.take(flat, index, axis=0)
    return mixed[: count // 2], mixed[count // 2 :]


def small_parts(unit, parts, count):
    flat = unit.reshape(-1)
    found, at = [], 0
    for v in parts:
        size = v.size // count
        block = flat[at : at + size]
        found.append(block if v.ndim == 1 else block.reshape(v.shape[0], -1))
        at = at + size
    return found


def dot_t(a, b):
    return lax.dot_general(a, b, (((1,), (1,)), ((), ())), preferred_element_type=f32)


def dot_n(a, b):
    return lax.dot_general(a, b, (((1,), (0,)), ((), ())), preferred_element_type=f32)


def dot_tl(a, b):
    return lax.dot_general(a, b, (((0,), (0,)), ((), ())), preferred_element_type=f32)


def head_lanes(a, rows):
    lane = lax.broadcasted_iota(jnp.int32, (rows, 2 * HEAD), 1)
    return (lane >= HEAD) if a else (lane < HEAD)


def keep_head(x, a):
    return jnp.where(head_lanes(a, x.shape[0]), x, jnp.zeros_like(x))


def stack_heads(x):
    return jnp.concatenate([keep_head(x, 0), keep_head(x, 1)], axis=0)


def join_heads(x):
    return jnp.where(head_lanes(0, FEW), x[:FEW], x[FEW:])


def few_rows(x):
    return jnp.concatenate([x, jnp.zeros_like(x)], axis=0)


def hide_few(s, first, last):
    row = lax.broadcasted_iota(jnp.int32, (EXTRA, s.shape[1]), 0)
    frame = lax.shift_right_logical(row, 1)
    seen = (frame >= first) & (frame <= last)
    count = s.shape[0] - EXTRA
    return jnp.concatenate([s[:count], jnp.where(seen, s[count:], masked_value)], axis=0)


def seen_rows(ref, lo, n):
    return jnp.concatenate([ref[pl.ds(lo, n * PATCH), :], ref[BODY:ROWS, :]], axis=0)


def seen_lanes(ref, a, lo, n):
    return jnp.concatenate(
        [ref[a * HEAD : (a + 1) * HEAD, pl.ds(lo, n * PATCH)], ref[a * HEAD : (a + 1) * HEAD, BODY:ROWS]],
        axis=1,
    )


def attend_kernel(seen_ref, q_ref, k_ref, v_ref, hide_ref, out_ref, lse_ref, few_ref, vt):
    f = pl.program_id(1)

    @pl.when(f == 0)
    def _():
        vt[...] = v_ref[...].T
        qs = stack_heads(q_ref[BODY:ROWS, :].astype(f32)[:FEW]).astype(bf16)
        s = dot_t(k_ref[...], qs) + hide_ref[...]
        top = jnp.max(s, axis=0, keepdims=True)
        p = jnp.exp(s - top)
        total = jnp.sum(p, axis=0, keepdims=True)
        o = dot_tl((p / total).astype(bf16), v_ref[...])
        out_ref[BODY:ROWS, :] = few_rows(join_heads(o)).astype(bf16)
        few_ref[0] = top + jnp.log(total)

    row = pl.multiple_of(f * PATCH, PATCH)
    seen = seen_ref[f]

    @pl.when(seen == 0)
    def _():
        out_ref[pl.ds(row, PATCH), :] = v_ref[pl.ds(row, PATCH), :]
        lse_ref[0, :, pl.ds(row, PATCH)] = jnp.zeros((2, PATCH), f32)

    for n in range(1, FRAMES + 1):

        @pl.when(seen == n)
        def _(n=n):
            first = f - (n - 1)
            lo = pl.multiple_of(first * PATCH, PATCH)
            keys = seen_rows(k_ref, lo, n)
            q = q_ref[pl.ds(row, PATCH), :]
            outs, sums = [], []
            for a in range(2):
                s = hide_few(dot_t(keys, keep_head(q, a)), first, f)
                top = jnp.max(s, axis=0, keepdims=True)
                p = jnp.exp(s - top)
                total = jnp.sum(p, axis=0, keepdims=True)
                o = dot_n(seen_lanes(vt, a, lo, n), p.astype(bf16))
                outs.append(o / total)
                sums.append(top + jnp.log(total))
            out_ref[pl.ds(row, PATCH), :] = jnp.concatenate(outs, axis=0).T.astype(bf16)
            lse_ref[0, :, pl.ds(row, PATCH)] = jnp.concatenate(sums, axis=0)


def attend(seen, qkv, hide, pair_lo, pair_hi, kept=None):
    width = qkv.shape[1] // 3
    pairs = width // (2 * HEAD)
    lanes = 2 * HEAD
    at = pair_lo
    some = pair_hi - pair_lo
    kernel = attend_kernel
    more, alias = [], {}
    if kept is not None:
        more, alias = [kept], {5: 0}

        def kernel(seen_ref, q_ref, k_ref, v_ref, hide_ref, kept_ref, *refs):
            attend_kernel(seen_ref, q_ref, k_ref, v_ref, hide_ref, *refs)

    return pl.pallas_call(
        kernel,
        grid_spec=pltpu.PrefetchScalarGridSpec(
            num_scalar_prefetch=1,
            grid=(some, FRAMES),
            in_specs=[
                pl.BlockSpec((ROWS, lanes), lambda h, f, s: (0, at + h)),
                pl.BlockSpec((ROWS, lanes), lambda h, f, s: (0, at + pairs + h)),
                pl.BlockSpec((ROWS, lanes), lambda h, f, s: (0, at + 2 * pairs + h)),
                pl.BlockSpec((ROWS, 2 * FEW), lambda h, f, s: (0, 0)),
            ]
            + [pl.BlockSpec(memory_space=pl.ANY)] * len(more),
            out_specs=[
                pl.BlockSpec((ROWS, lanes), lambda h, f, s: (0, at + h)),
                pl.BlockSpec((1, 2, BODY), lambda h, f, s: (h, 0, 0)),
                pl.BlockSpec((1, 1, 2 * FEW), lambda h, f, s: (h, 0, 0)),
            ],
            scratch_shapes=[pltpu.VMEM((lanes, ROWS), bf16)],
        ),
        out_shape=(
            jax.ShapeDtypeStruct((ROWS, width), bf16),
            jax.ShapeDtypeStruct((some, 2, BODY), f32),
            jax.ShapeDtypeStruct((some, 1, 2 * FEW), f32),
        ),
        input_output_aliases=alias,
        compiler_params=pltpu.CompilerParams(vmem_limit_bytes=vmem_most),
        cost_estimate=cost(1.6 * some),
    )(seen, qkv, qkv, qkv, hide, *more)


def unturn(x, cosine, sine, partner):
    return x * cosine - dot_n(x.astype(bf16), partner) * sine


def attend_back_kernel(
    scale, seen_ref, q_ref, k_ref, v_ref, o_ref, g_ref, lse_ref, few_ref, hide_ref, cos_ref, sin_ref,
    part_ref, out_ref, kt, dq, dk, dv,
):
    f = pl.program_id(1)
    ones = jnp.where(
        (lax.broadcasted_iota(jnp.int32, (8, 2 * HEAD), 1) >= HEAD).astype(jnp.int32)
        == lax.broadcasted_iota(jnp.int32, (8, 2 * HEAD), 0),
        1.0,
        0.0,
    ).astype(bf16)

    @pl.when(f == 0)
    def _():
        kt[...] = k_ref[...].T
        qs = stack_heads(q_ref[BODY:ROWS, :].astype(f32)[:FEW]).astype(bf16)
        gs = stack_heads(g_ref[BODY:ROWS, :].astype(f32)[:FEW])
        os = stack_heads(o_ref[BODY:ROWS, :].astype(f32)[:FEW])
        p = jnp.exp(dot_t(k_ref[...], qs) + hide_ref[...] - few_ref[0])
        gp = dot_t(v_ref[...], gs.astype(bf16))
        delta = jnp.sum(gp * p, axis=0, keepdims=True)
        ds = (p * (gp - delta)).astype(bf16)
        dv[...] = dot_n(p.astype(bf16), gs.astype(bf16))
        dk[...] = dot_n(ds, qs)
        dq[BODY:ROWS, :] = few_rows(join_heads(dot_tl(ds, k_ref[...])))

    row = pl.multiple_of(f * PATCH, PATCH)
    seen = seen_ref[f]

    @pl.when(seen == 0)
    def _():
        dv[pl.ds(row, PATCH), :] += g_ref[pl.ds(row, PATCH), :].astype(f32)
        dq[pl.ds(row, PATCH), :] = jnp.zeros((PATCH, 2 * HEAD), f32)

    for n in range(1, FRAMES + 1):

        @pl.when(seen == n)
        def _(n=n):
            first = f - (n - 1)
            lo = pl.multiple_of(first * PATCH, PATCH)
            keys = seen_rows(k_ref, lo, n)
            values = seen_rows(v_ref, lo, n)
            q = q_ref[pl.ds(row, PATCH), :]
            g = g_ref[pl.ds(row, PATCH), :]
            product = g.astype(f32) * o_ref[pl.ds(row, PATCH), :].astype(f32)
            upper = product.astype(bf16)
            lower = (product - upper.astype(f32)).astype(bf16)
            deltas = dot_t(ones, upper) + dot_t(ones, lower)
            back, add_k, add_v = [], None, None
            for a in range(2):
                qm, gm = keep_head(q, a), keep_head(g, a)
                s = hide_few(dot_t(keys, qm), first, f)
                p = jnp.exp(s - lse_ref[0, a : a + 1, pl.ds(row, PATCH)])
                gp = dot_t(values, gm)
                ds = (p * (gp - deltas[a : a + 1])).astype(bf16)
                more_v, more_k = dot_n(p.astype(bf16), gm), dot_n(ds, qm)
                add_v = more_v if add_v is None else add_v + more_v
                add_k = more_k if add_k is None else add_k + more_k
                back.append(dot_n(seen_lanes(kt, a, lo, n), ds))
            dq[pl.ds(row, PATCH), :] = jnp.concatenate(back, axis=0).T
            count = n * PATCH
            dk[pl.ds(lo, count), :] += add_k[:count]
            dk[BODY:ROWS, :] += add_k[count:]
            dv[pl.ds(lo, count), :] += add_v[:count]
            dv[BODY:ROWS, :] += add_v[count:]

    @pl.when(f == FRAMES - 1)
    def _():
        partner = part_ref[...]
        out_ref[0] = unturn(dq[...] * scale, cos_ref[...], sin_ref[...], partner).astype(bf16)
        out_ref[1] = unturn(dk[...], cos_ref[...], sin_ref[...], partner).astype(bf16)
        out_ref[2] = dv[...].astype(bf16)


def attend_back(
    seen, qkv, attended, grad, lse, few, hide, cosine, sine, partner, pair_lo, pair_hi, kept=None
):
    width = qkv.shape[1] // 3
    pairs = width // (2 * HEAD)
    lanes = 2 * HEAD
    at = pair_lo
    some = pair_hi - pair_lo
    inner = functools.partial(attend_back_kernel, 1.0 / math.sqrt(HEAD))
    kernel = inner
    more, alias = [], {}
    if kept is not None:
        more, alias = [kept], {12: 0}

        def kernel(*refs):
            inner(*refs[:12], *refs[13:])

    def whole(h, f, s):
        return (0, 0)

    return pl.pallas_call(
        kernel,
        grid_spec=pltpu.PrefetchScalarGridSpec(
            num_scalar_prefetch=1,
            grid=(some, FRAMES),
            in_specs=[
                pl.BlockSpec((ROWS, lanes), lambda h, f, s: (0, at + h)),
                pl.BlockSpec((ROWS, lanes), lambda h, f, s: (0, at + pairs + h)),
                pl.BlockSpec((ROWS, lanes), lambda h, f, s: (0, at + 2 * pairs + h)),
                pl.BlockSpec((ROWS, lanes), lambda h, f, s: (0, at + h)),
                pl.BlockSpec((ROWS, lanes), lambda h, f, s: (0, at + h)),
                pl.BlockSpec((1, 2, BODY), lambda h, f, s: (h, 0, 0)),
                pl.BlockSpec((1, 1, 2 * FEW), lambda h, f, s: (h, 0, 0)),
                pl.BlockSpec((ROWS, 2 * FEW), whole),
                pl.BlockSpec((ROWS, lanes), whole),
                pl.BlockSpec((ROWS, lanes), whole),
                pl.BlockSpec((lanes, lanes), whole),
            ]
            + [pl.BlockSpec(memory_space=pl.ANY)] * len(more),
            out_specs=pl.BlockSpec((3, ROWS, lanes), lambda h, f, s: (0, 0, at + h)),
            scratch_shapes=[
                pltpu.VMEM((lanes, ROWS), bf16),
                pltpu.VMEM((ROWS, lanes), f32),
                pltpu.VMEM((ROWS, lanes), f32),
                pltpu.VMEM((ROWS, lanes), f32),
            ],
        ),
        out_shape=jax.ShapeDtypeStruct((3, ROWS, width), bf16),
        input_output_aliases=alias,
        compiler_params=pltpu.CompilerParams(vmem_limit_bytes=vmem_most),
        cost_estimate=cost(1.9 * some),
    )(seen, qkv, qkv, qkv, attended, grad, lse, few, hide, cosine, sine, partner, *more)


def project_kernel(scale, x_ref, w_ref, b_ref, cos_ref, sin_ref, part_ref, out_ref):
    j = pl.program_id(0)
    third = pl.num_programs(0) // 3
    lanes = 2 * HEAD
    w = w_ref[...]
    mixed = dot_n(x_ref[...], w) + b_ref[...]

    @pl.when(j < 2 * third)
    def _():
        bias = jnp.broadcast_to(b_ref[...], (8, w.shape[1]))
        by = jnp.where(j < third, scale, 1.0)
        for h in range(w.shape[1] // lanes):
            at = slice(h * lanes, (h + 1) * lanes)
            turned = dot_n(w[:, at], part_ref[...]).astype(bf16)
            moved = dot_n(bias[:, at].astype(bf16), part_ref[...])[:1]
            other = dot_n(x_ref[...], turned) + moved
            out_ref[:, at] = ((mixed[:, at] * cos_ref[...] + other * sin_ref[...]) * by).astype(bf16)

    @pl.when(j >= 2 * third)
    def _():
        out_ref[...] = mixed.astype(bf16)


def project(x, w, bias, cosine, sine, partner):
    rows, width = x.shape
    cols = 256
    lanes = 2 * HEAD

    def whole(j):
        return (0, 0)

    return pl.pallas_call(
        functools.partial(project_kernel, 1.0 / math.sqrt(HEAD)),
        grid=(w.shape[1] // cols,),
        in_specs=[
            pl.BlockSpec((rows, width), whole),
            pl.BlockSpec((width, cols), lambda j: (0, j)),
            pl.BlockSpec((1, cols), lambda j: (0, j)),
            pl.BlockSpec((rows, lanes), whole),
            pl.BlockSpec((rows, lanes), whole),
            pl.BlockSpec((lanes, lanes), whole),
        ],
        out_specs=pl.BlockSpec((rows, cols), lambda j: (0, j)),
        out_shape=jax.ShapeDtypeStruct((rows, w.shape[1]), bf16),
        compiler_params=pltpu.CompilerParams(vmem_limit_bytes=vmem_most),
        cost_estimate=cost(6),
    )(x, w, bias, cosine, sine, partner)


def turn_tables(frame_ids):
    frequency, which, sign = [], [], []
    for kind, part in enumerate(part_sizes):
        half = part // 2
        frequency += [10000.0 ** (-i / half) for i in range(half)] * 2
        which += [kind] * part
        sign += [-1.0] * half + [1.0] * half
    frequency = jnp.asarray(np.tile(np.array(frequency, np.float32), 2))
    which = np.tile(np.array(which), 2)
    sign = np.tile(np.array(sign, np.float32), 2)
    time = frame_ids[:: FRAME_ROWS].astype(f32)[:, None] * frequency
    place = np.arange(GRID, dtype=np.float32)[:, None] * frequency

    def table(of, empty):
        by_time, by_place = of(time), of(place)
        still = jnp.full((FRAMES, 2, which.size), empty, f32)
        patches = jnp.where(which == 1, by_place[:, None], by_place[None]).reshape(1, PATCH, -1)
        patches = jnp.where(which == 0, by_time[:, None], patches).reshape(BODY, -1)
        few = jnp.where(which == 0, by_time[:, None], still).reshape(FEW, -1)
        return jnp.concatenate([patches, few, jnp.zeros_like(few)], axis=0)

    return table(jnp.cos, 1.0), table(lambda v: jnp.sin(v) * sign, 0.0)


def partner_matrix():
    lanes = 2 * HEAD
    matrix = np.zeros((lanes, lanes), np.float32)
    for head in range(2):
        at = head * HEAD
        for part in part_sizes:
            for i in range(part // 2):
                matrix[at + i, at + i + part // 2] = 1.0
                matrix[at + i + part // 2, at + i] = 1.0
            at += part
    return jnp.asarray(matrix, bf16)


def seen_frames(offset_row):
    frame = jnp.arange(FRAMES, dtype=jnp.int32)
    start = jnp.where(frame >= offset_row[1], offset_row[1], 0)
    return jnp.where(frame < offset_row[2], frame - start + 1, 0)


def hidden_few(seen):
    frame_of = np.concatenate([np.repeat(np.arange(FRAMES), PATCH), np.repeat(np.arange(FRAMES), 2), np.full(EXTRA - FEW, FRAMES)])
    own = np.zeros((ROWS, FEW), bool)
    own[BODY + np.arange(FEW), np.arange(FEW)] = True
    frame = jnp.asarray(frame_of, jnp.int32)[:, None]
    query = jnp.arange(FEW, dtype=jnp.int32)[None, :] // 2
    count = jnp.repeat(seen, 2)[None, :]
    allowed = ((frame <= query) & (frame > query - count)) | jnp.asarray(own)
    return jnp.tile(jnp.where(allowed, 0.0, masked_value), (1, 2))


def place(p, line, orders, core):
    own, other = relatives(line, orders, core)
    return (1, other.index(p)) if p in other else (0, own.index(p))


def find_piece(rels, p):
    for c, rel in enumerate(rels):
        if p in rel:
            return c, rel.index(p)
    raise ValueError(p)


def feed_kernel(
    rels, where, me_ref, x_ref, g_ref, bias_ref, shift_ref, mid_ref, up_ref, *refs
):
    pieces, refs = refs[: len(rels)], refs[len(rels) :]
    out_ref, gx_ref, gb_ref = refs[:3]
    grads = refs[3:5]
    wu, wd, su, sd, acc, xt, act, gup, in_sem, out_sem, mid_sem = refs[5:]
    count = sum(len(q) for q in rels)
    blocks = FEED_BLOCKS
    each = count // blocks
    shift = each.bit_length() - 1
    i = pl.program_id(0)
    me = me_ref[0]
    width = x_ref.shape[1]
    cols = wu.shape[2]
    rows = width // count
    part = cols // each
    hidden = blocks * cols
    stacks = part // rows
    slot = lax.rem(i, 2)

    def group(j):
        return lax.bitwise_xor(lax.shift_right_logical(me, shift), j)

    def fetch(j, to):
        at = pl.multiple_of(group(j) * cols, cols)
        pltpu.make_async_copy(up_ref.at[:, pl.ds(at, cols)], wu.at[to], in_sem.at[0, to]).start()
        for k in range(blocks):

            @pl.when(j == k)
            def _():
                for p in range(each):
                    c, n = find_piece(rels, (k << shift) | p)
                    start = pl.multiple_of(lax.bitwise_xor(me & (each - 1), p) * part, part)
                    for q in range(stacks):
                        pltpu.make_async_copy(
                            pieces[c].at[n, :, pl.ds(q * width, width)],
                            wd.at[to, pl.ds(start + q * rows, rows), :],
                            in_sem.at[1, to],
                        ).start()

    middle = pltpu.make_async_copy(mid_ref, acc, mid_sem)

    @pl.when(i == 0)
    def _():
        fetch(i, slot)
        middle.start()
        xt[...] = x_ref[...].T
        gx_ref[...] = jnp.zeros_like(gx_ref)

    @pl.when(i + 1 < blocks)
    def _():
        fetch(i + 1, 1 - slot)

    pltpu.make_async_copy(wu.at[slot], wu.at[slot], in_sem.at[0, slot]).wait()
    pltpu.make_async_copy(wd.at[slot], wd.at[slot], in_sem.at[1, slot]).wait()
    half = cols // 2
    for h in range(2):
        at = slice(h * half, (h + 1) * half)
        u = dot_n(x_ref[...], wu[slot, :, at]) + bias_ref[:, at]
        ga = dot_t(g_ref[...], wd[slot, at, :])
        e = jnp.exp(u * u * -0.5)
        d = 1.0 + jnp.abs(u) * (0.3275911 * inv_sqrt_two)
        t = pl.reciprocal(d, approx=True)
        t = t * (2.0 - d * t)
        poly = t * (0.127414796 + t * (-0.142248368 + t * (0.7107068705 + t * (-0.7265760135 + t * 0.5307027145))))
        tail = poly * e
        phi = jnp.where(u >= 0.0, 1.0 - tail, tail)
        act[:, at] = (u * phi).astype(bf16)
        gu = (ga * (phi + u * (e * inv_sqrt_tau))).astype(bf16)
        gup[:, at] = gu
        gb_ref[:, at] = jnp.sum(gu.astype(f32), axis=0, keepdims=True)

    @pl.when(i == 0)
    def _():
        middle.wait()

    acc[...] += dot_n(act[...], wd[slot])
    gx_ref[...] += dot_t(gup[...], wu[slot])

    @pl.when(i >= 2)
    def _():
        pltpu.make_async_copy(su.at[slot], su.at[slot], out_sem.at[0, slot]).wait()
        pltpu.make_async_copy(sd.at[slot], sd.at[slot], out_sem.at[1, slot]).wait()

    sd[slot] = dot_tl(act[...], g_ref[...]).astype(bf16)
    su[slot] = dot_n(xt[...], gup[...]).astype(bf16)
    at = pl.multiple_of(group(i) * cols, cols)
    for p in range(count):
        c, n = place(p, *where)
        start = pl.multiple_of(lax.bitwise_xor(me, p) * rows, rows)
        pltpu.make_async_copy(
            su.at[slot, pl.ds(start, rows), :],
            grads[c].at[n, :, pl.ds(at, cols)],
            out_sem.at[0, slot],
        ).start()
    for k in range(blocks):

        @pl.when(i == k)
        def _():
            for p in range(each):
                c, n = place((k << shift) | p, *where)
                start = pl.multiple_of(lax.bitwise_xor(me & (each - 1), p) * part, part)
                for q in range(stacks):
                    pltpu.make_async_copy(
                        sd.at[slot, pl.ds(start + q * rows, rows), :],
                        grads[c].at[n, :, pl.ds(hidden + q * width, width)],
                        out_sem.at[1, slot],
                    ).start()

    @pl.when(i == blocks - 1)
    def _():
        out_ref[...] = (acc[...] + shift_ref[...]).astype(bf16)
        for s in range(2):
            pltpu.make_async_copy(su.at[s], su.at[s], out_sem.at[0, s]).wait()
            pltpu.make_async_copy(sd.at[s], sd.at[s], out_sem.at[1, s]).wait()


FEED_BLOCKS = 8


def feed(x, grad, middle, bias, shift, up, pieces, line, orders, core, me):
    rels = [q for _, q in pieces]
    count = sum(len(q) for q in rels)
    tokens, width = x.shape
    hidden = bias.shape[1]
    cols = hidden // FEED_BLOCKS
    shift_by = (count // FEED_BLOCKS).bit_length() - 1

    def block(i, me_ref):
        return (0, lax.bitwise_xor(lax.shift_right_logical(me_ref[0], shift_by), i))

    def whole(i, me_ref):
        return (0, 0)

    once = pl.Buffered(1)
    anywhere = pl.BlockSpec(memory_space=pl.ANY)
    return pl.pallas_call(
        functools.partial(feed_kernel, rels, (line, orders, core)),
        grid_spec=pltpu.PrefetchScalarGridSpec(
            num_scalar_prefetch=1,
            grid=(FEED_BLOCKS,),
            in_specs=[
                pl.BlockSpec((tokens, width), whole, pipeline_mode=once),
                pl.BlockSpec((tokens, width), whole, pipeline_mode=once),
                pl.BlockSpec((1, cols), block),
                pl.BlockSpec((1, width), whole),
                anywhere,
                anywhere,
            ]
            + [anywhere] * len(pieces),
            out_specs=[
                pl.BlockSpec((tokens, width), whole, pipeline_mode=once),
                pl.BlockSpec((tokens, width), whole, pipeline_mode=once),
                pl.BlockSpec((1, cols), block),
            ]
            + [anywhere] * 2,
            scratch_shapes=[
                pltpu.VMEM((2, width, cols), bf16),
                pltpu.VMEM((2, cols, width), bf16),
                pltpu.VMEM((2, width, cols), bf16),
                pltpu.VMEM((2, cols, width), bf16),
                pltpu.VMEM((tokens, width), f32),
                pltpu.VMEM((width, tokens), bf16),
                pltpu.VMEM((tokens, cols), bf16),
                pltpu.VMEM((tokens, cols), bf16),
                pltpu.SemaphoreType.DMA((2, 2)),
                pltpu.SemaphoreType.DMA((2, 2)),
                pltpu.SemaphoreType.DMA,
            ],
        ),
        out_shape=[
            jax.ShapeDtypeStruct((tokens, width), bf16),
            jax.ShapeDtypeStruct((tokens, width), f32),
            jax.ShapeDtypeStruct((1, hidden), f32),
        ]
        + [jax.ShapeDtypeStruct((count // 2, width // count, 2 * hidden), bf16)] * 2,
        compiler_params=pltpu.CompilerParams(vmem_limit_bytes=vmem_most),
        cost_estimate=cost(20),
    )(me, x, grad, bias, shift, middle, up, *[v for v, _ in pieces])


def weight_kernel(where, left, count, me_ref, x_ref, g_ref, *refs):
    outs, (xt, staged, sem) = refs[-5:-3], refs[-3:]
    j = pl.program_id(0)
    me = me_ref[0]
    slot = lax.rem(j, 2)
    width, cols = staged.shape[1:]
    rows = width // count

    @pl.when(j == 0)
    def _():
        xt[...] = x_ref[...].T

    @pl.when(j >= 2)
    def _():
        pltpu.make_async_copy(staged.at[slot], staged.at[slot], sem.at[slot]).wait()

    staged[slot] = dot_n(xt[...], g_ref[...].reshape(g_ref.shape[-2:])).astype(bf16)
    at = pl.multiple_of(left + j * cols, cols)
    for out, rel in zip(outs, where):
        for n, p in enumerate(rel):
            start = pl.multiple_of(lax.bitwise_xor(me, p) * rows, rows)
            pltpu.make_async_copy(
                staged.at[slot, pl.ds(start, rows), :], out.at[n, :, pl.ds(at, cols)], sem.at[slot]
            ).start()

    @pl.when(j == pl.num_programs(0) - 1)
    def _():
        for s in range(2):
            pltpu.make_async_copy(staged.at[s], staged.at[s], sem.at[s]).wait()


def weight_grad(x, grad, where, left, total, me, into=()):
    tokens, width = x.shape
    count = sum(len(q) for q in where)
    cols = 512
    deep = grad.ndim == 3
    found = grad.shape[-1] * (grad.shape[0] if deep else 1)
    per = grad.shape[-1] // cols
    if deep:
        spec = pl.BlockSpec((1, tokens, cols), lambda j, m: (j // per, 0, j % per))
    else:
        spec = pl.BlockSpec((tokens, cols), lambda j, m: (0, j))
    anywhere = pl.BlockSpec(memory_space=pl.ANY)
    return pl.pallas_call(
        functools.partial(weight_kernel, where, left, count),
        grid_spec=pltpu.PrefetchScalarGridSpec(
            num_scalar_prefetch=1,
            grid=(found // cols,),
            in_specs=[pl.BlockSpec((tokens, width), lambda j, m: (0, 0)), spec]
            + [anywhere] * len(into),
            out_specs=[anywhere] * 2,
            scratch_shapes=[
                pltpu.VMEM((width, tokens), bf16),
                pltpu.VMEM((2, width, cols), bf16),
                pltpu.SemaphoreType.DMA((2,)),
            ],
        ),
        out_shape=[jax.ShapeDtypeStruct((count // 2, width // count, total), bf16)] * 2,
        input_output_aliases={3 + i: i for i in range(len(into))},
        compiler_params=pltpu.CompilerParams(vmem_limit_bytes=vmem_most),
        cost_estimate=cost(0.5 * found / 512),
    )(me, x, grad, *into)


def sort_kernel(x_ref, g_ref, x_out, g_out, sum_ref, wide):
    for source, target in ((x_ref, x_out), (g_ref, g_out)):
        wide[...] = source[...].astype(f32)
        for f in range(FRAMES):
            at = f * FRAME_ROWS + 2
            target[f * PATCH : (f + 1) * PATCH, :] = wide[at : at + PATCH, :].astype(bf16)
        few = [wide[f * FRAME_ROWS : f * FRAME_ROWS + 2, :] for f in range(FRAMES)]
        few = jnp.concatenate(few + [jnp.zeros((EXTRA - FEW, wide.shape[1]), f32)], axis=0)
        target[BODY:ROWS, :] = few.astype(bf16)
    sum_ref[...] = jnp.sum(wide[...], axis=0, keepdims=True)


def sort_rows(x, grad):
    tokens, width = x.shape
    return pl.pallas_call(
        sort_kernel,
        out_shape=[jax.ShapeDtypeStruct((ROWS, width), bf16)] * 2
        + [jax.ShapeDtypeStruct((1, width), f32)],
        scratch_shapes=[pltpu.VMEM((tokens, width), f32)],
        compiler_params=pltpu.CompilerParams(vmem_limit_bytes=vmem_most),
        cost_estimate=cost(1),
    )(x, grad)


def unsort_kernel(x_ref, out_ref, *scratch):
    wide = scratch[0] if scratch else out_ref
    for f in range(FRAMES):
        at = f * FRAME_ROWS
        wide[at + 2 : at + FRAME_ROWS, :] = x_ref[f * PATCH : (f + 1) * PATCH, :].astype(f32)
    few = x_ref[BODY:ROWS, :].astype(f32)
    for f in range(FRAMES):
        wide[f * FRAME_ROWS : f * FRAME_ROWS + 2, :] = few[2 * f : 2 * f + 2]
    if scratch:
        out_ref[...] = wide[...].astype(out_ref.dtype)


def unsort_rows(x):
    tokens, width = FRAMES * FRAME_ROWS, x.shape[1]
    return pl.pallas_call(
        unsort_kernel,
        out_shape=jax.ShapeDtypeStruct((tokens, width), x.dtype),
        scratch_shapes=[] if x.dtype == f32 else [pltpu.VMEM((tokens, width), f32)],
        compiler_params=pltpu.CompilerParams(vmem_limit_bytes=vmem_most),
        cost_estimate=cost(1),
    )(x)


def last_kernel(g_ref, w_ref, x_ref, mid_ref, gain_ref, out_ref, gain_out, bias_out, sum_ref, acc):
    i = pl.program_id(0)
    g = g_ref[0]
    more = dot_t(g, w_ref[...])

    @pl.when(i == 0)
    def _():
        acc[...] = more

    @pl.when(i > 0)
    def _():
        acc[...] += more

    sum_ref[0] = jnp.sum(g.astype(f32), axis=0, keepdims=True)

    @pl.when(i == pl.num_programs(0) - 1)
    def _():
        gain = gain_ref[...]
        gain_sum, bias_sum = 0.0, 0.0
        spans = [(f * PATCH, PATCH) for f in range(FRAMES)] + [(BODY, EXTRA)]
        for at, size in spans:
            rows = slice(at, at + size)
            x = x_ref[rows, :].astype(f32)
            center = x - jnp.mean(x, axis=-1, keepdims=True)
            inverse = lax.rsqrt(jnp.mean(center * center, axis=-1, keepdims=True) + eps_norm)
            unit = center * inverse
            grad = acc[rows, :]
            gain_sum += jnp.sum(grad * unit, axis=0, keepdims=True)
            bias_sum += jnp.sum(grad, axis=0, keepdims=True)
            scaled = grad * gain
            mean_grad = jnp.mean(scaled, axis=-1, keepdims=True)
            mean_cross = jnp.mean(scaled * unit, axis=-1, keepdims=True)
            found = mid_ref[rows, :] + inverse * (scaled - mean_grad - unit * mean_cross)
            if size == PATCH:
                start = at // PATCH * FRAME_ROWS + 2
                out_ref[start : start + PATCH, :] = found
            else:
                for f in range(FRAMES):
                    out_ref[f * FRAME_ROWS : f * FRAME_ROWS + 2, :] = found[2 * f : 2 * f + 2]
        gain_out[...] = gain_sum
        bias_out[...] = bias_sum


def last_step(grad_mixed, w, x, middle, gain):
    parts, rows, width = grad_mixed.shape

    def whole(i):
        return (0, 0)

    once = pl.Buffered(1)
    return pl.pallas_call(
        last_kernel,
        grid=(parts,),
        in_specs=[
            pl.BlockSpec((1, rows, width), lambda i: (i, 0, 0)),
            pl.BlockSpec((width, width), lambda i: (0, i)),
            pl.BlockSpec((rows, width), whole, pipeline_mode=once),
            pl.BlockSpec((rows, width), whole, pipeline_mode=once),
            pl.BlockSpec((1, width), whole),
        ],
        out_specs=[
            pl.BlockSpec((FRAMES * FRAME_ROWS, width), whole, pipeline_mode=once),
            pl.BlockSpec((1, width), whole),
            pl.BlockSpec((1, width), whole),
            pl.BlockSpec((1, 1, width), lambda i: (i, 0, 0)),
        ],
        out_shape=[
            jax.ShapeDtypeStruct((FRAMES * FRAME_ROWS, width), f32),
            jax.ShapeDtypeStruct((1, width), f32),
            jax.ShapeDtypeStruct((1, width), f32),
            jax.ShapeDtypeStruct((parts, 1, width), f32),
        ],
        scratch_shapes=[pltpu.VMEM((rows, width), f32)],
        compiler_params=pltpu.CompilerParams(vmem_limit_bytes=vmem_most),
        cost_estimate=cost(5),
    )(grad_mixed, w, x, middle, gain)


def normalize(values, gain, bias_add):
    center = values - jnp.mean(values, axis=-1, keepdims=True)
    scale_inv = lax.rsqrt(jnp.mean(center * center, axis=-1, keepdims=True) + eps_norm)
    unit_rows = center * scale_inv
    return (unit_rows * gain + bias_add, unit_rows, scale_inv)


def norm_back(grad_out, unit_rows, scale_inv, gain):
    scaled = grad_out * gain
    mean_grad = jnp.mean(scaled, axis=-1, keepdims=True)
    mean_cross = jnp.mean(scaled * unit_rows, axis=-1, keepdims=True)
    return scale_inv * (scaled - mean_grad - unit_rows * mean_cross)


def gather_joined(groups, orders, core, sizes):
    found = []
    for pieces, order in zip(groups, orders):
        for bit in order[:-1]:
            pieces = pieces + moved(pieces, bit, sizes)
        arrays, rels = zip(*pieces)
        pieces = [(jnp.concatenate(arrays, axis=0), sum(rels, []))]
        found += pieces + moved(pieces, order[-1], sizes)
    return found + moved(found, core, sizes)


def gather_rest(groups, orders, core, sizes):
    found = []
    for pieces, order in zip(groups, orders):
        for bit in order:
            pieces = pieces + moved(pieces, bit, sizes)
        found += pieces
    return found + moved(found, core, sizes)


def body(
    sizes,
    tokens,
    frame_ids,
    pad_mask,
    episode_offsets,
    ln1_gain,
    ln1_bias,
    w_qkv,
    b_qkv,
    w_out,
    b_out,
    ln2_gain,
    ln2_bias,
    w_up,
    b_up,
    w_down,
    b_down,
    cotangent,
):
    width = tokens.shape[1]
    count = sizes[0] * sizes[1]
    me = (lax.axis_index("dp") * sizes[1] + lax.axis_index("fsdp")).astype(jnp.int32)[None]
    core, line, orders = bit_orders(sizes)
    where = relatives(line, orders, core)
    out_matrix = lax.all_gather(w_out, ("dp", "fsdp"), axis=0, tiled=True)
    up_matrix = lax.all_gather(w_up, ("dp", "fsdp"), axis=0, tiled=True)
    smalls = [ln1_gain, ln1_bias, b_qkv, b_out, ln2_gain, ln2_bias, b_up, b_down]
    rows, third = w_qkv.shape
    first_unit = jnp.concatenate([w_qkv, pack_small(smalls, rows)], axis=1)
    firsts = gather_line(first_unit, line, sizes)
    tokens_in, cot, grad_b_down_local = sort_rows(tokens, cotangent)
    first = gather_joined(firsts, orders, core, sizes)
    seen = seen_frames(episode_offsets[0])
    hide = hidden_few(seen)
    cosine, sine = turn_tables(frame_ids)
    partner = partner_matrix()
    values_in = tokens_in.astype(f32)
    qkv_matrix, whole_small = assemble(
        first, me, [(0, rows, 0, third), (0, rows, third, first_unit.shape[1] - third)]
    )
    gain_one, bias_one, qkv_rows, out_bias, gain_two, bias_two, up_bias, down_bias = unpack_small(
        whole_small, rows, smalls
    )
    stacked = [w_down[at : at + rows] for at in range(0, w_down.shape[0], rows)]
    second_unit = after(jnp.concatenate(stacked, axis=1), qkv_matrix)
    seconds = gather_line(second_unit, line, sizes)
    normed_one, unit_one, inv_one = normalize(values_in, gain_one, bias_one)
    normed_one = normed_one.astype(bf16)
    qkv = project(normed_one, qkv_matrix, qkv_rows.reshape(1, 3 * width), cosine, sine, partner)
    pairs = width // (2 * HEAD)
    seconds = [after_pieces(pieces, qkv) for pieces in seconds]
    seconds = [
        [pieces, moved(pieces, order[0], sizes) + moved(pieces, order[1], sizes)]
        for pieces, order in zip(seconds, orders)
    ]
    attended, lse_a, few_a = attend(seen, qkv, hide, 0, pairs // 2)
    seconds = [[near, after_pieces(far, attended)] for near, far in seconds]
    found = []
    for (near, far), order in zip(seconds, orders):
        pieces = near + far + moved(far[:1], order[1], sizes)
        for bit in order[2:]:
            pieces = pieces + moved(pieces, bit, sizes)
        found.append(pieces)
    attended, lse_b, few_b = attend(seen, qkv, hide, pairs // 2, pairs, attended)
    second = []
    for pieces in found:
        arrays, rels = zip(*pieces)
        pieces = [(after(jnp.concatenate(arrays, axis=0), attended), sum(rels, []))]
        second += pieces + moved(pieces, core, sizes)
    hidden = w_up.shape[1]
    middle = values_in + jnp.dot(attended, out_matrix, preferred_element_type=f32) + out_bias
    normed_two, unit_two, inv_two = normalize(middle, gain_two, bias_two)
    normed_two = normed_two.astype(bf16)
    result, grad_normed_two, grad_b_up_local, feed_own, feed_other = feed(
        normed_two,
        cot,
        middle,
        up_bias[None],
        down_bias[None],
        up_matrix,
        second,
        line,
        orders,
        core,
        me,
    )
    feed_taken = swap(feed_other, 1 << core, sizes)
    grad_gain_two = jnp.sum(grad_normed_two * unit_two, axis=0)
    grad_bias_two = jnp.sum(grad_normed_two, axis=0)
    grad_middle = cot.astype(f32) + norm_back(grad_normed_two, unit_two, inv_two, gain_two)
    grad_branch = grad_middle.astype(bf16)
    grad_b_out_local = jnp.sum(grad_branch.astype(f32), axis=0)
    grads = weight_grad(attended, grad_branch, where, third, third + width, me)
    grad_attended = dot_t(grad_branch, out_matrix).astype(bf16)
    feed_sums = reduce_start(feed_own, feed_taken, orders, sizes)
    grad_attended = after(grad_attended, grads[0], *[v for group in feed_sums for v in group[:1] + group[2:]])
    feed_sums = [group[:2] for group in feed_sums]
    back = (hide, cosine, sine, partner)
    grad_mixed = attend_back(
        seen, qkv, attended, grad_attended, lse_a, few_a, *back, 0, pairs // 2
    )
    grad_mixed = attend_back(
        seen, qkv, attended, grad_attended, lse_b, few_b, *back, pairs // 2, pairs, grad_mixed
    )
    steps = len(orders[0])
    for step in range(1, steps):
        feed_sums = reduce_next(feed_sums, orders, step, sizes)
        grad_mixed = after(grad_mixed, *[v for group in feed_sums for v in group[:1] + group[2:]])
        feed_sums = [group[:2] for group in feed_sums]
    own, other = weight_grad(normed_one, grad_mixed, where, 0, third + width, me, grads)
    taken = swap(other, 1 << core, sizes)
    grad_mixed = after(grad_mixed, other)
    grad_tokens, grad_gain_one, grad_bias_one, grad_b_qkv_local = last_step(
        grad_mixed, qkv_matrix, tokens_in, grad_middle, gain_one[None]
    )
    vectors = [
        grad_gain_one[0],
        grad_bias_one[0],
        grad_b_qkv_local[:, 0],
        grad_b_out_local,
        grad_gain_two,
        grad_bias_two,
        grad_b_up_local[0],
        grad_b_down_local[0],
    ]
    small_own, small_other = small_units(vectors, rows, where, me)
    sums = reduce_start(
        own, taken, orders, sizes, jnp.concatenate([small_own, small_other], axis=2)
    )
    feed_parts = line_parts(feed_sums)
    going = [v for group in sums for v in group[:1] + group[2:]]
    feed_parts = feed_parts[:1] + [after(v.astype(bf16), *going) for v in feed_parts[1:]]
    sums = [group[:2] for group in sums]
    for step in range(1, steps):
        sums = [group[:2] for group in reduce_next(sums, orders, step, sizes)]
    parts = line_parts(sums)
    parts = parts[:1] + [v.astype(bf16) for v in parts[1:]]
    feed_parts[0] = after(feed_parts[0], *parts[1:])
    result = after(result, *going)
    feed_sum = reduce_line(feed_parts, line, sizes)
    sum_one = reduce_line(parts, line, sizes)
    output = unsort_rows(result)
    small = sum_one[:, third + width :]
    small = small[:, :128] + swap(small[:, 128:], 1 << core, sizes)
    small = small_parts(small, vectors, count)
    sum_down = feed_sum[:, hidden:].reshape(rows, -1, width).swapaxes(0, 1).reshape(-1, width)
    return (
        output,
        grad_tokens,
        small[0],
        small[1],
        sum_one[:, :third],
        small[2],
        sum_one[:, third : third + width],
        small[3],
        small[4],
        small[5],
        feed_sum[:, :hidden],
        small[6],
        sum_down,
        small[7],
    )


def solution(mesh):
    placed = (
        P(("dp", "fsdp"), None),
        P(("dp", "fsdp")),
        P(("dp", "fsdp")),
        P(("dp", "fsdp"), None),
        P(("dp", "fsdp")),
        P(("dp", "fsdp")),
        P(("dp", "fsdp"), None),
        P(None, ("dp", "fsdp")),
        P(("dp", "fsdp"), None),
        P(("dp", "fsdp")),
        P(("dp", "fsdp")),
        P(("dp", "fsdp")),
        P(("dp", "fsdp"), None),
        P(("dp", "fsdp")),
        P(("dp", "fsdp"), None),
        P(("dp", "fsdp")),
        P(("dp", "fsdp"), None),
    )
    sizes = (mesh.shape["dp"], mesh.shape["fsdp"])
    return jax.shard_map(
        functools.partial(body, sizes),
        mesh=mesh,
        in_specs=placed,
        out_specs=(
            P(("dp", "fsdp"), None),
            P(("dp", "fsdp"), None),
            P(("dp", "fsdp")),
            P(("dp", "fsdp")),
            P(("dp", "fsdp"), None),
            P(None, ("dp", "fsdp")),
            P(("dp", "fsdp"), None),
            P(("dp", "fsdp")),
            P(("dp", "fsdp")),
            P(("dp", "fsdp")),
            P(("dp", "fsdp"), None),
            P(("dp", "fsdp")),
            P(("dp", "fsdp"), None),
            P(("dp", "fsdp")),
        ),
        check_vma=False,
    )
```

```python
import functools
import math

import jax
import jax.numpy as jnp
import numpy as np
from jax import lax
from jax.experimental import pallas as pl
from jax.experimental.pallas import tpu as pltpu
from jax.sharding import PartitionSpec as P

HEAD = 64
GRID = 16
FRAME_ROWS = 258
FRAMES = 4
PATCH = GRID * GRID
EXTRA = 16
FEW = 8
BODY = FRAMES * PATCH
ROWS = BODY + EXTRA
eps_norm = 1e-06
part_sizes = (24, 20, 20)
masked_value = -1e30
inv_sqrt_two = 1.0 / math.sqrt(2.0)
inv_sqrt_tau = 1.0 / math.sqrt(2.0 * math.pi)
f32 = jnp.float32
bf16 = jnp.bfloat16
vmem_most = 60 * 1024 * 1024


def cost(micros):
    return pl.CostEstimate(flops=int(micros * 1e9), bytes_accessed=0, transcendentals=0)


def log2(n):
    return n.bit_length() - 1


def swap(value, mask, sizes):
    count = sizes[0] * sizes[1]
    return lax.ppermute(value, ("dp", "fsdp"), [(i, i ^ mask) for i in range(count)])


def bit_orders(sizes):
    inner, outer = log2(sizes[1]), log2(sizes[0])
    line = list(range(1, inner))
    cross = [0]
    other = list(range(inner + 1, inner + outer))
    return inner, line, (cross + other, other + cross)


def spread(bits):
    rel = [0]
    for bit in bits:
        rel = rel + [p | (1 << bit) for p in rel]
    return rel


def gather_line(shard, line, sizes):
    rel = spread(line)
    held = [shard[None]] + [swap(shard[None], p, sizes) for p in rel[1:]]
    half = len(rel) // 2
    return [
        [(jnp.concatenate(held[at : at + half], axis=0), rel[at : at + half])]
        for at in (0, half)
    ]


def gather_doubling(shard, line, sizes):
    held, rel = shard[None], [0]
    for bit in line[:-1]:
        held = jnp.concatenate([held, swap(held, 1 << bit, sizes)], axis=0)
        rel = rel + [p | (1 << bit) for p in rel]
    return [[(held, rel)], moved([(held, rel)], line[-1], sizes)]


def moved(pieces, bit, sizes):
    return [(swap(v, 1 << bit, sizes), [p | (1 << bit) for p in q]) for v, q in pieces]


def relatives(line, orders, core):
    low, top = line[:-1], 1 << line[-1]
    rel = spread(low + orders[0]) + [p | top for p in spread(low + orders[1])]
    return rel, [p | (1 << core) for p in rel]


def reduce_start(own, taken, orders, sizes):
    half = own.shape[0] // 2
    return [
        reduce_step(own[at : at + half], taken[at : at + half], 1 << order[-1], sizes)
        for at, order in zip((0, half), orders)
    ]


def reduce_step(kept, taken, mask, sizes):
    kind = kept.dtype
    half = kept.shape[0] // 2
    sent = (kept[half:].astype(f32) + taken[half:].astype(f32)).astype(kind)
    held = (kept[:half].astype(f32) + taken[:half].astype(f32)).astype(kind)
    return held, swap(sent, mask, sizes), sent


def reduce_next(groups, orders, step, sizes):
    return [
        reduce_step(*group, 1 << order[-1 - step], sizes) for group, order in zip(groups, orders)
    ]


def together(groups):
    (kept, came), (other_kept, other_came) = groups
    came = after(came, other_came)
    return [(kept, came), (other_kept, after(other_came, came))]


def after_pieces(pieces, *others):
    return [(after(v, *others), q) for v, q in pieces]


def line_parts(groups):
    return [
        kept[n].astype(f32) + taken[n].astype(f32)
        for kept, taken in groups
        for n in range(kept.shape[0])
    ]


def reduce_line(parts, line, sizes):
    total = parts[0]
    for part, p in zip(parts[1:], spread(line)[1:]):
        total = total + swap(part, p, sizes).astype(f32)
    return total


def after_kernel(*refs):
    del refs


def after(value, *others):
    anywhere = pl.BlockSpec(memory_space=pl.ANY)
    return pl.pallas_call(
        after_kernel,
        out_shape=jax.ShapeDtypeStruct(value.shape, value.dtype),
        in_specs=[anywhere] * (1 + len(others)),
        out_specs=anywhere,
        input_output_aliases={0: 0},
        cost_estimate=cost(0),
    )(value, *others)


def assemble_kernel(rels, parts, me_ref, *refs):
    pieces, refs = refs[: len(rels)], refs[len(rels) :]
    outs, sems = refs[: len(parts)], refs[-1]
    me = me_ref[0]
    for k, (top, height, left, cols) in enumerate(parts):
        for piece, rel in zip(pieces, rels):
            for at, p in enumerate(rel):
                start = pl.multiple_of(lax.bitwise_xor(me, p) * height, height)
                pltpu.make_async_copy(
                    piece.at[at, pl.ds(top, height), pl.ds(left, cols)],
                    outs[k].at[pl.ds(start, height)],
                    sems.at[k],
                ).start()
    for k, out in enumerate(outs):
        pltpu.make_async_copy(out, out, sems.at[k]).wait()


def assemble(pieces, me, parts):
    rels = [q for _, q in pieces]
    count = sum(len(q) for q in rels)
    total = sum(h * c for _, h, _, c in parts)
    return pl.pallas_call(
        functools.partial(assemble_kernel, rels, parts),
        out_shape=[jax.ShapeDtypeStruct((count * h, c), bf16) for _, h, _, c in parts],
        in_specs=[pl.BlockSpec(memory_space=pltpu.SMEM)]
        + [pl.BlockSpec(memory_space=pl.ANY)] * len(pieces),
        scratch_shapes=[pltpu.SemaphoreType.DMA((len(parts),))],
        compiler_params=pltpu.CompilerParams(vmem_limit_bytes=vmem_most),
        cost_estimate=cost(1.5),
    )(me, *[v for v, _ in pieces])


def pack_small(parts, rows):
    def fill(blocks):
        blocks = [jnp.pad(v, ((0, 0), (0, 128 - v.shape[1]))) for v in blocks]
        used = sum(v.shape[0] for v in blocks)
        return jnp.concatenate(blocks + [jnp.zeros((rows - used, 128), bf16)], axis=0)

    flat = fill([v[None] for v in parts if v.ndim == 1])
    return jnp.concatenate([flat] + [fill([v]) for v in parts if v.ndim == 2], axis=1)


def unpack_small(whole, rows, parts):
    whole = whole.reshape(-1, rows, whole.shape[1]).astype(f32)
    found, at, left = [], 0, 128
    for v in parts:
        size = v.shape[-1]
        if v.ndim == 2:
            block = whole[:, : v.shape[0], left : left + size].swapaxes(0, 1)
            found.append(block.reshape(v.shape[0], -1))
            left += 128
        else:
            found.append(whole[:, at, :size].reshape(-1))
            at += 1
    return found


def small_units(parts, rows, where, me):
    count = sum(len(q) for q in where)
    blocks = [
        v.reshape(count, -1)
        if v.ndim == 1
        else v.reshape(v.shape[0], count, -1).swapaxes(0, 1).reshape(count, -1)
        for v in parts
    ]
    flat = jnp.concatenate(blocks, axis=1)
    flat = jnp.pad(flat, ((0, 0), (0, rows * 128 - flat.shape[1]))).reshape(count, rows, 128)
    index = lax.bitwise_xor(jnp.asarray(where[0] + where[1], jnp.int32), me[0])
    mixed = jnp.take(flat, index, axis=0)
    return mixed[: count // 2], mixed[count // 2 :]


def small_parts(unit, parts, count):
    flat = unit.reshape(-1)
    found, at = [], 0
    for v in parts:
        size = v.size // count
        block = flat[at : at + size]
        found.append(block if v.ndim == 1 else block.reshape(v.shape[0], -1))
        at = at + size
    return found


def dot_t(a, b):
    return lax.dot_general(a, b, (((1,), (1,)), ((), ())), preferred_element_type=f32)


def dot_n(a, b):
    return lax.dot_general(a, b, (((1,), (0,)), ((), ())), preferred_element_type=f32)


def dot_tl(a, b):
    return lax.dot_general(a, b, (((0,), (0,)), ((), ())), preferred_element_type=f32)


def head_lanes(a, rows):
    lane = lax.broadcasted_iota(jnp.int32, (rows, 2 * HEAD), 1)
    return (lane >= HEAD) if a else (lane < HEAD)


def keep_head(x, a):
    return jnp.where(head_lanes(a, x.shape[0]), x, jnp.zeros_like(x))


def stack_heads(x):
    head = lax.broadcasted_iota(jnp.int32, x.shape, 1) // HEAD
    heads = x.shape[1] // HEAD
    return jnp.concatenate([jnp.where(head == a, x, jnp.zeros_like(x)) for a in range(heads)], axis=0)


def join_heads(x):
    heads = x.shape[0] // FEW
    head = lax.broadcasted_iota(jnp.int32, (FEW, x.shape[1]), 1) // HEAD
    found = x[:FEW]
    for a in range(1, heads):
        found = jnp.where(head == a, x[a * FEW : (a + 1) * FEW], found)
    return found


def few_rows(x):
    return jnp.concatenate([x, jnp.zeros_like(x)], axis=0)


def hide_few(s, first, last):
    row = lax.broadcasted_iota(jnp.int32, (EXTRA, s.shape[1]), 0)
    frame = lax.shift_right_logical(row, 1)
    seen = (frame >= first) & (frame <= last)
    count = s.shape[0] - EXTRA
    return jnp.concatenate([s[:count], jnp.where(seen, s[count:], masked_value)], axis=0)


def seen_rows(ref, lanes, lo, n):
    return jnp.concatenate([ref[pl.ds(lo, n * PATCH), lanes], ref[BODY:ROWS, lanes]], axis=0)


def seen_lanes(ref, a, lo, n):
    rows = slice(a * HEAD, (a + 1) * HEAD)
    return jnp.concatenate([ref[rows, pl.ds(lo, n * PATCH)], ref[rows, BODY:ROWS]], axis=1)


def pair_lanes(a):
    at = a // 2 * 2 * HEAD
    return slice(at, at + 2 * HEAD)


def attend_kernel(seen_ref, q_ref, k_ref, v_ref, hide_ref, out_ref, lse_ref, few_ref, vt):
    f = pl.program_id(1)
    heads = q_ref.shape[1] // HEAD

    @pl.when(f == 0)
    def _():
        vt[...] = v_ref[...].T
        qs = stack_heads(q_ref[BODY:ROWS, :].astype(f32)[:FEW]).astype(bf16)
        s = dot_t(k_ref[...], qs) + hide_ref[...]
        top = jnp.max(s, axis=0, keepdims=True)
        p = jnp.exp(s - top)
        total = jnp.sum(p, axis=0, keepdims=True)
        o = dot_tl((p / total).astype(bf16), v_ref[...])
        out_ref[BODY:ROWS, :] = few_rows(join_heads(o)).astype(bf16)
        few_ref[0] = top + jnp.log(total)

    row = pl.multiple_of(f * PATCH, PATCH)
    seen = seen_ref[f]

    @pl.when(seen == 0)
    def _():
        out_ref[pl.ds(row, PATCH), :] = v_ref[pl.ds(row, PATCH), :]
        lse_ref[0, :, pl.ds(row, PATCH)] = jnp.zeros((heads, PATCH), f32)

    for n in range(1, FRAMES + 1):

        @pl.when(seen == n)
        def _(n=n):
            first = f - (n - 1)
            lo = pl.multiple_of(first * PATCH, PATCH)

            def score(a):
                lanes = pair_lanes(a)
                q = keep_head(q_ref[pl.ds(row, PATCH), lanes], a % 2)
                return hide_few(dot_t(seen_rows(k_ref, lanes, lo, n), q), first, f)

            ahead = 4
            scores = [score(a) for a in range(ahead)]
            outs, sums = [], []
            for a in range(heads):
                s = scores[a]
                top = jnp.max(s, axis=0, keepdims=True)
                p = jnp.exp(s - top)
                total = jnp.sum(p, axis=0, keepdims=True)
                if a + ahead < heads:
                    scores.append(score(a + ahead))
                o = dot_n(seen_lanes(vt, a, lo, n), p.astype(bf16))
                outs.append(o / total)
                sums.append(top + jnp.log(total))
            out_ref[pl.ds(row, PATCH), :] = jnp.concatenate(outs, axis=0).T.astype(bf16)
            lse_ref[0, :, pl.ds(row, PATCH)] = jnp.concatenate(sums, axis=0)


PAIRS = 4


def attend(seen, qkv, hide, pair_lo, pair_hi, kept=None):
    width = qkv.shape[1] // 3
    lanes = 2 * HEAD * PAIRS
    groups = width // lanes
    at = pair_lo // PAIRS
    some = (pair_hi - pair_lo) // PAIRS
    kernel = attend_kernel
    more, alias = [], {}
    if kept is not None:
        more, alias = [kept], {5: 0}

        def kernel(seen_ref, q_ref, k_ref, v_ref, hide_ref, kept_ref, *refs):
            attend_kernel(seen_ref, q_ref, k_ref, v_ref, hide_ref, *refs)

    return pl.pallas_call(
        kernel,
        grid_spec=pltpu.PrefetchScalarGridSpec(
            num_scalar_prefetch=1,
            grid=(some, FRAMES),
            in_specs=[
                pl.BlockSpec((ROWS, lanes), lambda h, f, s: (0, at + h)),
                pl.BlockSpec((ROWS, lanes), lambda h, f, s: (0, at + groups + h)),
                pl.BlockSpec((ROWS, lanes), lambda h, f, s: (0, at + 2 * groups + h)),
                pl.BlockSpec((ROWS, 2 * PAIRS * FEW), lambda h, f, s: (0, 0)),
            ]
            + [pl.BlockSpec(memory_space=pl.ANY)] * len(more),
            out_specs=[
                pl.BlockSpec((ROWS, lanes), lambda h, f, s: (0, at + h)),
                pl.BlockSpec((1, 2 * PAIRS, BODY), lambda h, f, s: (h, 0, 0)),
                pl.BlockSpec((1, 1, 2 * PAIRS * FEW), lambda h, f, s: (h, 0, 0)),
            ],
            scratch_shapes=[pltpu.VMEM((lanes, ROWS), bf16)],
        ),
        out_shape=(
            jax.ShapeDtypeStruct((ROWS, width), bf16),
            jax.ShapeDtypeStruct((some, 2 * PAIRS, BODY), f32),
            jax.ShapeDtypeStruct((some, 1, 2 * PAIRS * FEW), f32),
        ),
        input_output_aliases=alias,
        compiler_params=pltpu.CompilerParams(vmem_limit_bytes=vmem_most),
        cost_estimate=cost(6.4 * some),
    )(seen, qkv, qkv, qkv, hide, *more)


def unturn(x, cosine, sine, partner):
    return x * cosine - dot_n(x.astype(bf16), partner) * sine


def attend_back_kernel(
    scale, seen_ref, q_ref, k_ref, v_ref, o_ref, g_ref, lse_ref, few_ref, hide_ref, cos_ref, sin_ref,
    part_ref, out_ref, kt, dq, dk, dv,
):
    f = pl.program_id(1)
    heads = q_ref.shape[1] // HEAD
    pairs = [slice(p * 2 * HEAD, (p + 1) * 2 * HEAD) for p in range(heads // 2)]
    ones = jnp.where(
        (lax.broadcasted_iota(jnp.int32, (8, 2 * HEAD), 1) >= HEAD).astype(jnp.int32)
        == lax.broadcasted_iota(jnp.int32, (8, 2 * HEAD), 0),
        1.0,
        0.0,
    ).astype(bf16)

    @pl.when(f == 0)
    def _():
        kt[...] = k_ref[...].T
        qs = stack_heads(q_ref[BODY:ROWS, :].astype(f32)[:FEW]).astype(bf16)
        gs = stack_heads(g_ref[BODY:ROWS, :].astype(f32)[:FEW]).astype(bf16)
        p = jnp.exp(dot_t(k_ref[...], qs) + hide_ref[...] - few_ref[0])
        gp = dot_t(v_ref[...], gs)
        delta = jnp.sum(gp * p, axis=0, keepdims=True)
        ds = (p * (gp - delta)).astype(bf16)
        dv[...] = dot_n(p.astype(bf16), gs)
        dk[...] = dot_n(ds, qs)
        dq[BODY:ROWS, :] = few_rows(join_heads(dot_tl(ds, k_ref[...])))

    row = pl.multiple_of(f * PATCH, PATCH)
    seen = seen_ref[f]

    @pl.when(seen == 0)
    def _():
        dv[pl.ds(row, PATCH), :] += g_ref[pl.ds(row, PATCH), :].astype(f32)
        dq[pl.ds(row, PATCH), :] = jnp.zeros((PATCH, heads * HEAD), f32)

    for n in range(1, FRAMES + 1):

        @pl.when(seen == n)
        def _(n=n):
            first = f - (n - 1)
            lo = pl.multiple_of(first * PATCH, PATCH)
            count = n * PATCH

            def start(a):
                lanes = pair_lanes(a)
                q = keep_head(q_ref[pl.ds(row, PATCH), lanes], a % 2)
                g = keep_head(g_ref[pl.ds(row, PATCH), lanes], a % 2)
                s = hide_few(dot_t(seen_rows(k_ref, lanes, lo, n), q), first, f)
                return q, g, s, dot_t(seen_rows(v_ref, lanes, lo, n), g)

            deltas = []
            for lanes in pairs:
                g = g_ref[pl.ds(row, PATCH), lanes].astype(f32)
                product = g * o_ref[pl.ds(row, PATCH), lanes].astype(f32)
                upper = product.astype(bf16)
                lower = (product - upper.astype(f32)).astype(bf16)
                deltas.append(dot_t(ones, upper) + dot_t(ones, lower))
            ahead = 4
            started = [start(a) for a in range(ahead)]
            back, add_k, add_v = [], None, None
            for a in range(heads):
                q, g, s, gp = started[a]
                p = jnp.exp(s - lse_ref[0, a : a + 1, pl.ds(row, PATCH)])
                ds = (p * (gp - deltas[a // 2][a % 2 : a % 2 + 1])).astype(bf16)
                p = p.astype(bf16)
                if a + ahead < heads:
                    started.append(start(a + ahead))
                more_v, more_k = dot_n(p, g), dot_n(ds, q)
                back.append(dot_n(seen_lanes(kt, a, lo, n), ds))
                if a % 2 == 0:
                    add_v, add_k = more_v, more_k
                else:
                    lanes = pairs[a // 2]
                    add_v, add_k = add_v + more_v, add_k + more_k
                    dk[pl.ds(lo, count), lanes] += add_k[:count]
                    dk[BODY:ROWS, lanes] += add_k[count:]
                    dv[pl.ds(lo, count), lanes] += add_v[:count]
                    dv[BODY:ROWS, lanes] += add_v[count:]
            dq[pl.ds(row, PATCH), :] = jnp.concatenate(back, axis=0).T

    @pl.when(f == FRAMES - 1)
    def _():
        partner = part_ref[...]
        for lanes in pairs:
            out_ref[0, :, lanes] = unturn(
                dq[:, lanes] * scale, cos_ref[...], sin_ref[...], partner
            ).astype(bf16)
            out_ref[1, :, lanes] = unturn(
                dk[:, lanes], cos_ref[...], sin_ref[...], partner
            ).astype(bf16)
        out_ref[2] = dv[...].astype(bf16)


def attend_back(
    seen, qkv, attended, grad, lse, few, hide, cosine, sine, partner, pair_lo, pair_hi, kept=None
):
    width = qkv.shape[1] // 3
    pair = 2 * HEAD
    lanes = pair * PAIRS
    groups = width // lanes
    at = pair_lo // PAIRS
    some = (pair_hi - pair_lo) // PAIRS
    inner = functools.partial(attend_back_kernel, 1.0 / math.sqrt(HEAD))
    kernel = inner
    more, alias = [], {}
    if kept is not None:
        more, alias = [kept], {12: 0}

        def kernel(*refs):
            inner(*refs[:12], *refs[13:])

    def whole(h, f, s):
        return (0, 0)

    return pl.pallas_call(
        kernel,
        grid_spec=pltpu.PrefetchScalarGridSpec(
            num_scalar_prefetch=1,
            grid=(some, FRAMES),
            in_specs=[
                pl.BlockSpec((ROWS, lanes), lambda h, f, s: (0, at + h)),
                pl.BlockSpec((ROWS, lanes), lambda h, f, s: (0, at + groups + h)),
                pl.BlockSpec((ROWS, lanes), lambda h, f, s: (0, at + 2 * groups + h)),
                pl.BlockSpec((ROWS, lanes), lambda h, f, s: (0, at + h)),
                pl.BlockSpec((ROWS, lanes), lambda h, f, s: (0, at + h)),
                pl.BlockSpec((1, 2 * PAIRS, BODY), lambda h, f, s: (h, 0, 0)),
                pl.BlockSpec((1, 1, 2 * PAIRS * FEW), lambda h, f, s: (h, 0, 0)),
                pl.BlockSpec((ROWS, 2 * PAIRS * FEW), whole),
                pl.BlockSpec((ROWS, pair), whole),
                pl.BlockSpec((ROWS, pair), whole),
                pl.BlockSpec((pair, pair), whole),
            ]
            + [pl.BlockSpec(memory_space=pl.ANY)] * len(more),
            out_specs=pl.BlockSpec((3, ROWS, lanes), lambda h, f, s: (0, 0, at + h)),
            scratch_shapes=[
                pltpu.VMEM((lanes, ROWS), bf16),
                pltpu.VMEM((ROWS, lanes), f32),
                pltpu.VMEM((ROWS, lanes), f32),
                pltpu.VMEM((ROWS, lanes), f32),
            ],
        ),
        out_shape=jax.ShapeDtypeStruct((3, ROWS, width), bf16),
        input_output_aliases=alias,
        compiler_params=pltpu.CompilerParams(vmem_limit_bytes=vmem_most),
        cost_estimate=cost(7.6 * some),
    )(seen, qkv, qkv, qkv, attended, grad, lse, few, hide, cosine, sine, partner, *more)


def project_kernel(scale, x_ref, w_ref, b_ref, cos_ref, sin_ref, part_ref, out_ref):
    j = pl.program_id(0)
    third = pl.num_programs(0) // 3
    lanes = 2 * HEAD
    wide = part_ref.shape[0]
    w = w_ref[...]
    mixed = dot_n(x_ref[...], w) + b_ref[...]

    @pl.when(j < 2 * third)
    def _():
        by = jnp.where(j < third, scale, 1.0)
        for left in range(0, w.shape[1], wide):
            x = mixed[:, left : left + wide]
            upper = x.astype(bf16)
            lower = (x - upper.astype(f32)).astype(bf16)
            other = dot_n(upper, part_ref[...]) + dot_n(lower, part_ref[...])
            for at in range(0, wide, lanes):
                here = mixed[:, left + at : left + at + lanes] * cos_ref[...]
                there = other[:, at : at + lanes] * sin_ref[...]
                out_ref[:, left + at : left + at + lanes] = ((here + there) * by).astype(bf16)

    @pl.when(j >= 2 * third)
    def _():
        out_ref[...] = mixed.astype(bf16)


def project(x, w, bias, cosine, sine, partner):
    rows, width = x.shape
    cols = 512
    lanes = 2 * HEAD
    wide = 2 * lanes
    zero = jnp.zeros_like(partner)
    partner = jnp.block([[partner, zero], [zero, partner]])

    def whole(j):
        return (0, 0)

    return pl.pallas_call(
        functools.partial(project_kernel, 1.0 / math.sqrt(HEAD)),
        grid=(w.shape[1] // cols,),
        in_specs=[
            pl.BlockSpec((rows, width), whole),
            pl.BlockSpec((width, cols), lambda j: (0, j)),
            pl.BlockSpec((1, cols), lambda j: (0, j)),
            pl.BlockSpec((rows, lanes), whole),
            pl.BlockSpec((rows, lanes), whole),
            pl.BlockSpec((wide, wide), whole),
        ],
        out_specs=pl.BlockSpec((rows, cols), lambda j: (0, j)),
        out_shape=jax.ShapeDtypeStruct((rows, w.shape[1]), bf16),
        compiler_params=pltpu.CompilerParams(vmem_limit_bytes=vmem_most),
        cost_estimate=cost(4),
    )(x, w, bias, cosine, sine, partner)


def turn_tables(frame_ids):
    frequency, which, sign = [], [], []
    for kind, part in enumerate(part_sizes):
        half = part // 2
        frequency += [10000.0 ** (-i / half) for i in range(half)] * 2
        which += [kind] * part
        sign += [-1.0] * half + [1.0] * half
    frequency = jnp.asarray(np.tile(np.array(frequency, np.float32), 2))
    which = np.tile(np.array(which), 2)
    sign = np.tile(np.array(sign, np.float32), 2)
    time = frame_ids[:: FRAME_ROWS].astype(f32)[:, None] * frequency
    place = np.arange(GRID, dtype=np.float32)[:, None] * frequency

    def table(of, empty):
        by_time, by_place = of(time), of(place)
        still = jnp.full((FRAMES, 2, which.size), empty, f32)
        patches = jnp.where(which == 1, by_place[:, None], by_place[None]).reshape(1, PATCH, -1)
        patches = jnp.where(which == 0, by_time[:, None], patches).reshape(BODY, -1)
        few = jnp.where(which == 0, by_time[:, None], still).reshape(FEW, -1)
        return jnp.concatenate([patches, few, jnp.zeros_like(few)], axis=0)

    return table(jnp.cos, 1.0), table(lambda v: jnp.sin(v) * sign, 0.0)


def partner_matrix():
    lanes = 2 * HEAD
    matrix = np.zeros((lanes, lanes), np.float32)
    for head in range(2):
        at = head * HEAD
        for part in part_sizes:
            for i in range(part // 2):
                matrix[at + i, at + i + part // 2] = 1.0
                matrix[at + i + part // 2, at + i] = 1.0
            at += part
    return jnp.asarray(matrix, bf16)


def seen_frames(offset_row):
    frame = jnp.arange(FRAMES, dtype=jnp.int32)
    start = jnp.where(frame >= offset_row[1], offset_row[1], 0)
    return jnp.where(frame < offset_row[2], frame - start + 1, 0)


def hidden_few(seen):
    frame_of = np.concatenate([np.repeat(np.arange(FRAMES), PATCH), np.repeat(np.arange(FRAMES), 2), np.full(EXTRA - FEW, FRAMES)])
    own = np.zeros((ROWS, FEW), bool)
    own[BODY + np.arange(FEW), np.arange(FEW)] = True
    frame = jnp.asarray(frame_of, jnp.int32)[:, None]
    query = jnp.arange(FEW, dtype=jnp.int32)[None, :] // 2
    count = jnp.repeat(seen, 2)[None, :]
    allowed = ((frame <= query) & (frame > query - count)) | jnp.asarray(own)
    return jnp.tile(jnp.where(allowed, 0.0, masked_value), (1, 2 * PAIRS))


def place(p, line, orders, core):
    own, other = relatives(line, orders, core)
    return (1, other.index(p)) if p in other else (0, own.index(p))


def find_piece(rels, p):
    for c, rel in enumerate(rels):
        if p in rel:
            return c, rel.index(p)
    raise ValueError(p)


def feed_kernel(
    rels, where, me_ref, x_ref, g_ref, bias_ref, shift_ref, mid_ref, up_ref, *refs
):
    pieces, refs = refs[: len(rels)], refs[len(rels) :]
    out_ref, gx_ref, gb_ref = refs[:3]
    grads = refs[3:5]
    wu, wd, su, sd, acc, xt, act, gup, in_sem, out_sem, mid_sem = refs[5:]
    count = sum(len(q) for q in rels)
    blocks = FEED_BLOCKS
    each = count // blocks
    shift = each.bit_length() - 1
    i = pl.program_id(0)
    me = me_ref[0]
    width = x_ref.shape[1]
    cols = wu.shape[2]
    rows = width // count
    part = cols // each
    hidden = blocks * cols
    stacks = part // rows
    slot = lax.rem(i, 2)

    def group(j):
        return lax.bitwise_xor(lax.shift_right_logical(me, shift), j)

    def fetch(j, to):
        at = pl.multiple_of(group(j) * cols, cols)
        pltpu.make_async_copy(up_ref.at[:, pl.ds(at, cols)], wu.at[to], in_sem.at[0, to]).start()
        for k in range(blocks):

            @pl.when(j == k)
            def _():
                for p in range(each):
                    c, n = find_piece(rels, (k << shift) | p)
                    start = pl.multiple_of(lax.bitwise_xor(me & (each - 1), p) * part, part)
                    for q in range(stacks):
                        pltpu.make_async_copy(
                            pieces[c].at[n, :, pl.ds(q * width, width)],
                            wd.at[to, pl.ds(start + q * rows, rows), :],
                            in_sem.at[1, to],
                        ).start()

    middle = pltpu.make_async_copy(mid_ref, acc, mid_sem)

    @pl.when(i == 0)
    def _():
        fetch(i, slot)
        middle.start()
        xt[...] = x_ref[...].T
        gx_ref[...] = jnp.zeros_like(gx_ref)

    @pl.when(i + 1 < blocks)
    def _():
        fetch(i + 1, 1 - slot)

    pltpu.make_async_copy(wu.at[slot], wu.at[slot], in_sem.at[0, slot]).wait()
    pltpu.make_async_copy(wd.at[slot], wd.at[slot], in_sem.at[1, slot]).wait()
    half = cols // 2
    low, high = slice(0, half), slice(half, cols)

    def curves(u, ga):
        e = jnp.exp2(u * u * (-0.5 * math.log2(math.e)))
        d = 1.0 + jnp.abs(u) * (0.3275911 * inv_sqrt_two)
        t = pl.reciprocal(d, approx=True)
        t = t * (2.0 - d * t)
        poly = t * (0.127414796 + t * (-0.142248368 + t * (0.7107068705 + t * (-0.7265760135 + t * 0.5307027145))))
        tail = poly * e
        phi = jnp.where(u >= 0.0, 1.0 - tail, tail)
        gu = ga * (phi + u * (e * inv_sqrt_tau))
        return (u * phi).astype(bf16), gu.astype(bf16), jnp.sum(gu, axis=0, keepdims=True)

    u0 = dot_n(x_ref[...], wu[slot, :, low]) + bias_ref[:, low]
    g0 = dot_t(g_ref[...], wd[slot, low, :])
    u1 = dot_n(x_ref[...], wu[slot, :, high]) + bias_ref[:, high]
    g1 = dot_t(g_ref[...], wd[slot, high, :])
    a, g, total = curves(u0, g0)
    act[:, low] = a
    gup[:, low] = g
    gb_ref[:, low] = total

    @pl.when(i >= 2)
    def _():
        pltpu.make_async_copy(su.at[slot], su.at[slot], out_sem.at[0, slot]).wait()
        pltpu.make_async_copy(sd.at[slot], sd.at[slot], out_sem.at[1, slot]).wait()

    @pl.when(i == 0)
    def _():
        middle.wait()

    sd[slot, low, :] = dot_tl(act[:, low], g_ref[...]).astype(bf16)
    su[slot, :, low] = dot_n(xt[...], gup[:, low]).astype(bf16)
    a, g, total = curves(u1, g1)
    act[:, high] = a
    gup[:, high] = g
    gb_ref[:, high] = total
    acc[...] += dot_n(act[...], wd[slot])
    gx_ref[...] += dot_t(gup[...], wu[slot])
    sd[slot, high, :] = dot_tl(act[:, high], g_ref[...]).astype(bf16)
    su[slot, :, high] = dot_n(xt[...], gup[:, high]).astype(bf16)
    at = pl.multiple_of(group(i) * cols, cols)
    for p in range(count):
        c, n = place(p, *where)
        start = pl.multiple_of(lax.bitwise_xor(me, p) * rows, rows)
        pltpu.make_async_copy(
            su.at[slot, pl.ds(start, rows), :],
            grads[c].at[n, :, pl.ds(at, cols)],
            out_sem.at[0, slot],
        ).start()
    for k in range(blocks):

        @pl.when(i == k)
        def _():
            for p in range(each):
                c, n = place((k << shift) | p, *where)
                start = pl.multiple_of(lax.bitwise_xor(me & (each - 1), p) * part, part)
                for q in range(stacks):
                    pltpu.make_async_copy(
                        sd.at[slot, pl.ds(start + q * rows, rows), :],
                        grads[c].at[n, :, pl.ds(hidden + q * width, width)],
                        out_sem.at[1, slot],
                    ).start()

    @pl.when(i == blocks - 1)
    def _():
        out_ref[...] = (acc[...] + shift_ref[...]).astype(bf16)
        for s in range(2):
            pltpu.make_async_copy(su.at[s], su.at[s], out_sem.at[0, s]).wait()
            pltpu.make_async_copy(sd.at[s], sd.at[s], out_sem.at[1, s]).wait()


FEED_BLOCKS = 4


def feed(x, grad, middle, bias, shift, up, pieces, line, orders, core, me):
    rels = [q for _, q in pieces]
    count = sum(len(q) for q in rels)
    tokens, width = x.shape
    hidden = bias.shape[1]
    cols = hidden // FEED_BLOCKS
    shift_by = (count // FEED_BLOCKS).bit_length() - 1

    def block(i, me_ref):
        return (0, lax.bitwise_xor(lax.shift_right_logical(me_ref[0], shift_by), i))

    def whole(i, me_ref):
        return (0, 0)

    once = pl.Buffered(1)
    anywhere = pl.BlockSpec(memory_space=pl.ANY)
    return pl.pallas_call(
        functools.partial(feed_kernel, rels, (line, orders, core)),
        grid_spec=pltpu.PrefetchScalarGridSpec(
            num_scalar_prefetch=1,
            grid=(FEED_BLOCKS,),
            in_specs=[
                pl.BlockSpec((tokens, width), whole, pipeline_mode=once),
                pl.BlockSpec((tokens, width), whole, pipeline_mode=once),
                pl.BlockSpec((1, cols), block),
                pl.BlockSpec((1, width), whole),
                anywhere,
                anywhere,
            ]
            + [anywhere] * len(pieces),
            out_specs=[
                pl.BlockSpec((tokens, width), whole, pipeline_mode=once),
                pl.BlockSpec((tokens, width), whole, pipeline_mode=once),
                pl.BlockSpec((1, cols), block),
            ]
            + [anywhere] * 2,
            scratch_shapes=[
                pltpu.VMEM((2, width, cols), bf16),
                pltpu.VMEM((2, cols, width), bf16),
                pltpu.VMEM((2, width, cols), bf16),
                pltpu.VMEM((2, cols, width), bf16),
                pltpu.VMEM((tokens, width), f32),
                pltpu.VMEM((width, tokens), bf16),
                pltpu.VMEM((tokens, cols), bf16),
                pltpu.VMEM((tokens, cols), bf16),
                pltpu.SemaphoreType.DMA((2, 2)),
                pltpu.SemaphoreType.DMA((2, 2)),
                pltpu.SemaphoreType.DMA,
            ],
        ),
        out_shape=[
            jax.ShapeDtypeStruct((tokens, width), bf16),
            jax.ShapeDtypeStruct((tokens, width), f32),
            jax.ShapeDtypeStruct((1, hidden), f32),
        ]
        + [jax.ShapeDtypeStruct((count // 2, width // count, 2 * hidden), bf16)] * 2,
        compiler_params=pltpu.CompilerParams(vmem_limit_bytes=vmem_most),
        cost_estimate=cost(20),
    )(me, x, grad, bias, shift, middle, up, *[v for v, _ in pieces])


def weight_kernel(where, left, count, me_ref, x_ref, g_ref, *refs):
    outs, (xt, staged, sem) = refs[-5:-3], refs[-3:]
    j = pl.program_id(0)
    me = me_ref[0]
    slot = lax.rem(j, 2)
    width, cols = staged.shape[1:]
    rows = width // count

    @pl.when(j == 0)
    def _():
        xt[...] = x_ref[...].T

    @pl.when(j >= 2)
    def _():
        pltpu.make_async_copy(staged.at[slot], staged.at[slot], sem.at[slot]).wait()

    staged[slot] = dot_n(xt[...], g_ref[...].reshape(g_ref.shape[-2:])).astype(bf16)
    at = pl.multiple_of(left + j * cols, cols)
    for out, rel in zip(outs, where):
        for n, p in enumerate(rel):
            start = pl.multiple_of(lax.bitwise_xor(me, p) * rows, rows)
            pltpu.make_async_copy(
                staged.at[slot, pl.ds(start, rows), :], out.at[n, :, pl.ds(at, cols)], sem.at[slot]
            ).start()

    @pl.when(j == pl.num_programs(0) - 1)
    def _():
        for s in range(2):
            pltpu.make_async_copy(staged.at[s], staged.at[s], sem.at[s]).wait()


def weight_grad(x, grad, where, left, total, me, into=()):
    tokens, width = x.shape
    count = sum(len(q) for q in where)
    cols = 512
    deep = grad.ndim == 3
    found = grad.shape[-1] * (grad.shape[0] if deep else 1)
    per = grad.shape[-1] // cols
    if deep:
        spec = pl.BlockSpec((1, tokens, cols), lambda j, m: (j // per, 0, j % per))
    else:
        spec = pl.BlockSpec((tokens, cols), lambda j, m: (0, j))
    anywhere = pl.BlockSpec(memory_space=pl.ANY)
    return pl.pallas_call(
        functools.partial(weight_kernel, where, left, count),
        grid_spec=pltpu.PrefetchScalarGridSpec(
            num_scalar_prefetch=1,
            grid=(found // cols,),
            in_specs=[pl.BlockSpec((tokens, width), lambda j, m: (0, 0)), spec]
            + [anywhere] * len(into),
            out_specs=[anywhere] * 2,
            scratch_shapes=[
                pltpu.VMEM((width, tokens), bf16),
                pltpu.VMEM((2, width, cols), bf16),
                pltpu.SemaphoreType.DMA((2,)),
            ],
        ),
        out_shape=[jax.ShapeDtypeStruct((count // 2, width // count, total), bf16)] * 2,
        input_output_aliases={3 + i: i for i in range(len(into))},
        compiler_params=pltpu.CompilerParams(vmem_limit_bytes=vmem_most),
        cost_estimate=cost(0.5 * found / 512),
    )(me, x, grad, *into)


def sort_kernel(x_ref, g_ref, x_out, g_out, sum_ref, wide):
    for source, target in ((x_ref, x_out), (g_ref, g_out)):
        wide[...] = source[...].astype(f32)
        for f in range(FRAMES):
            at = f * FRAME_ROWS + 2
            target[f * PATCH : (f + 1) * PATCH, :] = wide[at : at + PATCH, :].astype(bf16)
        few = [wide[f * FRAME_ROWS : f * FRAME_ROWS + 2, :] for f in range(FRAMES)]
        few = jnp.concatenate(few + [jnp.zeros((EXTRA - FEW, wide.shape[1]), f32)], axis=0)
        target[BODY:ROWS, :] = few.astype(bf16)
    sum_ref[...] = jnp.sum(wide[...], axis=0, keepdims=True)


def sort_rows(x, grad):
    tokens, width = x.shape
    return pl.pallas_call(
        sort_kernel,
        out_shape=[jax.ShapeDtypeStruct((ROWS, width), bf16)] * 2
        + [jax.ShapeDtypeStruct((1, width), f32)],
        scratch_shapes=[pltpu.VMEM((tokens, width), f32)],
        compiler_params=pltpu.CompilerParams(vmem_limit_bytes=vmem_most),
        cost_estimate=cost(1),
    )(x, grad)


def unsort_kernel(x_ref, out_ref, *scratch):
    wide = scratch[0] if scratch else out_ref
    for f in range(FRAMES):
        at = f * FRAME_ROWS
        wide[at + 2 : at + FRAME_ROWS, :] = x_ref[f * PATCH : (f + 1) * PATCH, :].astype(f32)
    few = x_ref[BODY:ROWS, :].astype(f32)
    for f in range(FRAMES):
        wide[f * FRAME_ROWS : f * FRAME_ROWS + 2, :] = few[2 * f : 2 * f + 2]
    if scratch:
        out_ref[...] = wide[...].astype(out_ref.dtype)


def unsort_rows(x):
    tokens, width = FRAMES * FRAME_ROWS, x.shape[1]
    return pl.pallas_call(
        unsort_kernel,
        out_shape=jax.ShapeDtypeStruct((tokens, width), x.dtype),
        scratch_shapes=[] if x.dtype == f32 else [pltpu.VMEM((tokens, width), f32)],
        compiler_params=pltpu.CompilerParams(vmem_limit_bytes=vmem_most),
        cost_estimate=cost(1),
    )(x)


def last_kernel(g_ref, w_ref, x_ref, mid_ref, gain_ref, out_ref, gain_out, bias_out, sum_ref, acc):
    i = pl.program_id(0)
    g = g_ref[0]
    more = dot_t(g, w_ref[...])

    @pl.when(i == 0)
    def _():
        acc[...] = more

    @pl.when(i > 0)
    def _():
        acc[...] += more

    sum_ref[0] = jnp.sum(g.astype(f32), axis=0, keepdims=True)

    @pl.when(i == pl.num_programs(0) - 1)
    def _():
        gain = gain_ref[...]
        gain_sum, bias_sum = 0.0, 0.0
        spans = [(f * PATCH, PATCH) for f in range(FRAMES)] + [(BODY, EXTRA)]
        for at, size in spans:
            rows = slice(at, at + size)
            x = x_ref[rows, :].astype(f32)
            center = x - jnp.mean(x, axis=-1, keepdims=True)
            inverse = lax.rsqrt(jnp.mean(center * center, axis=-1, keepdims=True) + eps_norm)
            unit = center * inverse
            grad = acc[rows, :]
            gain_sum += jnp.sum(grad * unit, axis=0, keepdims=True)
            bias_sum += jnp.sum(grad, axis=0, keepdims=True)
            scaled = grad * gain
            mean_grad = jnp.mean(scaled, axis=-1, keepdims=True)
            mean_cross = jnp.mean(scaled * unit, axis=-1, keepdims=True)
            found = mid_ref[rows, :] + inverse * (scaled - mean_grad - unit * mean_cross)
            if size == PATCH:
                start = at // PATCH * FRAME_ROWS + 2
                out_ref[start : start + PATCH, :] = found
            else:
                for f in range(FRAMES):
                    out_ref[f * FRAME_ROWS : f * FRAME_ROWS + 2, :] = found[2 * f : 2 * f + 2]
        gain_out[...] = gain_sum
        bias_out[...] = bias_sum


def last_step(grad_mixed, w, x, middle, gain):
    parts, rows, width = grad_mixed.shape

    def whole(i):
        return (0, 0)

    once = pl.Buffered(1)
    return pl.pallas_call(
        last_kernel,
        grid=(parts,),
        in_specs=[
            pl.BlockSpec((1, rows, width), lambda i: (i, 0, 0)),
            pl.BlockSpec((width, width), lambda i: (0, i)),
            pl.BlockSpec((rows, width), whole, pipeline_mode=once),
            pl.BlockSpec((rows, width), whole, pipeline_mode=once),
            pl.BlockSpec((1, width), whole),
        ],
        out_specs=[
            pl.BlockSpec((FRAMES * FRAME_ROWS, width), whole, pipeline_mode=once),
            pl.BlockSpec((1, width), whole),
            pl.BlockSpec((1, width), whole),
            pl.BlockSpec((1, 1, width), lambda i: (i, 0, 0)),
        ],
        out_shape=[
            jax.ShapeDtypeStruct((FRAMES * FRAME_ROWS, width), f32),
            jax.ShapeDtypeStruct((1, width), f32),
            jax.ShapeDtypeStruct((1, width), f32),
            jax.ShapeDtypeStruct((parts, 1, width), f32),
        ],
        scratch_shapes=[pltpu.VMEM((rows, width), f32)],
        compiler_params=pltpu.CompilerParams(vmem_limit_bytes=vmem_most),
        cost_estimate=cost(5),
    )(grad_mixed, w, x, middle, gain)


def normalize(values, gain, bias_add):
    center = values - jnp.mean(values, axis=-1, keepdims=True)
    scale_inv = lax.rsqrt(jnp.mean(center * center, axis=-1, keepdims=True) + eps_norm)
    unit_rows = center * scale_inv
    return (unit_rows * gain + bias_add, unit_rows, scale_inv)


def norm_back(grad_out, unit_rows, scale_inv, gain):
    scaled = grad_out * gain
    mean_grad = jnp.mean(scaled, axis=-1, keepdims=True)
    mean_cross = jnp.mean(scaled * unit_rows, axis=-1, keepdims=True)
    return scale_inv * (scaled - mean_grad - unit_rows * mean_cross)


def gather_joined(groups, orders, core, sizes):
    found = []
    for pieces, order in zip(groups, orders):
        for bit in order[:-1]:
            pieces = pieces + moved(pieces, bit, sizes)
        arrays, rels = zip(*pieces)
        pieces = [(jnp.concatenate(arrays, axis=0), sum(rels, []))]
        found += pieces + moved(pieces, order[-1], sizes)
    return found + moved(found, core, sizes)


def gather_rest(groups, orders, core, sizes):
    found = []
    for pieces, order in zip(groups, orders):
        for bit in order:
            pieces = pieces + moved(pieces, bit, sizes)
        found += pieces
    return found + moved(found, core, sizes)


def body(
    sizes,
    tokens,
    frame_ids,
    pad_mask,
    episode_offsets,
    ln1_gain,
    ln1_bias,
    w_qkv,
    b_qkv,
    w_out,
    b_out,
    ln2_gain,
    ln2_bias,
    w_up,
    b_up,
    w_down,
    b_down,
    cotangent,
):
    width = tokens.shape[1]
    count = sizes[0] * sizes[1]
    me = (lax.axis_index("dp") * sizes[1] + lax.axis_index("fsdp")).astype(jnp.int32)[None]
    core, line, orders = bit_orders(sizes)
    where = relatives(line, orders, core)
    out_matrix = lax.all_gather(w_out, ("dp", "fsdp"), axis=0, tiled=True)
    up_matrix = lax.all_gather(w_up, ("dp", "fsdp"), axis=0, tiled=True)
    smalls = [ln1_gain, ln1_bias, b_qkv, b_out, ln2_gain, ln2_bias, b_up, b_down]
    rows, third = w_qkv.shape
    first_unit = jnp.concatenate([w_qkv, pack_small(smalls, rows)], axis=1)
    firsts = gather_line(first_unit, line, sizes)
    tokens_in, cot, grad_b_down_local = sort_rows(tokens, cotangent)
    first = gather_joined(firsts, orders, core, sizes)
    seen = seen_frames(episode_offsets[0])
    hide = hidden_few(seen)
    cosine, sine = turn_tables(frame_ids)
    partner = partner_matrix()
    values_in = tokens_in.astype(f32)
    qkv_matrix, whole_small = assemble(
        first, me, [(0, rows, 0, third), (0, rows, third, first_unit.shape[1] - third)]
    )
    gain_one, bias_one, qkv_rows, out_bias, gain_two, bias_two, up_bias, down_bias = unpack_small(
        whole_small, rows, smalls
    )
    stacked = [w_down[at : at + rows] for at in range(0, w_down.shape[0], rows)]
    second_unit = after(jnp.concatenate(stacked, axis=1), qkv_matrix)
    seconds = gather_line(second_unit, line, sizes)
    normed_one, unit_one, inv_one = normalize(values_in, gain_one, bias_one)
    normed_one = normed_one.astype(bf16)
    qkv = project(normed_one, qkv_matrix, qkv_rows.reshape(1, 3 * width), cosine, sine, partner)
    pairs = width // (2 * HEAD)
    seconds = [after_pieces(pieces, qkv) for pieces in seconds]
    seconds = [
        [pieces, moved(pieces, order[0], sizes) + moved(pieces, order[1], sizes)]
        for pieces, order in zip(seconds, orders)
    ]
    attended, lse_a, few_a = attend(seen, qkv, hide, 0, pairs // 2)
    seconds = [[near, after_pieces(far, attended)] for near, far in seconds]
    found = []
    for (near, far), order in zip(seconds, orders):
        pieces = near + far + moved(far[:1], order[1], sizes)
        for bit in order[2:]:
            pieces = pieces + moved(pieces, bit, sizes)
        found.append(pieces)
    attended, lse_b, few_b = attend(seen, qkv, hide, pairs // 2, pairs, attended)
    second = []
    for pieces in found:
        arrays, rels = zip(*pieces)
        pieces = [(after(jnp.concatenate(arrays, axis=0), attended), sum(rels, []))]
        second += pieces + moved(pieces, core, sizes)
    hidden = w_up.shape[1]
    middle = values_in + jnp.dot(attended, out_matrix, preferred_element_type=f32) + out_bias
    normed_two, unit_two, inv_two = normalize(middle, gain_two, bias_two)
    normed_two = normed_two.astype(bf16)
    result, grad_normed_two, grad_b_up_local, feed_own, feed_other = feed(
        normed_two,
        cot,
        middle,
        up_bias[None],
        down_bias[None],
        up_matrix,
        second,
        line,
        orders,
        core,
        me,
    )
    feed_taken = swap(feed_other, 1 << core, sizes)
    grad_gain_two = jnp.sum(grad_normed_two * unit_two, axis=0)
    grad_bias_two = jnp.sum(grad_normed_two, axis=0)
    grad_middle = cot.astype(f32) + norm_back(grad_normed_two, unit_two, inv_two, gain_two)
    grad_branch = grad_middle.astype(bf16)
    grad_b_out_local = jnp.sum(grad_branch.astype(f32), axis=0)
    grads = weight_grad(attended, grad_branch, where, third, third + width, me)
    grad_attended = dot_t(grad_branch, out_matrix).astype(bf16)
    feed_sums = reduce_start(feed_own, feed_taken, orders, sizes)
    grad_attended = after(grad_attended, grads[0], *[v for group in feed_sums for v in group[:1] + group[2:]])
    feed_sums = [group[:2] for group in feed_sums]
    back = (hide, cosine, sine, partner)
    grad_mixed = attend_back(
        seen, qkv, attended, grad_attended, lse_a, few_a, *back, 0, pairs // 2
    )
    grad_mixed = attend_back(
        seen, qkv, attended, grad_attended, lse_b, few_b, *back, pairs // 2, pairs, grad_mixed
    )
    steps = len(orders[0])
    for step in range(1, steps):
        feed_sums = [(kept, after(came, grad_mixed)) for kept, came in together(feed_sums)]
        feed_sums = reduce_next(feed_sums, orders, step, sizes)
        grad_mixed = after(grad_mixed, *[v for group in feed_sums for v in group[:1] + group[2:]])
        feed_sums = [group[:2] for group in feed_sums]
    own, other = weight_grad(normed_one, grad_mixed, where, 0, third + width, me, grads)
    taken = swap(other, 1 << core, sizes)
    feed_parts = line_parts(together(feed_sums))
    feed_parts = feed_parts[:1] + [v.astype(bf16) for v in feed_parts[1:]]
    own = after(own, *feed_parts[1:])
    sums = reduce_start(own, taken, orders, sizes)
    going = [v for group in sums for v in group[:1] + group[2:]]
    sums = [group[:2] for group in sums]
    grad_mixed = after(grad_mixed, *going)
    grad_tokens, grad_gain_one, grad_bias_one, grad_b_qkv_local = last_step(
        grad_mixed, qkv_matrix, tokens_in, grad_middle, gain_one[None]
    )
    vectors = [
        grad_gain_one[0],
        grad_bias_one[0],
        grad_b_qkv_local[:, 0],
        grad_b_out_local,
        grad_gain_two,
        grad_bias_two,
        grad_b_up_local[0],
        grad_b_down_local[0],
    ]
    small_own, small_other = small_units(vectors, rows, where, me)
    small = jnp.concatenate([small_own, small_other], axis=2).astype(bf16)
    half = small.shape[0] // 2
    joined = []
    for (kept, came), at, order in zip(sums, (0, half), orders):
        here = small[at : at + half // 2]
        there = swap(small[at + half // 2 : at + half], 1 << order[-1], sizes)
        joined.append(
            (jnp.concatenate([kept, here], axis=2), jnp.concatenate([came, there], axis=2))
        )
    sums = joined
    for step in range(1, steps):
        sums = [group[:2] for group in reduce_next(sums, orders, step, sizes)]
    parts = line_parts(sums)
    parts = parts[:1] + [v.astype(bf16) for v in parts[1:]]
    feed_parts[0] = after(feed_parts[0], *parts[1:])
    result = after(result, *parts[1:])
    feed_sum = reduce_line(feed_parts, line, sizes)
    sum_one = reduce_line(parts, line, sizes)
    output = unsort_rows(result)
    small = sum_one[:, third + width :]
    small = small[:, :128] + swap(small[:, 128:], 1 << core, sizes)
    small = small_parts(small, vectors, count)
    sum_down = feed_sum[:, hidden:].reshape(rows, -1, width).swapaxes(0, 1).reshape(-1, width)
    return (
        output,
        grad_tokens,
        small[0],
        small[1],
        sum_one[:, :third],
        small[2],
        sum_one[:, third : third + width],
        small[3],
        small[4],
        small[5],
        feed_sum[:, :hidden],
        small[6],
        sum_down,
        small[7],
    )


def solution(mesh):
    placed = (
        P(("dp", "fsdp"), None),
        P(("dp", "fsdp")),
        P(("dp", "fsdp")),
        P(("dp", "fsdp"), None),
        P(("dp", "fsdp")),
        P(("dp", "fsdp")),
        P(("dp", "fsdp"), None),
        P(None, ("dp", "fsdp")),
        P(("dp", "fsdp"), None),
        P(("dp", "fsdp")),
        P(("dp", "fsdp")),
        P(("dp", "fsdp")),
        P(("dp", "fsdp"), None),
        P(("dp", "fsdp")),
        P(("dp", "fsdp"), None),
        P(("dp", "fsdp")),
        P(("dp", "fsdp"), None),
    )
    sizes = (mesh.shape["dp"], mesh.shape["fsdp"])
    return jax.shard_map(
        functools.partial(body, sizes),
        mesh=mesh,
        in_specs=placed,
        out_specs=(
            P(("dp", "fsdp"), None),
            P(("dp", "fsdp"), None),
            P(("dp", "fsdp")),
            P(("dp", "fsdp")),
            P(("dp", "fsdp"), None),
            P(None, ("dp", "fsdp")),
            P(("dp", "fsdp"), None),
            P(("dp", "fsdp")),
            P(("dp", "fsdp")),
            P(("dp", "fsdp")),
            P(("dp", "fsdp"), None),
            P(("dp", "fsdp")),
            P(("dp", "fsdp"), None),
            P(("dp", "fsdp")),
        ),
        check_vma=False,
    )
```

```python
import functools
import math

import jax
import jax.numpy as jnp
import numpy as np
from jax import lax
from jax.experimental import pallas as pl
from jax.experimental.pallas import tpu as pltpu
from jax.sharding import PartitionSpec as P

HEAD = 64
GRID = 16
FRAME_ROWS = 258
FRAMES = 4
PATCH = GRID * GRID
EXTRA = 16
FEW = 8
BODY = FRAMES * PATCH
ROWS = BODY + EXTRA
eps_norm = 1e-06
part_sizes = (24, 20, 20)
masked_value = -1e30
inv_sqrt_two = 1.0 / math.sqrt(2.0)
inv_sqrt_tau = 1.0 / math.sqrt(2.0 * math.pi)
f32 = jnp.float32
bf16 = jnp.bfloat16
vmem_most = 60 * 1024 * 1024


def cost(micros):
    return pl.CostEstimate(flops=int(micros * 1e9), bytes_accessed=0, transcendentals=0)


def log2(n):
    return n.bit_length() - 1


def swap(value, mask, sizes):
    count = sizes[0] * sizes[1]
    return lax.ppermute(value, ("dp", "fsdp"), [(i, i ^ mask) for i in range(count)])


def bit_orders(sizes):
    inner, outer = log2(sizes[1]), log2(sizes[0])
    line = list(range(1, inner))
    cross = [0]
    other = list(range(inner + 1, inner + outer))
    return inner, line, (cross + other, other + cross)


def spread(bits):
    rel = [0]
    for bit in bits:
        rel = rel + [p | (1 << bit) for p in rel]
    return rel


def gather_line(shard, line, sizes):
    rel = spread(line)
    held = [shard[None]] + [swap(shard[None], p, sizes) for p in rel[1:]]
    half = len(rel) // 2
    return [
        [(jnp.concatenate(held[at : at + half], axis=0), rel[at : at + half])]
        for at in (0, half)
    ]


def gather_doubling(shard, line, sizes):
    held, rel = shard[None], [0]
    for bit in line[:-1]:
        held = jnp.concatenate([held, swap(held, 1 << bit, sizes)], axis=0)
        rel = rel + [p | (1 << bit) for p in rel]
    return [[(held, rel)], moved([(held, rel)], line[-1], sizes)]


def moved(pieces, bit, sizes):
    return [(swap(v, 1 << bit, sizes), [p | (1 << bit) for p in q]) for v, q in pieces]


def relatives(line, orders, core):
    low, top = line[:-1], 1 << line[-1]
    rel = spread(low + orders[0]) + [p | top for p in spread(low + orders[1])]
    return rel, [p | (1 << core) for p in rel]


def reduce_start(own, taken, orders, sizes):
    half = own.shape[0] // 2
    return [
        reduce_step(own[at : at + half], taken[at : at + half], 1 << order[-1], sizes)
        for at, order in zip((0, half), orders)
    ]


def reduce_step(kept, taken, mask, sizes):
    kind = kept.dtype
    half = kept.shape[0] // 2
    sent = (kept[half:].astype(f32) + taken[half:].astype(f32)).astype(kind)
    held = (kept[:half].astype(f32) + taken[:half].astype(f32)).astype(kind)
    return held, swap(sent, mask, sizes), sent


def reduce_next(groups, orders, step, sizes):
    return [
        reduce_step(*group, 1 << order[-1 - step], sizes) for group, order in zip(groups, orders)
    ]


def together(groups, *others):
    came = [group[1] for group in groups]
    return [(after(kept, *came, *others), taken) for kept, taken in groups]


def after_pieces(pieces, *others):
    return [(after(v, *others), q) for v, q in pieces]


def line_parts(groups):
    return [
        kept[n].astype(f32) + taken[n].astype(f32)
        for kept, taken in groups
        for n in range(kept.shape[0])
    ]


def reduce_line(parts, line, sizes):
    total = parts[0]
    for part, p in zip(parts[1:], spread(line)[1:]):
        total = total + swap(part, p, sizes).astype(f32)
    return total


def after_kernel(*refs):
    del refs


def after(value, *others):
    anywhere = pl.BlockSpec(memory_space=pl.ANY)
    return pl.pallas_call(
        after_kernel,
        out_shape=jax.ShapeDtypeStruct(value.shape, value.dtype),
        in_specs=[anywhere] * (1 + len(others)),
        out_specs=anywhere,
        input_output_aliases={0: 0},
        cost_estimate=cost(0),
    )(value, *others)


def assemble_kernel(rels, parts, me_ref, *refs):
    pieces, refs = refs[: len(rels)], refs[len(rels) :]
    outs, sems = refs[: len(parts)], refs[-1]
    me = me_ref[0]
    for k, (top, height, left, cols) in enumerate(parts):
        for piece, rel in zip(pieces, rels):
            for at, p in enumerate(rel):
                start = pl.multiple_of(lax.bitwise_xor(me, p) * height, height)
                pltpu.make_async_copy(
                    piece.at[at, pl.ds(top, height), pl.ds(left, cols)],
                    outs[k].at[pl.ds(start, height)],
                    sems.at[k],
                ).start()
    for k, out in enumerate(outs):
        pltpu.make_async_copy(out, out, sems.at[k]).wait()


def assemble(pieces, me, parts):
    rels = [q for _, q in pieces]
    count = sum(len(q) for q in rels)
    total = sum(h * c for _, h, _, c in parts)
    return pl.pallas_call(
        functools.partial(assemble_kernel, rels, parts),
        out_shape=[jax.ShapeDtypeStruct((count * h, c), bf16) for _, h, _, c in parts],
        in_specs=[pl.BlockSpec(memory_space=pltpu.SMEM)]
        + [pl.BlockSpec(memory_space=pl.ANY)] * len(pieces),
        scratch_shapes=[pltpu.SemaphoreType.DMA((len(parts),))],
        compiler_params=pltpu.CompilerParams(vmem_limit_bytes=vmem_most),
        cost_estimate=cost(1.5),
    )(me, *[v for v, _ in pieces])


def pack_small(parts, rows):
    def fill(blocks):
        size = max(v.shape[1] for v in blocks)
        same = [v for v in blocks if v.shape[1] < size]
        rest = [v for v in blocks if v.shape[1] == size]
        if same:
            joined = jnp.concatenate(same, axis=0)
            rest = [jnp.pad(joined, ((0, 0), (0, size - joined.shape[1])))] + rest
        block = jnp.concatenate(rest, axis=0)
        return jnp.pad(block, ((0, rows - block.shape[0]), (0, 128 - size)))

    flat = sorted((v for v in parts if v.ndim == 1), key=lambda v: v.shape[0])
    flat = fill([v[None] for v in flat])
    return jnp.concatenate([flat] + [fill([v]) for v in parts if v.ndim == 2], axis=1)


def unpack_small(whole, rows, parts):
    whole = whole.reshape(-1, rows, whole.shape[1]).astype(f32)
    found, left = [], 128
    flat = sorted((i for i, v in enumerate(parts) if v.ndim == 1), key=lambda i: parts[i].shape[0])
    for i, v in enumerate(parts):
        size = v.shape[-1]
        if v.ndim == 2:
            block = whole[:, : v.shape[0], left : left + size].swapaxes(0, 1)
            found.append(block.reshape(v.shape[0], -1))
            left += 128
        else:
            found.append(whole[:, flat.index(i), :size].reshape(-1))
    return found


def small_units(parts, rows, where, me):
    count = sum(len(q) for q in where)
    blocks = [
        v.reshape(count, -1)
        if v.ndim == 1
        else v.reshape(v.shape[0], count, -1).swapaxes(0, 1).reshape(count, -1)
        for v in parts
    ]
    flat = jnp.concatenate(blocks, axis=1)
    flat = jnp.pad(flat, ((0, 0), (0, rows * 128 - flat.shape[1]))).reshape(count, rows, 128)
    index = lax.bitwise_xor(jnp.asarray(where[0] + where[1], jnp.int32), me[0])
    mixed = jnp.take(flat, index, axis=0)
    return mixed[: count // 2], mixed[count // 2 :]


def small_parts(unit, parts, count):
    flat = unit.reshape(-1)
    found, at = [], 0
    for v in parts:
        size = v.size // count
        block = flat[at : at + size]
        found.append(block if v.ndim == 1 else block.reshape(v.shape[0], -1))
        at = at + size
    return found


def dot_t(a, b):
    return lax.dot_general(a, b, (((1,), (1,)), ((), ())), preferred_element_type=f32)


def dot_n(a, b):
    return lax.dot_general(a, b, (((1,), (0,)), ((), ())), preferred_element_type=f32)


def dot_tl(a, b):
    return lax.dot_general(a, b, (((0,), (0,)), ((), ())), preferred_element_type=f32)


def head_lanes(a, rows):
    lane = lax.broadcasted_iota(jnp.int32, (rows, 2 * HEAD), 1)
    return (lane >= HEAD) if a else (lane < HEAD)


def keep_head(x, a):
    return jnp.where(head_lanes(a, x.shape[0]), x, jnp.zeros_like(x))


def stack_heads(x):
    head = lax.broadcasted_iota(jnp.int32, x.shape, 1) // HEAD
    heads = x.shape[1] // HEAD
    return jnp.concatenate([jnp.where(head == a, x, jnp.zeros_like(x)) for a in range(heads)], axis=0)


def join_heads(x):
    heads = x.shape[0] // FEW
    head = lax.broadcasted_iota(jnp.int32, (FEW, x.shape[1]), 1) // HEAD
    found = x[:FEW]
    for a in range(1, heads):
        found = jnp.where(head == a, x[a * FEW : (a + 1) * FEW], found)
    return found


def few_rows(x):
    return jnp.concatenate([x, jnp.zeros_like(x)], axis=0)


def hide_few(s, first, last):
    row = lax.broadcasted_iota(jnp.int32, (EXTRA, s.shape[1]), 0)
    frame = lax.shift_right_logical(row, 1)
    seen = (frame >= first) & (frame <= last)
    count = s.shape[0] - EXTRA
    return jnp.concatenate([s[:count], jnp.where(seen, s[count:], masked_value)], axis=0)


def seen_rows(ref, lanes, lo, n):
    return jnp.concatenate([ref[pl.ds(lo, n * PATCH), lanes], ref[BODY:ROWS, lanes]], axis=0)


def seen_lanes(ref, a, lo, n):
    rows = slice(a * HEAD, (a + 1) * HEAD)
    return jnp.concatenate([ref[rows, pl.ds(lo, n * PATCH)], ref[rows, BODY:ROWS]], axis=1)


def pair_lanes(a):
    at = a // 2 * 2 * HEAD
    return slice(at, at + 2 * HEAD)


def attend_kernel(seen_ref, q_ref, k_ref, v_ref, hide_ref, out_ref, lse_ref, few_ref, vt):
    f = pl.program_id(1)
    heads = q_ref.shape[1] // HEAD

    @pl.when(f == 0)
    def _():
        vt[...] = v_ref[...].T
        qs = stack_heads(q_ref[BODY:ROWS, :].astype(f32)[:FEW]).astype(bf16)
        s = dot_t(k_ref[...], qs) + hide_ref[...]
        top = jnp.max(s, axis=0, keepdims=True)
        p = jnp.exp(s - top)
        total = jnp.sum(p, axis=0, keepdims=True)
        o = dot_tl((p / total).astype(bf16), v_ref[...])
        out_ref[BODY:ROWS, :] = few_rows(join_heads(o)).astype(bf16)
        few_ref[0] = top + jnp.log(total)

    row = pl.multiple_of(f * PATCH, PATCH)
    seen = seen_ref[f]

    @pl.when(seen == 0)
    def _():
        out_ref[pl.ds(row, PATCH), :] = v_ref[pl.ds(row, PATCH), :]
        lse_ref[0, :, pl.ds(row, PATCH)] = jnp.zeros((heads, PATCH), f32)

    for n in range(1, FRAMES + 1):

        @pl.when(seen == n)
        def _(n=n):
            first = f - (n - 1)
            lo = pl.multiple_of(first * PATCH, PATCH)

            def score(a):
                lanes = pair_lanes(a)
                q = keep_head(q_ref[pl.ds(row, PATCH), lanes], a % 2)
                return hide_few(dot_t(seen_rows(k_ref, lanes, lo, n), q), first, f)

            ahead = 4
            scores = [score(a) for a in range(ahead)]
            outs, sums = [], []
            for a in range(heads):
                s = scores[a]
                top = jnp.max(s, axis=0, keepdims=True)
                p = jnp.exp(s - top)
                total = jnp.sum(p, axis=0, keepdims=True)
                if a + ahead < heads:
                    scores.append(score(a + ahead))
                o = dot_n(seen_lanes(vt, a, lo, n), p.astype(bf16))
                outs.append(o / total)
                sums.append(top + jnp.log(total))
            out_ref[pl.ds(row, PATCH), :] = jnp.concatenate(outs, axis=0).T.astype(bf16)
            lse_ref[0, :, pl.ds(row, PATCH)] = jnp.concatenate(sums, axis=0)


PAIRS = 4


def attend(seen, qkv, hide, pair_lo, pair_hi, kept=None):
    width = qkv.shape[1] // 3
    lanes = 2 * HEAD * PAIRS
    groups = width // lanes
    at = pair_lo // PAIRS
    some = (pair_hi - pair_lo) // PAIRS
    kernel = attend_kernel
    more, alias = [], {}
    if kept is not None:
        more, alias = [kept], {5: 0}

        def kernel(seen_ref, q_ref, k_ref, v_ref, hide_ref, kept_ref, *refs):
            attend_kernel(seen_ref, q_ref, k_ref, v_ref, hide_ref, *refs)

    return pl.pallas_call(
        kernel,
        grid_spec=pltpu.PrefetchScalarGridSpec(
            num_scalar_prefetch=1,
            grid=(some, FRAMES),
            in_specs=[
                pl.BlockSpec((ROWS, lanes), lambda h, f, s: (0, at + h)),
                pl.BlockSpec((ROWS, lanes), lambda h, f, s: (0, at + groups + h)),
                pl.BlockSpec((ROWS, lanes), lambda h, f, s: (0, at + 2 * groups + h)),
                pl.BlockSpec((ROWS, 2 * PAIRS * FEW), lambda h, f, s: (0, 0)),
            ]
            + [pl.BlockSpec(memory_space=pl.ANY)] * len(more),
            out_specs=[
                pl.BlockSpec((ROWS, lanes), lambda h, f, s: (0, at + h)),
                pl.BlockSpec((1, 2 * PAIRS, BODY), lambda h, f, s: (h, 0, 0)),
                pl.BlockSpec((1, 1, 2 * PAIRS * FEW), lambda h, f, s: (h, 0, 0)),
            ],
            scratch_shapes=[pltpu.VMEM((lanes, ROWS), bf16)],
        ),
        out_shape=(
            jax.ShapeDtypeStruct((ROWS, width), bf16),
            jax.ShapeDtypeStruct((some, 2 * PAIRS, BODY), f32),
            jax.ShapeDtypeStruct((some, 1, 2 * PAIRS * FEW), f32),
        ),
        input_output_aliases=alias,
        compiler_params=pltpu.CompilerParams(vmem_limit_bytes=vmem_most),
        cost_estimate=cost(6.4 * some),
    )(seen, qkv, qkv, qkv, hide, *more)


def unturn(x, cosine, sine, partner):
    return x * cosine - dot_n(x.astype(bf16), partner) * sine


def attend_back_kernel(
    scale, seen_ref, q_ref, k_ref, v_ref, o_ref, g_ref, lse_ref, few_ref, hide_ref, cos_ref, sin_ref,
    part_ref, out_ref, kt, dq, dk, dv,
):
    f = pl.program_id(1)
    heads = q_ref.shape[1] // HEAD
    pairs = [slice(p * 2 * HEAD, (p + 1) * 2 * HEAD) for p in range(heads // 2)]
    ones = jnp.where(
        (lax.broadcasted_iota(jnp.int32, (8, 2 * HEAD), 1) >= HEAD).astype(jnp.int32)
        == lax.broadcasted_iota(jnp.int32, (8, 2 * HEAD), 0),
        1.0,
        0.0,
    ).astype(bf16)

    @pl.when(f == 0)
    def _():
        kt[...] = k_ref[...].T
        qs = stack_heads(q_ref[BODY:ROWS, :].astype(f32)[:FEW]).astype(bf16)
        gs = stack_heads(g_ref[BODY:ROWS, :].astype(f32)[:FEW]).astype(bf16)
        p = jnp.exp(dot_t(k_ref[...], qs) + hide_ref[...] - few_ref[0])
        gp = dot_t(v_ref[...], gs)
        delta = jnp.sum(gp * p, axis=0, keepdims=True)
        ds = (p * (gp - delta)).astype(bf16)
        dv[...] = dot_n(p.astype(bf16), gs)
        dk[...] = dot_n(ds, qs)
        dq[BODY:ROWS, :] = few_rows(join_heads(dot_tl(ds, k_ref[...])))

    row = pl.multiple_of(f * PATCH, PATCH)
    seen = seen_ref[f]

    @pl.when(seen == 0)
    def _():
        dv[pl.ds(row, PATCH), :] += g_ref[pl.ds(row, PATCH), :].astype(f32)
        dq[pl.ds(row, PATCH), :] = jnp.zeros((PATCH, heads * HEAD), f32)

    for n in range(1, FRAMES + 1):

        @pl.when(seen == n)
        def _(n=n):
            first = f - (n - 1)
            lo = pl.multiple_of(first * PATCH, PATCH)
            count = n * PATCH

            def start(a):
                lanes = pair_lanes(a)
                q = keep_head(q_ref[pl.ds(row, PATCH), lanes], a % 2)
                g = keep_head(g_ref[pl.ds(row, PATCH), lanes], a % 2)
                s = hide_few(dot_t(seen_rows(k_ref, lanes, lo, n), q), first, f)
                return q, g, s, dot_t(seen_rows(v_ref, lanes, lo, n), g)

            deltas = []
            for lanes in pairs:
                g = g_ref[pl.ds(row, PATCH), lanes].astype(f32)
                product = g * o_ref[pl.ds(row, PATCH), lanes].astype(f32)
                upper = product.astype(bf16)
                lower = (product - upper.astype(f32)).astype(bf16)
                deltas.append(dot_t(ones, upper) + dot_t(ones, lower))
            ahead = 4
            started = [start(a) for a in range(ahead)]
            back, add_k, add_v = [], None, None
            for a in range(heads):
                q, g, s, gp = started[a]
                p = jnp.exp(s - lse_ref[0, a : a + 1, pl.ds(row, PATCH)])
                ds = (p * (gp - deltas[a // 2][a % 2 : a % 2 + 1])).astype(bf16)
                p = p.astype(bf16)
                if a + ahead < heads:
                    started.append(start(a + ahead))
                more_v, more_k = dot_n(p, g), dot_n(ds, q)
                back.append(dot_n(seen_lanes(kt, a, lo, n), ds))
                if a % 2 == 0:
                    add_v, add_k = more_v, more_k
                else:
                    lanes = pairs[a // 2]
                    add_v, add_k = add_v + more_v, add_k + more_k
                    dk[pl.ds(lo, count), lanes] += add_k[:count]
                    dk[BODY:ROWS, lanes] += add_k[count:]
                    dv[pl.ds(lo, count), lanes] += add_v[:count]
                    dv[BODY:ROWS, lanes] += add_v[count:]
            dq[pl.ds(row, PATCH), :] = jnp.concatenate(back, axis=0).T

    @pl.when(f == FRAMES - 1)
    def _():
        partner = part_ref[...]
        for lanes in pairs:
            out_ref[0, :, lanes] = unturn(
                dq[:, lanes] * scale, cos_ref[...], sin_ref[...], partner
            ).astype(bf16)
            out_ref[1, :, lanes] = unturn(
                dk[:, lanes], cos_ref[...], sin_ref[...], partner
            ).astype(bf16)
        out_ref[2] = dv[...].astype(bf16)


def attend_back(
    seen, qkv, attended, grad, lse, few, hide, cosine, sine, partner, pair_lo, pair_hi, kept=None
):
    width = qkv.shape[1] // 3
    pair = 2 * HEAD
    lanes = pair * PAIRS
    groups = width // lanes
    at = pair_lo // PAIRS
    some = (pair_hi - pair_lo) // PAIRS
    inner = functools.partial(attend_back_kernel, 1.0 / math.sqrt(HEAD))
    kernel = inner
    more, alias = [], {}
    if kept is not None:
        more, alias = [kept], {12: 0}

        def kernel(*refs):
            inner(*refs[:12], *refs[13:])

    def whole(h, f, s):
        return (0, 0)

    return pl.pallas_call(
        kernel,
        grid_spec=pltpu.PrefetchScalarGridSpec(
            num_scalar_prefetch=1,
            grid=(some, FRAMES),
            in_specs=[
                pl.BlockSpec((ROWS, lanes), lambda h, f, s: (0, at + h)),
                pl.BlockSpec((ROWS, lanes), lambda h, f, s: (0, at + groups + h)),
                pl.BlockSpec((ROWS, lanes), lambda h, f, s: (0, at + 2 * groups + h)),
                pl.BlockSpec((ROWS, lanes), lambda h, f, s: (0, at + h)),
                pl.BlockSpec((ROWS, lanes), lambda h, f, s: (0, at + h)),
                pl.BlockSpec((1, 2 * PAIRS, BODY), lambda h, f, s: (h, 0, 0)),
                pl.BlockSpec((1, 1, 2 * PAIRS * FEW), lambda h, f, s: (h, 0, 0)),
                pl.BlockSpec((ROWS, 2 * PAIRS * FEW), whole),
                pl.BlockSpec((ROWS, pair), whole),
                pl.BlockSpec((ROWS, pair), whole),
                pl.BlockSpec((pair, pair), whole),
            ]
            + [pl.BlockSpec(memory_space=pl.ANY)] * len(more),
            out_specs=pl.BlockSpec((3, ROWS, lanes), lambda h, f, s: (0, 0, at + h)),
            scratch_shapes=[
                pltpu.VMEM((lanes, ROWS), bf16),
                pltpu.VMEM((ROWS, lanes), f32),
                pltpu.VMEM((ROWS, lanes), f32),
                pltpu.VMEM((ROWS, lanes), f32),
            ],
        ),
        out_shape=jax.ShapeDtypeStruct((3, ROWS, width), bf16),
        input_output_aliases=alias,
        compiler_params=pltpu.CompilerParams(vmem_limit_bytes=vmem_most),
        cost_estimate=cost(7.6 * some),
    )(seen, qkv, qkv, qkv, attended, grad, lse, few, hide, cosine, sine, partner, *more)


def project_kernel(scale, x_ref, w_ref, b_ref, cos_ref, sin_ref, part_ref, out_ref):
    j = pl.program_id(0)
    third = pl.num_programs(0) // 3
    lanes = 2 * HEAD
    wide = part_ref.shape[0]
    w = w_ref[...]
    mixed = dot_n(x_ref[...], w) + b_ref[...]

    @pl.when(j < 2 * third)
    def _():
        by = jnp.where(j < third, scale, 1.0)
        for left in range(0, w.shape[1], wide):
            x = mixed[:, left : left + wide]
            upper = x.astype(bf16)
            lower = (x - upper.astype(f32)).astype(bf16)
            other = dot_n(upper, part_ref[...]) + dot_n(lower, part_ref[...])
            for at in range(0, wide, lanes):
                here = mixed[:, left + at : left + at + lanes] * cos_ref[...]
                there = other[:, at : at + lanes] * sin_ref[...]
                out_ref[:, left + at : left + at + lanes] = ((here + there) * by).astype(bf16)

    @pl.when(j >= 2 * third)
    def _():
        out_ref[...] = mixed.astype(bf16)


def project(x, w, bias, cosine, sine, partner):
    rows, width = x.shape
    cols = 512
    lanes = 2 * HEAD
    wide = 2 * lanes
    zero = jnp.zeros_like(partner)
    partner = jnp.block([[partner, zero], [zero, partner]])

    def whole(j):
        return (0, 0)

    return pl.pallas_call(
        functools.partial(project_kernel, 1.0 / math.sqrt(HEAD)),
        grid=(w.shape[1] // cols,),
        in_specs=[
            pl.BlockSpec((rows, width), whole),
            pl.BlockSpec((width, cols), lambda j: (0, j)),
            pl.BlockSpec((1, cols), lambda j: (0, j)),
            pl.BlockSpec((rows, lanes), whole),
            pl.BlockSpec((rows, lanes), whole),
            pl.BlockSpec((wide, wide), whole),
        ],
        out_specs=pl.BlockSpec((rows, cols), lambda j: (0, j)),
        out_shape=jax.ShapeDtypeStruct((rows, w.shape[1]), bf16),
        compiler_params=pltpu.CompilerParams(vmem_limit_bytes=vmem_most),
        cost_estimate=cost(4),
    )(x, w, bias, cosine, sine, partner)


def turn_tables(frame_ids):
    frequency, which, sign = [], [], []
    for kind, part in enumerate(part_sizes):
        half = part // 2
        frequency += [10000.0 ** (-i / half) for i in range(half)] * 2
        which += [kind] * part
        sign += [-1.0] * half + [1.0] * half
    frequency = jnp.asarray(np.tile(np.array(frequency, np.float32), 2))
    which = np.tile(np.array(which), 2)
    sign = np.tile(np.array(sign, np.float32), 2)
    time = frame_ids[:: FRAME_ROWS].astype(f32)[:, None] * frequency
    place = np.arange(GRID, dtype=np.float32)[:, None] * frequency

    def table(of, empty):
        by_time, by_place = of(time), of(place)
        still = jnp.full((FRAMES, 2, which.size), empty, f32)
        patches = jnp.where(which == 1, by_place[:, None], by_place[None]).reshape(1, PATCH, -1)
        patches = jnp.where(which == 0, by_time[:, None], patches).reshape(BODY, -1)
        few = jnp.where(which == 0, by_time[:, None], still).reshape(FEW, -1)
        return jnp.concatenate([patches, few, jnp.zeros_like(few)], axis=0)

    return table(jnp.cos, 1.0), table(lambda v: jnp.sin(v) * sign, 0.0)


def partner_matrix():
    lanes = 2 * HEAD
    matrix = np.zeros((lanes, lanes), np.float32)
    for head in range(2):
        at = head * HEAD
        for part in part_sizes:
            for i in range(part // 2):
                matrix[at + i, at + i + part // 2] = 1.0
                matrix[at + i + part // 2, at + i] = 1.0
            at += part
    return jnp.asarray(matrix, bf16)


def seen_frames(offset_row):
    frame = jnp.arange(FRAMES, dtype=jnp.int32)
    start = jnp.where(frame >= offset_row[1], offset_row[1], 0)
    return jnp.where(frame < offset_row[2], frame - start + 1, 0)


def hidden_few(seen):
    frame_of = np.concatenate([np.repeat(np.arange(FRAMES), PATCH), np.repeat(np.arange(FRAMES), 2), np.full(EXTRA - FEW, FRAMES)])
    own = np.zeros((ROWS, FEW), bool)
    own[BODY + np.arange(FEW), np.arange(FEW)] = True
    frame = jnp.asarray(frame_of, jnp.int32)[:, None]
    query = jnp.arange(FEW, dtype=jnp.int32)[None, :] // 2
    count = jnp.repeat(seen, 2)[None, :]
    allowed = ((frame <= query) & (frame > query - count)) | jnp.asarray(own)
    return jnp.tile(jnp.where(allowed, 0.0, masked_value), (1, 2 * PAIRS))


def place(p, line, orders, core):
    own, other = relatives(line, orders, core)
    return (1, other.index(p)) if p in other else (0, own.index(p))


def find_piece(rels, p):
    for c, rel in enumerate(rels):
        if p in rel:
            return c, rel.index(p)
    raise ValueError(p)


def feed_kernel(
    rels, where, me_ref, x_ref, g_ref, bias_ref, shift_ref, mid_ref, up_ref, *refs
):
    pieces, refs = refs[: len(rels)], refs[len(rels) :]
    out_ref, gx_ref, gb_ref = refs[:3]
    grads = refs[3:5]
    wu, wd, su, sd, acc, xt, act, gup, in_sem, out_sem, mid_sem = refs[5:]
    count = sum(len(q) for q in rels)
    blocks = FEED_BLOCKS
    each = count // blocks
    shift = each.bit_length() - 1
    i = pl.program_id(0)
    me = me_ref[0]
    width = x_ref.shape[1]
    cols = wu.shape[2]
    rows = width // count
    part = cols // each
    hidden = blocks * cols
    stacks = part // rows
    slot = lax.rem(i, 2)

    def group(j):
        return lax.bitwise_xor(lax.shift_right_logical(me, shift), j)

    def fetch(j, to):
        at = pl.multiple_of(group(j) * cols, cols)
        pltpu.make_async_copy(up_ref.at[:, pl.ds(at, cols)], wu.at[to], in_sem.at[0, to]).start()
        for k in range(blocks):

            @pl.when(j == k)
            def _():
                for p in range(each):
                    c, n = find_piece(rels, (k << shift) | p)
                    start = pl.multiple_of(lax.bitwise_xor(me & (each - 1), p) * part, part)
                    for q in range(stacks):
                        pltpu.make_async_copy(
                            pieces[c].at[n, :, pl.ds(q * width, width)],
                            wd.at[to, pl.ds(start + q * rows, rows), :],
                            in_sem.at[1, to],
                        ).start()

    middle = pltpu.make_async_copy(mid_ref, acc, mid_sem)

    @pl.when(i == 0)
    def _():
        fetch(i, slot)
        middle.start()
        xt[...] = x_ref[...].T
        gx_ref[...] = jnp.zeros_like(gx_ref)

    @pl.when(i + 1 < blocks)
    def _():
        fetch(i + 1, 1 - slot)

    pltpu.make_async_copy(wu.at[slot], wu.at[slot], in_sem.at[0, slot]).wait()
    pltpu.make_async_copy(wd.at[slot], wd.at[slot], in_sem.at[1, slot]).wait()
    half = cols // 2
    low, high = slice(0, half), slice(half, cols)

    def curves(u, ga):
        e = jnp.exp2(u * u * (-0.5 * math.log2(math.e)))
        d = 1.0 + jnp.abs(u) * (0.3275911 * inv_sqrt_two)
        t = pl.reciprocal(d, approx=True)
        t = t * (2.0 - d * t)
        poly = t * (0.127414796 + t * (-0.142248368 + t * (0.7107068705 + t * (-0.7265760135 + t * 0.5307027145))))
        tail = poly * e
        phi = jnp.where(u >= 0.0, 1.0 - tail, tail)
        gu = ga * (phi + u * (e * inv_sqrt_tau))
        return (u * phi).astype(bf16), gu.astype(bf16), jnp.sum(gu, axis=0, keepdims=True)

    u0 = dot_n(x_ref[...], wu[slot, :, low]) + bias_ref[:, low]
    g0 = dot_t(g_ref[...], wd[slot, low, :])
    u1 = dot_n(x_ref[...], wu[slot, :, high]) + bias_ref[:, high]
    g1 = dot_t(g_ref[...], wd[slot, high, :])
    a, g, total = curves(u0, g0)
    act[:, low] = a
    gup[:, low] = g
    gb_ref[:, low] = total

    @pl.when(i >= 2)
    def _():
        pltpu.make_async_copy(su.at[slot], su.at[slot], out_sem.at[0, slot]).wait()
        pltpu.make_async_copy(sd.at[slot], sd.at[slot], out_sem.at[1, slot]).wait()

    @pl.when(i == 0)
    def _():
        middle.wait()

    sd[slot, low, :] = dot_tl(act[:, low], g_ref[...]).astype(bf16)
    su[slot, :, low] = dot_n(xt[...], gup[:, low]).astype(bf16)
    a, g, total = curves(u1, g1)
    act[:, high] = a
    gup[:, high] = g
    gb_ref[:, high] = total
    acc[...] += dot_n(act[...], wd[slot])
    gx_ref[...] += dot_t(gup[...], wu[slot])
    sd[slot, high, :] = dot_tl(act[:, high], g_ref[...]).astype(bf16)
    su[slot, :, high] = dot_n(xt[...], gup[:, high]).astype(bf16)
    at = pl.multiple_of(group(i) * cols, cols)
    for p in range(count):
        c, n = place(p, *where)
        start = pl.multiple_of(lax.bitwise_xor(me, p) * rows, rows)
        pltpu.make_async_copy(
            su.at[slot, pl.ds(start, rows), :],
            grads[c].at[n, :, pl.ds(at, cols)],
            out_sem.at[0, slot],
        ).start()
    for k in range(blocks):

        @pl.when(i == k)
        def _():
            for p in range(each):
                c, n = place((k << shift) | p, *where)
                start = pl.multiple_of(lax.bitwise_xor(me & (each - 1), p) * part, part)
                for q in range(stacks):
                    pltpu.make_async_copy(
                        sd.at[slot, pl.ds(start + q * rows, rows), :],
                        grads[c].at[n, :, pl.ds(hidden + q * width, width)],
                        out_sem.at[1, slot],
                    ).start()

    @pl.when(i == blocks - 1)
    def _():
        out_ref[...] = (acc[...] + shift_ref[...]).astype(bf16)
        for s in range(2):
            pltpu.make_async_copy(su.at[s], su.at[s], out_sem.at[0, s]).wait()
            pltpu.make_async_copy(sd.at[s], sd.at[s], out_sem.at[1, s]).wait()


FEED_BLOCKS = 4


def feed(x, grad, middle, bias, shift, up, pieces, line, orders, core, me):
    rels = [q for _, q in pieces]
    count = sum(len(q) for q in rels)
    tokens, width = x.shape
    hidden = bias.shape[1]
    cols = hidden // FEED_BLOCKS
    shift_by = (count // FEED_BLOCKS).bit_length() - 1

    def block(i, me_ref):
        return (0, lax.bitwise_xor(lax.shift_right_logical(me_ref[0], shift_by), i))

    def whole(i, me_ref):
        return (0, 0)

    once = pl.Buffered(1)
    anywhere = pl.BlockSpec(memory_space=pl.ANY)
    return pl.pallas_call(
        functools.partial(feed_kernel, rels, (line, orders, core)),
        grid_spec=pltpu.PrefetchScalarGridSpec(
            num_scalar_prefetch=1,
            grid=(FEED_BLOCKS,),
            in_specs=[
                pl.BlockSpec((tokens, width), whole, pipeline_mode=once),
                pl.BlockSpec((tokens, width), whole, pipeline_mode=once),
                pl.BlockSpec((1, cols), block),
                pl.BlockSpec((1, width), whole),
                anywhere,
                anywhere,
            ]
            + [anywhere] * len(pieces),
            out_specs=[
                pl.BlockSpec((tokens, width), whole, pipeline_mode=once),
                pl.BlockSpec((tokens, width), whole, pipeline_mode=once),
                pl.BlockSpec((1, cols), block),
            ]
            + [anywhere] * 2,
            scratch_shapes=[
                pltpu.VMEM((2, width, cols), bf16),
                pltpu.VMEM((2, cols, width), bf16),
                pltpu.VMEM((2, width, cols), bf16),
                pltpu.VMEM((2, cols, width), bf16),
                pltpu.VMEM((tokens, width), f32),
                pltpu.VMEM((width, tokens), bf16),
                pltpu.VMEM((tokens, cols), bf16),
                pltpu.VMEM((tokens, cols), bf16),
                pltpu.SemaphoreType.DMA((2, 2)),
                pltpu.SemaphoreType.DMA((2, 2)),
                pltpu.SemaphoreType.DMA,
            ],
        ),
        out_shape=[
            jax.ShapeDtypeStruct((tokens, width), bf16),
            jax.ShapeDtypeStruct((tokens, width), f32),
            jax.ShapeDtypeStruct((1, hidden), f32),
        ]
        + [jax.ShapeDtypeStruct((count // 2, width // count, 2 * hidden), bf16)] * 2,
        compiler_params=pltpu.CompilerParams(vmem_limit_bytes=vmem_most),
        cost_estimate=cost(20),
    )(me, x, grad, bias, shift, middle, up, *[v for v, _ in pieces])


def weight_kernel(where, left, count, me_ref, x_ref, g_ref, *refs):
    outs, (xt, staged, sem) = refs[-5:-3], refs[-3:]
    j = pl.program_id(0)
    me = me_ref[0]
    slot = lax.rem(j, 2)
    width, cols = staged.shape[1:]
    rows = width // count

    @pl.when(j == 0)
    def _():
        xt[...] = x_ref[...].T

    @pl.when(j >= 2)
    def _():
        pltpu.make_async_copy(staged.at[slot], staged.at[slot], sem.at[slot]).wait()

    staged[slot] = dot_n(xt[...], g_ref[...].reshape(g_ref.shape[-2:])).astype(bf16)
    at = pl.multiple_of(left + j * cols, cols)
    for out, rel in zip(outs, where):
        for n, p in enumerate(rel):
            start = pl.multiple_of(lax.bitwise_xor(me, p) * rows, rows)
            pltpu.make_async_copy(
                staged.at[slot, pl.ds(start, rows), :], out.at[n, :, pl.ds(at, cols)], sem.at[slot]
            ).start()

    @pl.when(j == pl.num_programs(0) - 1)
    def _():
        for s in range(2):
            pltpu.make_async_copy(staged.at[s], staged.at[s], sem.at[s]).wait()


def weight_grad(x, grad, where, left, total, me, into=()):
    tokens, width = x.shape
    count = sum(len(q) for q in where)
    cols = 512
    deep = grad.ndim == 3
    found = grad.shape[-1] * (grad.shape[0] if deep else 1)
    per = grad.shape[-1] // cols
    if deep:
        spec = pl.BlockSpec((1, tokens, cols), lambda j, m: (j // per, 0, j % per))
    else:
        spec = pl.BlockSpec((tokens, cols), lambda j, m: (0, j))
    anywhere = pl.BlockSpec(memory_space=pl.ANY)
    return pl.pallas_call(
        functools.partial(weight_kernel, where, left, count),
        grid_spec=pltpu.PrefetchScalarGridSpec(
            num_scalar_prefetch=1,
            grid=(found // cols,),
            in_specs=[pl.BlockSpec((tokens, width), lambda j, m: (0, 0)), spec]
            + [anywhere] * len(into),
            out_specs=[anywhere] * 2,
            scratch_shapes=[
                pltpu.VMEM((width, tokens), bf16),
                pltpu.VMEM((2, width, cols), bf16),
                pltpu.SemaphoreType.DMA((2,)),
            ],
        ),
        out_shape=[jax.ShapeDtypeStruct((count // 2, width // count, total), bf16)] * 2,
        input_output_aliases={3 + i: i for i in range(len(into))},
        compiler_params=pltpu.CompilerParams(vmem_limit_bytes=vmem_most),
        cost_estimate=cost(0.5 * found / 512),
    )(me, x, grad, *into)


def sort_kernel(x_ref, g_ref, x_out, g_out, sum_ref, wide):
    for source, target in ((x_ref, x_out), (g_ref, g_out)):
        wide[...] = source[...].astype(f32)
        for f in range(FRAMES):
            at = f * FRAME_ROWS + 2
            target[f * PATCH : (f + 1) * PATCH, :] = wide[at : at + PATCH, :].astype(bf16)
        few = [wide[f * FRAME_ROWS : f * FRAME_ROWS + 2, :] for f in range(FRAMES)]
        few = jnp.concatenate(few + [jnp.zeros((EXTRA - FEW, wide.shape[1]), f32)], axis=0)
        target[BODY:ROWS, :] = few.astype(bf16)
    sum_ref[...] = jnp.sum(wide[...], axis=0, keepdims=True)


def sort_rows(x, grad):
    tokens, width = x.shape
    return pl.pallas_call(
        sort_kernel,
        out_shape=[jax.ShapeDtypeStruct((ROWS, width), bf16)] * 2
        + [jax.ShapeDtypeStruct((1, width), f32)],
        scratch_shapes=[pltpu.VMEM((tokens, width), f32)],
        compiler_params=pltpu.CompilerParams(vmem_limit_bytes=vmem_most),
        cost_estimate=cost(1),
    )(x, grad)


def unsort_kernel(x_ref, out_ref, *scratch):
    wide = scratch[0] if scratch else out_ref
    for f in range(FRAMES):
        at = f * FRAME_ROWS
        wide[at + 2 : at + FRAME_ROWS, :] = x_ref[f * PATCH : (f + 1) * PATCH, :].astype(f32)
    few = x_ref[BODY:ROWS, :].astype(f32)
    for f in range(FRAMES):
        wide[f * FRAME_ROWS : f * FRAME_ROWS + 2, :] = few[2 * f : 2 * f + 2]
    if scratch:
        out_ref[...] = wide[...].astype(out_ref.dtype)


def unsort_rows(x):
    tokens, width = FRAMES * FRAME_ROWS, x.shape[1]
    return pl.pallas_call(
        unsort_kernel,
        out_shape=jax.ShapeDtypeStruct((tokens, width), x.dtype),
        scratch_shapes=[] if x.dtype == f32 else [pltpu.VMEM((tokens, width), f32)],
        compiler_params=pltpu.CompilerParams(vmem_limit_bytes=vmem_most),
        cost_estimate=cost(1),
    )(x)


def last_kernel(g_ref, w_ref, x_ref, mid_ref, gain_ref, out_ref, gain_out, bias_out, sum_ref, acc):
    i = pl.program_id(0)
    g = g_ref[0]
    more = dot_t(g, w_ref[...])

    @pl.when(i == 0)
    def _():
        acc[...] = more

    @pl.when(i > 0)
    def _():
        acc[...] += more

    sum_ref[0] = jnp.sum(g.astype(f32), axis=0, keepdims=True)

    @pl.when(i == pl.num_programs(0) - 1)
    def _():
        gain = gain_ref[...]
        gain_sum, bias_sum = 0.0, 0.0
        spans = [(f * PATCH, PATCH) for f in range(FRAMES)] + [(BODY, EXTRA)]
        for at, size in spans:
            rows = slice(at, at + size)
            x = x_ref[rows, :].astype(f32)
            center = x - jnp.mean(x, axis=-1, keepdims=True)
            inverse = lax.rsqrt(jnp.mean(center * center, axis=-1, keepdims=True) + eps_norm)
            unit = center * inverse
            grad = acc[rows, :]
            gain_sum += jnp.sum(grad * unit, axis=0, keepdims=True)
            bias_sum += jnp.sum(grad, axis=0, keepdims=True)
            scaled = grad * gain
            mean_grad = jnp.mean(scaled, axis=-1, keepdims=True)
            mean_cross = jnp.mean(scaled * unit, axis=-1, keepdims=True)
            found = mid_ref[rows, :] + inverse * (scaled - mean_grad - unit * mean_cross)
            if size == PATCH:
                start = at // PATCH * FRAME_ROWS + 2
                out_ref[start : start + PATCH, :] = found
            else:
                for f in range(FRAMES):
                    out_ref[f * FRAME_ROWS : f * FRAME_ROWS + 2, :] = found[2 * f : 2 * f + 2]
        gain_out[...] = gain_sum
        bias_out[...] = bias_sum


def last_step(grad_mixed, w, x, middle, gain):
    parts, rows, width = grad_mixed.shape

    def whole(i):
        return (0, 0)

    once = pl.Buffered(1)
    return pl.pallas_call(
        last_kernel,
        grid=(parts,),
        in_specs=[
            pl.BlockSpec((1, rows, width), lambda i: (i, 0, 0)),
            pl.BlockSpec((width, width), lambda i: (0, i)),
            pl.BlockSpec((rows, width), whole, pipeline_mode=once),
            pl.BlockSpec((rows, width), whole, pipeline_mode=once),
            pl.BlockSpec((1, width), whole),
        ],
        out_specs=[
            pl.BlockSpec((FRAMES * FRAME_ROWS, width), whole, pipeline_mode=once),
            pl.BlockSpec((1, width), whole),
            pl.BlockSpec((1, width), whole),
            pl.BlockSpec((1, 1, width), lambda i: (i, 0, 0)),
        ],
        out_shape=[
            jax.ShapeDtypeStruct((FRAMES * FRAME_ROWS, width), f32),
            jax.ShapeDtypeStruct((1, width), f32),
            jax.ShapeDtypeStruct((1, width), f32),
            jax.ShapeDtypeStruct((parts, 1, width), f32),
        ],
        scratch_shapes=[pltpu.VMEM((rows, width), f32)],
        compiler_params=pltpu.CompilerParams(vmem_limit_bytes=vmem_most),
        cost_estimate=cost(5),
    )(grad_mixed, w, x, middle, gain)


def normalize(values, gain, bias_add):
    center = values - jnp.mean(values, axis=-1, keepdims=True)
    scale_inv = lax.rsqrt(jnp.mean(center * center, axis=-1, keepdims=True) + eps_norm)
    unit_rows = center * scale_inv
    return (unit_rows * gain + bias_add, unit_rows, scale_inv)


def norm_back(grad_out, unit_rows, scale_inv, gain):
    scaled = grad_out * gain
    mean_grad = jnp.mean(scaled, axis=-1, keepdims=True)
    mean_cross = jnp.mean(scaled * unit_rows, axis=-1, keepdims=True)
    return scale_inv * (scaled - mean_grad - unit_rows * mean_cross)


def gather_joined(groups, orders, core, sizes):
    found = []
    for pieces, order in zip(groups, orders):
        for bit in order[:-1]:
            pieces = pieces + moved(pieces, bit, sizes)
        arrays, rels = zip(*pieces)
        pieces = [(jnp.concatenate(arrays, axis=0), sum(rels, []))]
        found += pieces + moved(pieces, order[-1], sizes)
    return found + moved(found, core, sizes)


def gather_rest(groups, orders, core, sizes):
    found = []
    for pieces, order in zip(groups, orders):
        for bit in order:
            pieces = pieces + moved(pieces, bit, sizes)
        found += pieces
    return found + moved(found, core, sizes)


def body(
    sizes,
    tokens,
    frame_ids,
    pad_mask,
    episode_offsets,
    ln1_gain,
    ln1_bias,
    w_qkv,
    b_qkv,
    w_out,
    b_out,
    ln2_gain,
    ln2_bias,
    w_up,
    b_up,
    w_down,
    b_down,
    cotangent,
):
    width = tokens.shape[1]
    count = sizes[0] * sizes[1]
    me = (lax.axis_index("dp") * sizes[1] + lax.axis_index("fsdp")).astype(jnp.int32)[None]
    core, line, orders = bit_orders(sizes)
    where = relatives(line, orders, core)
    out_matrix = lax.all_gather(w_out, ("dp", "fsdp"), axis=0, tiled=True)
    up_matrix = lax.all_gather(w_up, ("dp", "fsdp"), axis=0, tiled=True)
    smalls = [ln1_gain, ln1_bias, b_qkv, b_out, ln2_gain, ln2_bias, b_up, b_down]
    rows, third = w_qkv.shape
    first_unit = jnp.concatenate([w_qkv, pack_small(smalls, rows)], axis=1)
    firsts = gather_line(first_unit, line, sizes)
    tokens_in, cot, grad_b_down_local = sort_rows(tokens, cotangent)
    first = gather_joined(firsts, orders, core, sizes)
    seen = seen_frames(episode_offsets[0])
    hide = hidden_few(seen)
    cosine, sine = turn_tables(frame_ids)
    partner = partner_matrix()
    values_in = tokens_in.astype(f32)
    qkv_matrix, whole_small = assemble(
        first, me, [(0, rows, 0, third), (0, rows, third, first_unit.shape[1] - third)]
    )
    gain_one, bias_one, qkv_rows, *_ = unpack_small(whole_small, rows, smalls)
    stacked = [w_down[at : at + rows] for at in range(0, w_down.shape[0], rows)]
    second_unit = after(jnp.concatenate(stacked, axis=1), first[0][0], first[2][0])
    seconds = gather_line(second_unit, line, sizes)
    normed_one, unit_one, inv_one = normalize(values_in, gain_one, bias_one)
    normed_one = normed_one.astype(bf16)
    qkv = project(normed_one, qkv_matrix, qkv_rows.reshape(1, 3 * width), cosine, sine, partner)
    pairs = width // (2 * HEAD)
    seconds = [after_pieces(pieces, qkv_matrix) for pieces in seconds]
    seconds = [
        [pieces, moved(pieces, order[0], sizes) + moved(pieces, order[1], sizes)]
        for pieces, order in zip(seconds, orders)
    ]
    attended, lse_a, few_a = attend(seen, qkv, hide, 0, pairs // 2)
    seconds = [[near, after_pieces(far, attended)] for near, far in seconds]
    found = []
    for (near, far), order in zip(seconds, orders):
        pieces = near + far + moved(far[:1], order[1], sizes)
        for bit in order[2:]:
            pieces = pieces + moved(pieces, bit, sizes)
        found.append(pieces)
    attended, lse_b, few_b = attend(seen, qkv, hide, pairs // 2, pairs, attended)
    second = []
    for pieces in found:
        arrays, rels = zip(*pieces)
        pieces = [(after(jnp.concatenate(arrays, axis=0), attended), sum(rels, []))]
        second += pieces + moved(pieces, core, sizes)
    whole_small = after(whole_small, attended)
    *_, out_bias, gain_two, bias_two, up_bias, down_bias = unpack_small(whole_small, rows, smalls)
    hidden = w_up.shape[1]
    middle = values_in + jnp.dot(attended, out_matrix, preferred_element_type=f32) + out_bias
    normed_two, unit_two, inv_two = normalize(middle, gain_two, bias_two)
    normed_two = normed_two.astype(bf16)
    result, grad_normed_two, grad_b_up_local, feed_own, feed_other = feed(
        normed_two,
        cot,
        middle,
        up_bias[None],
        down_bias[None],
        up_matrix,
        second,
        line,
        orders,
        core,
        me,
    )
    feed_taken = swap(feed_other, 1 << core, sizes)
    grad_gain_two = jnp.sum(grad_normed_two * unit_two, axis=0)
    grad_bias_two = jnp.sum(grad_normed_two, axis=0)
    grad_middle = cot.astype(f32) + norm_back(grad_normed_two, unit_two, inv_two, gain_two)
    grad_branch = grad_middle.astype(bf16)
    grad_b_out_local = jnp.sum(grad_branch.astype(f32), axis=0)
    grads = weight_grad(attended, grad_branch, where, third, third + width, me)
    grad_attended = dot_t(grad_branch, out_matrix).astype(bf16)
    feed_own = after(feed_own, feed_taken, grads[0])
    feed_sums = reduce_start(feed_own, feed_taken, orders, sizes)
    grad_attended = after(grad_attended, grads[0], *[v for group in feed_sums for v in group[:1] + group[2:]])
    feed_sums = [group[:2] for group in feed_sums]
    back = (hide, cosine, sine, partner)
    grad_mixed = attend_back(
        seen, qkv, attended, grad_attended, lse_a, few_a, *back, 0, pairs // 2
    )
    grad_mixed = attend_back(
        seen, qkv, attended, grad_attended, lse_b, few_b, *back, pairs // 2, pairs, grad_mixed
    )
    steps = len(orders[0])
    for step in range(1, steps):
        feed_sums = together(feed_sums, grad_mixed)
        feed_sums = reduce_next(feed_sums, orders, step, sizes)
        grad_mixed = after(grad_mixed, *[v for group in feed_sums for v in group[:1] + group[2:]])
        feed_sums = [group[:2] for group in feed_sums]
    own, other = weight_grad(normed_one, grad_mixed, where, 0, third + width, me, grads)
    taken = swap(other, 1 << core, sizes)
    feed_parts = line_parts(together(feed_sums))
    feed_parts = feed_parts[:1] + [v.astype(bf16) for v in feed_parts[1:]]
    own = after(own, *feed_parts[1:])
    sums = reduce_start(own, taken, orders, sizes)
    going = [v for group in sums for v in group[:1] + group[2:]]
    sums = [group[:2] for group in sums]
    grad_mixed = after(grad_mixed, *going)
    grad_tokens, grad_gain_one, grad_bias_one, grad_b_qkv_local = last_step(
        grad_mixed, qkv_matrix, tokens_in, grad_middle, gain_one[None]
    )
    vectors = [
        grad_gain_one[0],
        grad_bias_one[0],
        grad_b_qkv_local[:, 0],
        grad_b_out_local,
        grad_gain_two,
        grad_bias_two,
        grad_b_up_local[0],
        grad_b_down_local[0],
    ]
    small_own, small_other = small_units(vectors, rows, where, me)
    small = jnp.concatenate([small_own, small_other], axis=2).astype(bf16)
    half = small.shape[0] // 2
    joined = []
    for (kept, came), at, order in zip(sums, (0, half), orders):
        here = small[at : at + half // 2]
        there = swap(small[at + half // 2 : at + half], 1 << order[-1], sizes)
        joined.append(
            (jnp.concatenate([kept, here], axis=2), jnp.concatenate([came, there], axis=2))
        )
    sums = joined
    for step in range(1, steps):
        sums = [group[:2] for group in reduce_next(sums, orders, step, sizes)]
    parts = line_parts(sums)
    parts = parts[:1] + [v.astype(bf16) for v in parts[1:]]
    feed_parts[0] = after(feed_parts[0], *parts[1:])
    output = unsort_rows(after(result, *parts[1:]))
    parts[0] = after(parts[0], output)
    feed_sum = reduce_line(feed_parts, line, sizes)
    sum_one = reduce_line(parts, line, sizes)
    small = sum_one[:, third + width :]
    small = small[:, :128] + swap(small[:, 128:], 1 << core, sizes)
    small = small_parts(small, vectors, count)
    sum_down = feed_sum[:, hidden:].reshape(rows, -1, width).swapaxes(0, 1).reshape(-1, width)
    return (
        output,
        grad_tokens,
        small[0],
        small[1],
        sum_one[:, :third],
        small[2],
        sum_one[:, third : third + width],
        small[3],
        small[4],
        small[5],
        feed_sum[:, :hidden],
        small[6],
        sum_down,
        small[7],
    )


def solution(mesh):
    placed = (
        P(("dp", "fsdp"), None),
        P(("dp", "fsdp")),
        P(("dp", "fsdp")),
        P(("dp", "fsdp"), None),
        P(("dp", "fsdp")),
        P(("dp", "fsdp")),
        P(("dp", "fsdp"), None),
        P(None, ("dp", "fsdp")),
        P(("dp", "fsdp"), None),
        P(("dp", "fsdp")),
        P(("dp", "fsdp")),
        P(("dp", "fsdp")),
        P(("dp", "fsdp"), None),
        P(("dp", "fsdp")),
        P(("dp", "fsdp"), None),
        P(("dp", "fsdp")),
        P(("dp", "fsdp"), None),
    )
    sizes = (mesh.shape["dp"], mesh.shape["fsdp"])
    return jax.shard_map(
        functools.partial(body, sizes),
        mesh=mesh,
        in_specs=placed,
        out_specs=(
            P(("dp", "fsdp"), None),
            P(("dp", "fsdp"), None),
            P(("dp", "fsdp")),
            P(("dp", "fsdp")),
            P(("dp", "fsdp"), None),
            P(None, ("dp", "fsdp")),
            P(("dp", "fsdp"), None),
            P(("dp", "fsdp")),
            P(("dp", "fsdp")),
            P(("dp", "fsdp")),
            P(("dp", "fsdp"), None),
            P(("dp", "fsdp")),
            P(("dp", "fsdp"), None),
            P(("dp", "fsdp")),
        ),
        check_vma=False,
    )
```

```python
import functools
import math

import jax
import jax.numpy as jnp
import numpy as np
from jax import lax
from jax.experimental import pallas as pl
from jax.experimental.pallas import tpu as pltpu
from jax.sharding import PartitionSpec as P

HEAD = 64
GRID = 16
FRAME_ROWS = 258
FRAMES = 4
PATCH = GRID * GRID
EXTRA = 16
FEW = 8
BODY = FRAMES * PATCH
ROWS = BODY + EXTRA
eps_norm = 1e-06
part_sizes = (24, 20, 20)
masked_value = -1e30
inv_sqrt_two = 1.0 / math.sqrt(2.0)
inv_sqrt_tau = 1.0 / math.sqrt(2.0 * math.pi)
f32 = jnp.float32
bf16 = jnp.bfloat16
vmem_most = 60 * 1024 * 1024


def cost(micros):
    return pl.CostEstimate(flops=int(micros * 1e9), bytes_accessed=0, transcendentals=0)


def log2(n):
    return n.bit_length() - 1


def swap(value, mask, sizes):
    count = sizes[0] * sizes[1]
    return lax.ppermute(value, ("dp", "fsdp"), [(i, i ^ mask) for i in range(count)])


def bit_orders(sizes):
    inner, outer = log2(sizes[1]), log2(sizes[0])
    line = list(range(1, inner))
    cross = [0]
    other = list(range(inner + 1, inner + outer))
    return inner, line, (cross + other, other + cross)


def spread(bits):
    rel = [0]
    for bit in bits:
        rel = rel + [p | (1 << bit) for p in rel]
    return rel


def gather_line(shard, line, sizes):
    rel = spread(line)
    held = [shard[None]] + [swap(shard[None], p, sizes) for p in rel[1:]]
    half = len(rel) // 2
    return [
        [(jnp.concatenate(held[at : at + half], axis=0), rel[at : at + half])]
        for at in (0, half)
    ]


def gather_doubling(shard, line, sizes):
    held, rel = shard[None], [0]
    for bit in line[:-1]:
        held = jnp.concatenate([held, swap(held, 1 << bit, sizes)], axis=0)
        rel = rel + [p | (1 << bit) for p in rel]
    return [[(held, rel)], moved([(held, rel)], line[-1], sizes)]


def moved(pieces, bit, sizes):
    return [(swap(v, 1 << bit, sizes), [p | (1 << bit) for p in q]) for v, q in pieces]


def relatives(line, orders, core):
    low, top = line[:-1], 1 << line[-1]
    rel = spread(low + orders[0]) + [p | top for p in spread(low + orders[1])]
    return rel, [p | (1 << core) for p in rel]


def reduce_start(own, taken, orders, sizes):
    half = own.shape[0] // 2
    return [
        reduce_step(own[at : at + half], taken[at : at + half], 1 << order[-1], sizes)
        for at, order in zip((0, half), orders)
    ]


def reduce_step(kept, taken, mask, sizes):
    kind = kept.dtype
    half = kept.shape[0] // 2
    sent = (kept[half:].astype(f32) + taken[half:].astype(f32)).astype(kind)
    held = (kept[:half].astype(f32) + taken[:half].astype(f32)).astype(kind)
    return held, swap(sent, mask, sizes), sent


def reduce_next(groups, orders, step, sizes):
    return [
        reduce_step(*group, 1 << order[-1 - step], sizes) for group, order in zip(groups, orders)
    ]


def together(groups, *others):
    came = [group[1] for group in groups]
    return [(after(kept, *came, *others), taken) for kept, taken in groups]


def after_pieces(pieces, *others):
    return [(after(v, *others), q) for v, q in pieces]


def line_parts(groups):
    return [
        kept[n].astype(f32) + taken[n].astype(f32)
        for kept, taken in groups
        for n in range(kept.shape[0])
    ]


def reduce_line(parts, line, sizes):
    total = parts[0]
    for part, p in zip(parts[1:], spread(line)[1:]):
        total = total + swap(part, p, sizes).astype(f32)
    return total


def after_kernel(*refs):
    del refs


def after(value, *others):
    anywhere = pl.BlockSpec(memory_space=pl.ANY)
    return pl.pallas_call(
        after_kernel,
        out_shape=jax.ShapeDtypeStruct(value.shape, value.dtype),
        in_specs=[anywhere] * (1 + len(others)),
        out_specs=anywhere,
        input_output_aliases={0: 0},
        cost_estimate=cost(0),
    )(value, *others)


def assemble_kernel(rels, parts, me_ref, *refs):
    pieces, refs = refs[: len(rels)], refs[len(rels) :]
    outs, sems = refs[: len(parts)], refs[-1]
    me = me_ref[0]
    for k, (top, height, left, cols) in enumerate(parts):
        for piece, rel in zip(pieces, rels):
            for at, p in enumerate(rel):
                start = pl.multiple_of(lax.bitwise_xor(me, p) * height, height)
                pltpu.make_async_copy(
                    piece.at[at, pl.ds(top, height), pl.ds(left, cols)],
                    outs[k].at[pl.ds(start, height)],
                    sems.at[k],
                ).start()
    for k, out in enumerate(outs):
        pltpu.make_async_copy(out, out, sems.at[k]).wait()


def assemble(pieces, me, parts):
    rels = [q for _, q in pieces]
    count = sum(len(q) for q in rels)
    total = sum(h * c for _, h, _, c in parts)
    return pl.pallas_call(
        functools.partial(assemble_kernel, rels, parts),
        out_shape=[jax.ShapeDtypeStruct((count * h, c), bf16) for _, h, _, c in parts],
        in_specs=[pl.BlockSpec(memory_space=pltpu.SMEM)]
        + [pl.BlockSpec(memory_space=pl.ANY)] * len(pieces),
        scratch_shapes=[pltpu.SemaphoreType.DMA((len(parts),))],
        compiler_params=pltpu.CompilerParams(vmem_limit_bytes=vmem_most),
        cost_estimate=cost(1.5),
    )(me, *[v for v, _ in pieces])


def pack_small(parts, rows):
    def fill(blocks):
        size = max(v.shape[1] for v in blocks)
        same = [v for v in blocks if v.shape[1] < size]
        rest = [v for v in blocks if v.shape[1] == size]
        if same:
            joined = jnp.concatenate(same, axis=0)
            rest = [jnp.pad(joined, ((0, 0), (0, size - joined.shape[1])))] + rest
        block = jnp.concatenate(rest, axis=0)
        return jnp.pad(block, ((0, rows - block.shape[0]), (0, 128 - size)))

    flat = sorted((v for v in parts if v.ndim == 1), key=lambda v: v.shape[0])
    flat = fill([v[None] for v in flat])
    return jnp.concatenate([flat] + [fill([v]) for v in parts if v.ndim == 2], axis=1)


def unpack_small(whole, rows, parts):
    whole = whole.reshape(-1, rows, whole.shape[1]).astype(f32)
    found, left = [], 128
    flat = sorted((i for i, v in enumerate(parts) if v.ndim == 1), key=lambda i: parts[i].shape[0])
    for i, v in enumerate(parts):
        size = v.shape[-1]
        if v.ndim == 2:
            block = whole[:, : v.shape[0], left : left + size].swapaxes(0, 1)
            found.append(block.reshape(v.shape[0], -1))
            left += 128
        else:
            found.append(whole[:, flat.index(i), :size].reshape(-1))
    return found


def small_units(parts, rows, where, me):
    count = sum(len(q) for q in where)
    blocks = [
        v.reshape(count, -1)
        if v.ndim == 1
        else v.reshape(v.shape[0], count, -1).swapaxes(0, 1).reshape(count, -1)
        for v in parts
    ]
    flat = jnp.concatenate(blocks, axis=1)
    flat = jnp.pad(flat, ((0, 0), (0, rows * 128 - flat.shape[1]))).reshape(count, rows, 128)
    index = lax.bitwise_xor(jnp.asarray(where[0] + where[1], jnp.int32), me[0])
    mixed = jnp.take(flat, index, axis=0)
    return mixed[: count // 2], mixed[count // 2 :]


def small_parts(unit, parts, count):
    flat = unit.reshape(-1)
    found, at = [], 0
    for v in parts:
        size = v.size // count
        block = flat[at : at + size]
        found.append(block if v.ndim == 1 else block.reshape(v.shape[0], -1))
        at = at + size
    return found


def dot_t(a, b):
    return lax.dot_general(a, b, (((1,), (1,)), ((), ())), preferred_element_type=f32)


def dot_n(a, b):
    return lax.dot_general(a, b, (((1,), (0,)), ((), ())), preferred_element_type=f32)


def dot_tl(a, b):
    return lax.dot_general(a, b, (((0,), (0,)), ((), ())), preferred_element_type=f32)


def head_lanes(a, rows):
    lane = lax.broadcasted_iota(jnp.int32, (rows, 2 * HEAD), 1)
    return (lane >= HEAD) if a else (lane < HEAD)


def keep_head(x, a):
    return jnp.where(head_lanes(a, x.shape[0]), x, jnp.zeros_like(x))


def stack_heads(x):
    head = lax.broadcasted_iota(jnp.int32, x.shape, 1) // HEAD
    heads = x.shape[1] // HEAD
    return jnp.concatenate([jnp.where(head == a, x, jnp.zeros_like(x)) for a in range(heads)], axis=0)


def join_heads(x):
    heads = x.shape[0] // FEW
    head = lax.broadcasted_iota(jnp.int32, (FEW, x.shape[1]), 1) // HEAD
    found = x[:FEW]
    for a in range(1, heads):
        found = jnp.where(head == a, x[a * FEW : (a + 1) * FEW], found)
    return found


def few_rows(x):
    return jnp.concatenate([x, jnp.zeros_like(x)], axis=0)


def hide_few(s, first, last):
    row = lax.broadcasted_iota(jnp.int32, (EXTRA, s.shape[1]), 0)
    frame = lax.shift_right_logical(row, 1)
    seen = (frame >= first) & (frame <= last)
    count = s.shape[0] - EXTRA
    return jnp.concatenate([s[:count], jnp.where(seen, s[count:], masked_value)], axis=0)


def seen_rows(ref, lanes, lo, n):
    return jnp.concatenate([ref[pl.ds(lo, n * PATCH), lanes], ref[BODY:ROWS, lanes]], axis=0)


def seen_lanes(ref, a, lo, n):
    rows = slice(a * HEAD, (a + 1) * HEAD)
    return jnp.concatenate([ref[rows, pl.ds(lo, n * PATCH)], ref[rows, BODY:ROWS]], axis=1)


def pair_lanes(a):
    at = a // 2 * 2 * HEAD
    return slice(at, at + 2 * HEAD)


def attend_kernel(seen_ref, q_ref, k_ref, v_ref, hide_ref, out_ref, lse_ref, few_ref, vt):
    f = pl.program_id(1)
    heads = q_ref.shape[1] // HEAD

    @pl.when(f == 0)
    def _():
        vt[...] = v_ref[...].T
        qs = stack_heads(q_ref[BODY:ROWS, :].astype(f32)[:FEW]).astype(bf16)
        s = dot_t(k_ref[...], qs) + hide_ref[...]
        top = jnp.max(s, axis=0, keepdims=True)
        p = jnp.exp(s - top)
        total = jnp.sum(p, axis=0, keepdims=True)
        o = dot_tl((p / total).astype(bf16), v_ref[...])
        out_ref[BODY:ROWS, :] = few_rows(join_heads(o)).astype(bf16)
        few_ref[0] = top + jnp.log(total)

    row = pl.multiple_of(f * PATCH, PATCH)
    seen = seen_ref[f]

    @pl.when(seen == 0)
    def _():
        out_ref[pl.ds(row, PATCH), :] = v_ref[pl.ds(row, PATCH), :]
        lse_ref[0, :, pl.ds(row, PATCH)] = jnp.zeros((heads, PATCH), f32)

    for n in range(1, FRAMES + 1):

        @pl.when(seen == n)
        def _(n=n):
            first = f - (n - 1)
            lo = pl.multiple_of(first * PATCH, PATCH)

            def score(a):
                lanes = pair_lanes(a)
                q = keep_head(q_ref[pl.ds(row, PATCH), lanes], a % 2)
                return hide_few(dot_t(seen_rows(k_ref, lanes, lo, n), q), first, f)

            ahead = 4
            scores = [score(a) for a in range(ahead)]
            outs, sums = [], []
            for a in range(heads):
                s = scores[a]
                top = jnp.max(s, axis=0, keepdims=True)
                p = jnp.exp(s - top)
                total = jnp.sum(p, axis=0, keepdims=True)
                if a + ahead < heads:
                    scores.append(score(a + ahead))
                o = dot_n(seen_lanes(vt, a, lo, n), p.astype(bf16))
                outs.append(o / total)
                sums.append(top + jnp.log(total))
            out_ref[pl.ds(row, PATCH), :] = jnp.concatenate(outs, axis=0).T.astype(bf16)
            lse_ref[0, :, pl.ds(row, PATCH)] = jnp.concatenate(sums, axis=0)


PAIRS = 4


def attend(seen, qkv, hide, pair_lo, pair_hi, kept=None):
    width = qkv.shape[1] // 3
    lanes = 2 * HEAD * PAIRS
    groups = width // lanes
    at = pair_lo // PAIRS
    some = (pair_hi - pair_lo) // PAIRS
    kernel = attend_kernel
    more, alias = [], {}
    if kept is not None:
        more, alias = [kept], {5: 0}

        def kernel(seen_ref, q_ref, k_ref, v_ref, hide_ref, kept_ref, *refs):
            attend_kernel(seen_ref, q_ref, k_ref, v_ref, hide_ref, *refs)

    return pl.pallas_call(
        kernel,
        grid_spec=pltpu.PrefetchScalarGridSpec(
            num_scalar_prefetch=1,
            grid=(some, FRAMES),
            in_specs=[
                pl.BlockSpec((ROWS, lanes), lambda h, f, s: (0, at + h)),
                pl.BlockSpec((ROWS, lanes), lambda h, f, s: (0, at + groups + h)),
                pl.BlockSpec((ROWS, lanes), lambda h, f, s: (0, at + 2 * groups + h)),
                pl.BlockSpec((ROWS, 2 * PAIRS * FEW), lambda h, f, s: (0, 0)),
            ]
            + [pl.BlockSpec(memory_space=pl.ANY)] * len(more),
            out_specs=[
                pl.BlockSpec((ROWS, lanes), lambda h, f, s: (0, at + h)),
                pl.BlockSpec((1, 2 * PAIRS, BODY), lambda h, f, s: (h, 0, 0)),
                pl.BlockSpec((1, 1, 2 * PAIRS * FEW), lambda h, f, s: (h, 0, 0)),
            ],
            scratch_shapes=[pltpu.VMEM((lanes, ROWS), bf16)],
        ),
        out_shape=(
            jax.ShapeDtypeStruct((ROWS, width), bf16),
            jax.ShapeDtypeStruct((some, 2 * PAIRS, BODY), f32),
            jax.ShapeDtypeStruct((some, 1, 2 * PAIRS * FEW), f32),
        ),
        input_output_aliases=alias,
        compiler_params=pltpu.CompilerParams(vmem_limit_bytes=vmem_most),
        cost_estimate=cost(6.4 * some),
    )(seen, qkv, qkv, qkv, hide, *more)


def unturn(x, cosine, sine, partner):
    return x * cosine - dot_n(x.astype(bf16), partner) * sine


def attend_back_kernel(
    scale, seen_ref, q_ref, k_ref, v_ref, o_ref, g_ref, lse_ref, few_ref, hide_ref, cos_ref, sin_ref,
    part_ref, out_ref, kt, dq, dk, dv,
):
    f = pl.program_id(1)
    heads = q_ref.shape[1] // HEAD
    pairs = [slice(p * 2 * HEAD, (p + 1) * 2 * HEAD) for p in range(heads // 2)]
    ones = jnp.where(
        (lax.broadcasted_iota(jnp.int32, (8, 2 * HEAD), 1) >= HEAD).astype(jnp.int32)
        == lax.broadcasted_iota(jnp.int32, (8, 2 * HEAD), 0),
        1.0,
        0.0,
    ).astype(bf16)

    @pl.when(f == 0)
    def _():
        kt[...] = k_ref[...].T
        qs = stack_heads(q_ref[BODY:ROWS, :].astype(f32)[:FEW]).astype(bf16)
        gs = stack_heads(g_ref[BODY:ROWS, :].astype(f32)[:FEW]).astype(bf16)
        p = jnp.exp(dot_t(k_ref[...], qs) + hide_ref[...] - few_ref[0])
        gp = dot_t(v_ref[...], gs)
        delta = jnp.sum(gp * p, axis=0, keepdims=True)
        ds = (p * (gp - delta)).astype(bf16)
        dv[...] = dot_n(p.astype(bf16), gs)
        dk[...] = dot_n(ds, qs)
        dq[BODY:ROWS, :] = few_rows(join_heads(dot_tl(ds, k_ref[...])))

    row = pl.multiple_of(f * PATCH, PATCH)
    seen = seen_ref[f]

    @pl.when(seen == 0)
    def _():
        dv[pl.ds(row, PATCH), :] += g_ref[pl.ds(row, PATCH), :].astype(f32)
        dq[pl.ds(row, PATCH), :] = jnp.zeros((PATCH, heads * HEAD), f32)

    for n in range(1, FRAMES + 1):

        @pl.when(seen == n)
        def _(n=n):
            first = f - (n - 1)
            lo = pl.multiple_of(first * PATCH, PATCH)
            count = n * PATCH

            def start(a):
                lanes = pair_lanes(a)
                q = keep_head(q_ref[pl.ds(row, PATCH), lanes], a % 2)
                g = keep_head(g_ref[pl.ds(row, PATCH), lanes], a % 2)
                s = hide_few(dot_t(seen_rows(k_ref, lanes, lo, n), q), first, f)
                return q, g, s, dot_t(seen_rows(v_ref, lanes, lo, n), g)

            deltas = []
            for lanes in pairs:
                g = g_ref[pl.ds(row, PATCH), lanes].astype(f32)
                product = g * o_ref[pl.ds(row, PATCH), lanes].astype(f32)
                upper = product.astype(bf16)
                lower = (product - upper.astype(f32)).astype(bf16)
                deltas.append(dot_t(ones, upper) + dot_t(ones, lower))
            ahead = 4
            started = [start(a) for a in range(ahead)]
            back, add_k, add_v = [], None, None
            for a in range(heads):
                q, g, s, gp = started[a]
                p = jnp.exp(s - lse_ref[0, a : a + 1, pl.ds(row, PATCH)])
                ds = (p * (gp - deltas[a // 2][a % 2 : a % 2 + 1])).astype(bf16)
                p = p.astype(bf16)
                if a + ahead < heads:
                    started.append(start(a + ahead))
                more_v, more_k = dot_n(p, g), dot_n(ds, q)
                back.append(dot_n(seen_lanes(kt, a, lo, n), ds))
                if a % 2 == 0:
                    add_v, add_k = more_v, more_k
                else:
                    lanes = pairs[a // 2]
                    add_v, add_k = add_v + more_v, add_k + more_k
                    dk[pl.ds(lo, count), lanes] += add_k[:count]
                    dk[BODY:ROWS, lanes] += add_k[count:]
                    dv[pl.ds(lo, count), lanes] += add_v[:count]
                    dv[BODY:ROWS, lanes] += add_v[count:]
            dq[pl.ds(row, PATCH), :] = jnp.concatenate(back, axis=0).T

    @pl.when(f == FRAMES - 1)
    def _():
        partner = part_ref[...]
        for lanes in pairs:
            out_ref[0, :, lanes] = unturn(
                dq[:, lanes] * scale, cos_ref[...], sin_ref[...], partner
            ).astype(bf16)
            out_ref[1, :, lanes] = unturn(
                dk[:, lanes], cos_ref[...], sin_ref[...], partner
            ).astype(bf16)
        out_ref[2] = dv[...].astype(bf16)


def attend_back(
    seen, qkv, attended, grad, lse, few, hide, cosine, sine, partner, pair_lo, pair_hi, kept=None
):
    width = qkv.shape[1] // 3
    pair = 2 * HEAD
    lanes = pair * PAIRS
    groups = width // lanes
    at = pair_lo // PAIRS
    some = (pair_hi - pair_lo) // PAIRS
    inner = functools.partial(attend_back_kernel, 1.0 / math.sqrt(HEAD))
    kernel = inner
    more, alias = [], {}
    if kept is not None:
        more, alias = [kept], {12: 0}

        def kernel(*refs):
            inner(*refs[:12], *refs[13:])

    def whole(h, f, s):
        return (0, 0)

    return pl.pallas_call(
        kernel,
        grid_spec=pltpu.PrefetchScalarGridSpec(
            num_scalar_prefetch=1,
            grid=(some, FRAMES),
            in_specs=[
                pl.BlockSpec((ROWS, lanes), lambda h, f, s: (0, at + h)),
                pl.BlockSpec((ROWS, lanes), lambda h, f, s: (0, at + groups + h)),
                pl.BlockSpec((ROWS, lanes), lambda h, f, s: (0, at + 2 * groups + h)),
                pl.BlockSpec((ROWS, lanes), lambda h, f, s: (0, at + h)),
                pl.BlockSpec((ROWS, lanes), lambda h, f, s: (0, at + h)),
                pl.BlockSpec((1, 2 * PAIRS, BODY), lambda h, f, s: (h, 0, 0)),
                pl.BlockSpec((1, 1, 2 * PAIRS * FEW), lambda h, f, s: (h, 0, 0)),
                pl.BlockSpec((ROWS, 2 * PAIRS * FEW), whole),
                pl.BlockSpec((ROWS, pair), whole),
                pl.BlockSpec((ROWS, pair), whole),
                pl.BlockSpec((pair, pair), whole),
            ]
            + [pl.BlockSpec(memory_space=pl.ANY)] * len(more),
            out_specs=pl.BlockSpec((3, ROWS, lanes), lambda h, f, s: (0, 0, at + h)),
            scratch_shapes=[
                pltpu.VMEM((lanes, ROWS), bf16),
                pltpu.VMEM((ROWS, lanes), f32),
                pltpu.VMEM((ROWS, lanes), f32),
                pltpu.VMEM((ROWS, lanes), f32),
            ],
        ),
        out_shape=jax.ShapeDtypeStruct((3, ROWS, width), bf16),
        input_output_aliases=alias,
        compiler_params=pltpu.CompilerParams(vmem_limit_bytes=vmem_most),
        cost_estimate=cost(7.6 * some),
    )(seen, qkv, qkv, qkv, attended, grad, lse, few, hide, cosine, sine, partner, *more)


def project_kernel(scale, x_ref, w_ref, b_ref, cos_ref, sin_ref, part_ref, out_ref):
    j = pl.program_id(0)
    third = pl.num_programs(0) // 3
    lanes = 2 * HEAD
    wide = part_ref.shape[0]
    w = w_ref[...]
    mixed = dot_n(x_ref[...], w) + b_ref[...]

    @pl.when(j < 2 * third)
    def _():
        by = jnp.where(j < third, scale, 1.0)
        for left in range(0, w.shape[1], wide):
            x = mixed[:, left : left + wide]
            upper = x.astype(bf16)
            lower = (x - upper.astype(f32)).astype(bf16)
            other = dot_n(upper, part_ref[...]) + dot_n(lower, part_ref[...])
            for at in range(0, wide, lanes):
                here = mixed[:, left + at : left + at + lanes] * cos_ref[...]
                there = other[:, at : at + lanes] * sin_ref[...]
                out_ref[:, left + at : left + at + lanes] = ((here + there) * by).astype(bf16)

    @pl.when(j >= 2 * third)
    def _():
        out_ref[...] = mixed.astype(bf16)


def project(x, w, bias, cosine, sine, partner):
    rows, width = x.shape
    cols = 512
    lanes = 2 * HEAD
    wide = 2 * lanes
    zero = jnp.zeros_like(partner)
    partner = jnp.block([[partner, zero], [zero, partner]])

    def whole(j):
        return (0, 0)

    return pl.pallas_call(
        functools.partial(project_kernel, 1.0 / math.sqrt(HEAD)),
        grid=(w.shape[1] // cols,),
        in_specs=[
            pl.BlockSpec((rows, width), whole),
            pl.BlockSpec((width, cols), lambda j: (0, j)),
            pl.BlockSpec((1, cols), lambda j: (0, j)),
            pl.BlockSpec((rows, lanes), whole),
            pl.BlockSpec((rows, lanes), whole),
            pl.BlockSpec((wide, wide), whole),
        ],
        out_specs=pl.BlockSpec((rows, cols), lambda j: (0, j)),
        out_shape=jax.ShapeDtypeStruct((rows, w.shape[1]), bf16),
        compiler_params=pltpu.CompilerParams(vmem_limit_bytes=vmem_most),
        cost_estimate=cost(4),
    )(x, w, bias, cosine, sine, partner)


def turn_tables(frame_ids):
    frequency, which, sign = [], [], []
    for kind, part in enumerate(part_sizes):
        half = part // 2
        frequency += [10000.0 ** (-i / half) for i in range(half)] * 2
        which += [kind] * part
        sign += [-1.0] * half + [1.0] * half
    frequency = jnp.asarray(np.tile(np.array(frequency, np.float32), 2))
    which = np.tile(np.array(which), 2)
    sign = np.tile(np.array(sign, np.float32), 2)
    time = frame_ids[:: FRAME_ROWS].astype(f32)[:, None] * frequency
    place = np.arange(GRID, dtype=np.float32)[:, None] * frequency

    def table(of, empty):
        by_time, by_place = of(time), of(place)
        still = jnp.full((FRAMES, 2, which.size), empty, f32)
        patches = jnp.where(which == 1, by_place[:, None], by_place[None]).reshape(1, PATCH, -1)
        patches = jnp.where(which == 0, by_time[:, None], patches).reshape(BODY, -1)
        few = jnp.where(which == 0, by_time[:, None], still).reshape(FEW, -1)
        return jnp.concatenate([patches, few, jnp.zeros_like(few)], axis=0)

    return table(jnp.cos, 1.0), table(lambda v: jnp.sin(v) * sign, 0.0)


def partner_matrix():
    lanes = 2 * HEAD
    matrix = np.zeros((lanes, lanes), np.float32)
    for head in range(2):
        at = head * HEAD
        for part in part_sizes:
            for i in range(part // 2):
                matrix[at + i, at + i + part // 2] = 1.0
                matrix[at + i + part // 2, at + i] = 1.0
            at += part
    return jnp.asarray(matrix, bf16)


def seen_frames(offset_row):
    frame = jnp.arange(FRAMES, dtype=jnp.int32)
    start = jnp.where(frame >= offset_row[1], offset_row[1], 0)
    return jnp.where(frame < offset_row[2], frame - start + 1, 0)


def hidden_few(seen):
    frame_of = np.concatenate([np.repeat(np.arange(FRAMES), PATCH), np.repeat(np.arange(FRAMES), 2), np.full(EXTRA - FEW, FRAMES)])
    own = np.zeros((ROWS, FEW), bool)
    own[BODY + np.arange(FEW), np.arange(FEW)] = True
    frame = jnp.asarray(frame_of, jnp.int32)[:, None]
    query = jnp.arange(FEW, dtype=jnp.int32)[None, :] // 2
    count = jnp.repeat(seen, 2)[None, :]
    allowed = ((frame <= query) & (frame > query - count)) | jnp.asarray(own)
    return jnp.tile(jnp.where(allowed, 0.0, masked_value), (1, 2 * PAIRS))


def place(p, line, orders, core):
    own, other = relatives(line, orders, core)
    return (1, other.index(p)) if p in other else (0, own.index(p))


def find_piece(rels, p):
    for c, rel in enumerate(rels):
        if p in rel:
            return c, rel.index(p)
    raise ValueError(p)


def feed_kernel(
    rels, where, me_ref, x_ref, g_ref, bias_ref, shift_ref, mid_ref, up_ref, *refs
):
    pieces, refs = refs[: len(rels)], refs[len(rels) :]
    out_ref, gx_ref, gb_ref = refs[:3]
    grads = refs[3:5]
    wu, wd, su, sd, acc, xt, act, gup, in_sem, out_sem, mid_sem = refs[5:]
    count = sum(len(q) for q in rels)
    blocks = FEED_BLOCKS
    each = count // blocks
    shift = each.bit_length() - 1
    i = pl.program_id(0)
    me = me_ref[0]
    width = x_ref.shape[1]
    cols = wu.shape[2]
    rows = width // count
    part = cols // each
    hidden = blocks * cols
    stacks = part // rows
    slot = lax.rem(i, 2)

    def group(j):
        return lax.bitwise_xor(lax.shift_right_logical(me, shift), j)

    def fetch(j, to):
        at = pl.multiple_of(group(j) * cols, cols)
        pltpu.make_async_copy(up_ref.at[:, pl.ds(at, cols)], wu.at[to], in_sem.at[0, to]).start()
        for k in range(blocks):

            @pl.when(j == k)
            def _():
                for p in range(each):
                    c, n = find_piece(rels, (k << shift) | p)
                    start = pl.multiple_of(lax.bitwise_xor(me & (each - 1), p) * part, part)
                    for q in range(stacks):
                        pltpu.make_async_copy(
                            pieces[c].at[n, :, pl.ds(q * width, width)],
                            wd.at[to, pl.ds(start + q * rows, rows), :],
                            in_sem.at[1, to],
                        ).start()

    middle = pltpu.make_async_copy(mid_ref, acc, mid_sem)

    @pl.when(i == 0)
    def _():
        fetch(i, slot)
        middle.start()
        xt[...] = x_ref[...].T
        gx_ref[...] = jnp.zeros_like(gx_ref)

    @pl.when(i + 1 < blocks)
    def _():
        fetch(i + 1, 1 - slot)

    pltpu.make_async_copy(wu.at[slot], wu.at[slot], in_sem.at[0, slot]).wait()
    pltpu.make_async_copy(wd.at[slot], wd.at[slot], in_sem.at[1, slot]).wait()
    half = cols // 2
    low, high = slice(0, half), slice(half, cols)

    def curves(u, ga):
        e = jnp.exp2(u * u * (-0.5 * math.log2(math.e)))
        d = 1.0 + jnp.abs(u) * (0.3275911 * inv_sqrt_two)
        t = pl.reciprocal(d, approx=True)
        t = t * (2.0 - d * t)
        poly = t * (0.127414796 + t * (-0.142248368 + t * (0.7107068705 + t * (-0.7265760135 + t * 0.5307027145))))
        tail = poly * e
        phi = jnp.where(u >= 0.0, 1.0 - tail, tail)
        gu = ga * (phi + u * (e * inv_sqrt_tau))
        return (u * phi).astype(bf16), gu.astype(bf16), jnp.sum(gu, axis=0, keepdims=True)

    u0 = dot_n(x_ref[...], wu[slot, :, low]) + bias_ref[:, low]
    g0 = dot_t(g_ref[...], wd[slot, low, :])
    u1 = dot_n(x_ref[...], wu[slot, :, high]) + bias_ref[:, high]
    g1 = dot_t(g_ref[...], wd[slot, high, :])
    a, g, total = curves(u0, g0)
    act[:, low] = a
    gup[:, low] = g
    gb_ref[:, low] = total

    @pl.when(i >= 2)
    def _():
        pltpu.make_async_copy(su.at[slot], su.at[slot], out_sem.at[0, slot]).wait()
        pltpu.make_async_copy(sd.at[slot], sd.at[slot], out_sem.at[1, slot]).wait()

    @pl.when(i == 0)
    def _():
        middle.wait()

    sd[slot, low, :] = dot_tl(act[:, low], g_ref[...]).astype(bf16)
    su[slot, :, low] = dot_n(xt[...], gup[:, low]).astype(bf16)
    a, g, total = curves(u1, g1)
    act[:, high] = a
    gup[:, high] = g
    gb_ref[:, high] = total
    acc[...] += dot_n(act[...], wd[slot])
    gx_ref[...] += dot_t(gup[...], wu[slot])
    sd[slot, high, :] = dot_tl(act[:, high], g_ref[...]).astype(bf16)
    su[slot, :, high] = dot_n(xt[...], gup[:, high]).astype(bf16)
    at = pl.multiple_of(group(i) * cols, cols)
    for p in range(count):
        c, n = place(p, *where)
        start = pl.multiple_of(lax.bitwise_xor(me, p) * rows, rows)
        pltpu.make_async_copy(
            su.at[slot, pl.ds(start, rows), :],
            grads[c].at[n, :, pl.ds(at, cols)],
            out_sem.at[0, slot],
        ).start()
    for k in range(blocks):

        @pl.when(i == k)
        def _():
            for p in range(each):
                c, n = place((k << shift) | p, *where)
                start = pl.multiple_of(lax.bitwise_xor(me & (each - 1), p) * part, part)
                for q in range(stacks):
                    pltpu.make_async_copy(
                        sd.at[slot, pl.ds(start + q * rows, rows), :],
                        grads[c].at[n, :, pl.ds(hidden + q * width, width)],
                        out_sem.at[1, slot],
                    ).start()

    @pl.when(i == blocks - 1)
    def _():
        out_ref[...] = (acc[...] + shift_ref[...]).astype(bf16)
        for s in range(2):
            pltpu.make_async_copy(su.at[s], su.at[s], out_sem.at[0, s]).wait()
            pltpu.make_async_copy(sd.at[s], sd.at[s], out_sem.at[1, s]).wait()


FEED_BLOCKS = 4


def feed(x, grad, middle, bias, shift, up, pieces, line, orders, core, me):
    rels = [q for _, q in pieces]
    count = sum(len(q) for q in rels)
    tokens, width = x.shape
    hidden = bias.shape[1]
    cols = hidden // FEED_BLOCKS
    shift_by = (count // FEED_BLOCKS).bit_length() - 1

    def block(i, me_ref):
        return (0, lax.bitwise_xor(lax.shift_right_logical(me_ref[0], shift_by), i))

    def whole(i, me_ref):
        return (0, 0)

    once = pl.Buffered(1)
    anywhere = pl.BlockSpec(memory_space=pl.ANY)
    return pl.pallas_call(
        functools.partial(feed_kernel, rels, (line, orders, core)),
        grid_spec=pltpu.PrefetchScalarGridSpec(
            num_scalar_prefetch=1,
            grid=(FEED_BLOCKS,),
            in_specs=[
                pl.BlockSpec((tokens, width), whole, pipeline_mode=once),
                pl.BlockSpec((tokens, width), whole, pipeline_mode=once),
                pl.BlockSpec((1, cols), block),
                pl.BlockSpec((1, width), whole),
                anywhere,
                anywhere,
            ]
            + [anywhere] * len(pieces),
            out_specs=[
                pl.BlockSpec((tokens, width), whole, pipeline_mode=once),
                pl.BlockSpec((tokens, width), whole, pipeline_mode=once),
                pl.BlockSpec((1, cols), block),
            ]
            + [anywhere] * 2,
            scratch_shapes=[
                pltpu.VMEM((2, width, cols), bf16),
                pltpu.VMEM((2, cols, width), bf16),
                pltpu.VMEM((2, width, cols), bf16),
                pltpu.VMEM((2, cols, width), bf16),
                pltpu.VMEM((tokens, width), f32),
                pltpu.VMEM((width, tokens), bf16),
                pltpu.VMEM((tokens, cols), bf16),
                pltpu.VMEM((tokens, cols), bf16),
                pltpu.SemaphoreType.DMA((2, 2)),
                pltpu.SemaphoreType.DMA((2, 2)),
                pltpu.SemaphoreType.DMA,
            ],
        ),
        out_shape=[
            jax.ShapeDtypeStruct((tokens, width), bf16),
            jax.ShapeDtypeStruct((tokens, width), f32),
            jax.ShapeDtypeStruct((1, hidden), f32),
        ]
        + [jax.ShapeDtypeStruct((count // 2, width // count, 2 * hidden), bf16)] * 2,
        compiler_params=pltpu.CompilerParams(vmem_limit_bytes=vmem_most),
        cost_estimate=cost(20),
    )(me, x, grad, bias, shift, middle, up, *[v for v, _ in pieces])


def weight_kernel(where, left, count, me_ref, x_ref, g_ref, *refs):
    outs, (xt, staged, sem) = refs[-5:-3], refs[-3:]
    j = pl.program_id(0)
    me = me_ref[0]
    slot = lax.rem(j, 2)
    width, cols = staged.shape[1:]
    rows = width // count

    @pl.when(j == 0)
    def _():
        xt[...] = x_ref[...].T

    @pl.when(j >= 2)
    def _():
        pltpu.make_async_copy(staged.at[slot], staged.at[slot], sem.at[slot]).wait()

    staged[slot] = dot_n(xt[...], g_ref[...].reshape(g_ref.shape[-2:])).astype(bf16)
    at = pl.multiple_of(left + j * cols, cols)
    for out, rel in zip(outs, where):
        for n, p in enumerate(rel):
            start = pl.multiple_of(lax.bitwise_xor(me, p) * rows, rows)
            pltpu.make_async_copy(
                staged.at[slot, pl.ds(start, rows), :], out.at[n, :, pl.ds(at, cols)], sem.at[slot]
            ).start()

    @pl.when(j == pl.num_programs(0) - 1)
    def _():
        for s in range(2):
            pltpu.make_async_copy(staged.at[s], staged.at[s], sem.at[s]).wait()


def weight_grad(x, grad, where, left, total, me, into=()):
    tokens, width = x.shape
    count = sum(len(q) for q in where)
    cols = 512
    deep = grad.ndim == 3
    found = grad.shape[-1] * (grad.shape[0] if deep else 1)
    per = grad.shape[-1] // cols
    if deep:
        spec = pl.BlockSpec((1, tokens, cols), lambda j, m: (j // per, 0, j % per))
    else:
        spec = pl.BlockSpec((tokens, cols), lambda j, m: (0, j))
    anywhere = pl.BlockSpec(memory_space=pl.ANY)
    return pl.pallas_call(
        functools.partial(weight_kernel, where, left, count),
        grid_spec=pltpu.PrefetchScalarGridSpec(
            num_scalar_prefetch=1,
            grid=(found // cols,),
            in_specs=[pl.BlockSpec((tokens, width), lambda j, m: (0, 0)), spec]
            + [anywhere] * len(into),
            out_specs=[anywhere] * 2,
            scratch_shapes=[
                pltpu.VMEM((width, tokens), bf16),
                pltpu.VMEM((2, width, cols), bf16),
                pltpu.SemaphoreType.DMA((2,)),
            ],
        ),
        out_shape=[jax.ShapeDtypeStruct((count // 2, width // count, total), bf16)] * 2,
        input_output_aliases={3 + i: i for i in range(len(into))},
        compiler_params=pltpu.CompilerParams(vmem_limit_bytes=vmem_most),
        cost_estimate=cost(0.5 * found / 512),
    )(me, x, grad, *into)


def sort_kernel(x_ref, g_ref, x_out, g_out, sum_ref, wide):
    for source, target in ((x_ref, x_out), (g_ref, g_out)):
        wide[...] = source[...].astype(f32)
        for f in range(FRAMES):
            at = f * FRAME_ROWS + 2
            target[f * PATCH : (f + 1) * PATCH, :] = wide[at : at + PATCH, :].astype(bf16)
        few = [wide[f * FRAME_ROWS : f * FRAME_ROWS + 2, :] for f in range(FRAMES)]
        few = jnp.concatenate(few + [jnp.zeros((EXTRA - FEW, wide.shape[1]), f32)], axis=0)
        target[BODY:ROWS, :] = few.astype(bf16)
    sum_ref[...] = jnp.sum(wide[...], axis=0, keepdims=True)


def sort_rows(x, grad):
    tokens, width = x.shape
    return pl.pallas_call(
        sort_kernel,
        out_shape=[jax.ShapeDtypeStruct((ROWS, width), bf16)] * 2
        + [jax.ShapeDtypeStruct((1, width), f32)],
        scratch_shapes=[pltpu.VMEM((tokens, width), f32)],
        compiler_params=pltpu.CompilerParams(vmem_limit_bytes=vmem_most),
        cost_estimate=cost(1),
    )(x, grad)


def unsort_kernel(x_ref, out_ref, *scratch):
    wide = scratch[0] if scratch else out_ref
    for f in range(FRAMES):
        at = f * FRAME_ROWS
        wide[at + 2 : at + FRAME_ROWS, :] = x_ref[f * PATCH : (f + 1) * PATCH, :].astype(f32)
    few = x_ref[BODY:ROWS, :].astype(f32)
    for f in range(FRAMES):
        wide[f * FRAME_ROWS : f * FRAME_ROWS + 2, :] = few[2 * f : 2 * f + 2]
    if scratch:
        out_ref[...] = wide[...].astype(out_ref.dtype)


def unsort_rows(x):
    tokens, width = FRAMES * FRAME_ROWS, x.shape[1]
    return pl.pallas_call(
        unsort_kernel,
        out_shape=jax.ShapeDtypeStruct((tokens, width), x.dtype),
        scratch_shapes=[] if x.dtype == f32 else [pltpu.VMEM((tokens, width), f32)],
        compiler_params=pltpu.CompilerParams(vmem_limit_bytes=vmem_most),
        cost_estimate=cost(1),
    )(x)


def last_kernel(g_ref, w_ref, x_ref, mid_ref, gain_ref, out_ref, gain_out, bias_out, sum_ref, acc):
    i = pl.program_id(0)
    g = g_ref[0]
    more = dot_t(g, w_ref[...])

    @pl.when(i == 0)
    def _():
        acc[...] = more

    @pl.when(i > 0)
    def _():
        acc[...] += more

    sum_ref[0] = jnp.sum(g.astype(f32), axis=0, keepdims=True)

    @pl.when(i == pl.num_programs(0) - 1)
    def _():
        gain = gain_ref[...]
        gain_sum, bias_sum = 0.0, 0.0
        spans = [(f * PATCH, PATCH) for f in range(FRAMES)] + [(BODY, EXTRA)]
        for at, size in spans:
            rows = slice(at, at + size)
            x = x_ref[rows, :].astype(f32)
            center = x - jnp.mean(x, axis=-1, keepdims=True)
            inverse = lax.rsqrt(jnp.mean(center * center, axis=-1, keepdims=True) + eps_norm)
            unit = center * inverse
            grad = acc[rows, :]
            gain_sum += jnp.sum(grad * unit, axis=0, keepdims=True)
            bias_sum += jnp.sum(grad, axis=0, keepdims=True)
            scaled = grad * gain
            mean_grad = jnp.mean(scaled, axis=-1, keepdims=True)
            mean_cross = jnp.mean(scaled * unit, axis=-1, keepdims=True)
            found = mid_ref[rows, :] + inverse * (scaled - mean_grad - unit * mean_cross)
            if size == PATCH:
                start = at // PATCH * FRAME_ROWS + 2
                out_ref[start : start + PATCH, :] = found
            else:
                for f in range(FRAMES):
                    out_ref[f * FRAME_ROWS : f * FRAME_ROWS + 2, :] = found[2 * f : 2 * f + 2]
        gain_out[...] = gain_sum
        bias_out[...] = bias_sum


def last_step(grad_mixed, w, x, middle, gain):
    parts, rows, width = grad_mixed.shape

    def whole(i):
        return (0, 0)

    once = pl.Buffered(1)
    return pl.pallas_call(
        last_kernel,
        grid=(parts,),
        in_specs=[
            pl.BlockSpec((1, rows, width), lambda i: (i, 0, 0)),
            pl.BlockSpec((width, width), lambda i: (0, i)),
            pl.BlockSpec((rows, width), whole, pipeline_mode=once),
            pl.BlockSpec((rows, width), whole, pipeline_mode=once),
            pl.BlockSpec((1, width), whole),
        ],
        out_specs=[
            pl.BlockSpec((FRAMES * FRAME_ROWS, width), whole, pipeline_mode=once),
            pl.BlockSpec((1, width), whole),
            pl.BlockSpec((1, width), whole),
            pl.BlockSpec((1, 1, width), lambda i: (i, 0, 0)),
        ],
        out_shape=[
            jax.ShapeDtypeStruct((FRAMES * FRAME_ROWS, width), f32),
            jax.ShapeDtypeStruct((1, width), f32),
            jax.ShapeDtypeStruct((1, width), f32),
            jax.ShapeDtypeStruct((parts, 1, width), f32),
        ],
        scratch_shapes=[pltpu.VMEM((rows, width), f32)],
        compiler_params=pltpu.CompilerParams(vmem_limit_bytes=vmem_most),
        cost_estimate=cost(5),
    )(grad_mixed, w, x, middle, gain)


def normalize(values, gain, bias_add):
    center = values - jnp.mean(values, axis=-1, keepdims=True)
    scale_inv = lax.rsqrt(jnp.mean(center * center, axis=-1, keepdims=True) + eps_norm)
    unit_rows = center * scale_inv
    return (unit_rows * gain + bias_add, unit_rows, scale_inv)


def norm_back(grad_out, unit_rows, scale_inv, gain):
    scaled = grad_out * gain
    mean_grad = jnp.mean(scaled, axis=-1, keepdims=True)
    mean_cross = jnp.mean(scaled * unit_rows, axis=-1, keepdims=True)
    return scale_inv * (scaled - mean_grad - unit_rows * mean_cross)


def gather_joined(groups, orders, core, sizes):
    found = []
    for pieces, order in zip(groups, orders):
        for bit in order[:-1]:
            pieces = pieces + moved(pieces, bit, sizes)
        arrays, rels = zip(*pieces)
        pieces = [(jnp.concatenate(arrays, axis=0), sum(rels, []))]
        found += pieces + moved(pieces, order[-1], sizes)
    return found + moved(found, core, sizes)


def gather_rest(groups, orders, core, sizes):
    found = []
    for pieces, order in zip(groups, orders):
        for bit in order:
            pieces = pieces + moved(pieces, bit, sizes)
        found += pieces
    return found + moved(found, core, sizes)


def body(
    sizes,
    tokens,
    frame_ids,
    pad_mask,
    episode_offsets,
    ln1_gain,
    ln1_bias,
    w_qkv,
    b_qkv,
    w_out,
    b_out,
    ln2_gain,
    ln2_bias,
    w_up,
    b_up,
    w_down,
    b_down,
    cotangent,
):
    width = tokens.shape[1]
    count = sizes[0] * sizes[1]
    me = (lax.axis_index("dp") * sizes[1] + lax.axis_index("fsdp")).astype(jnp.int32)[None]
    core, line, orders = bit_orders(sizes)
    where = relatives(line, orders, core)
    out_matrix = lax.all_gather(w_out, ("dp", "fsdp"), axis=0, tiled=True)
    up_matrix = lax.all_gather(w_up, ("dp", "fsdp"), axis=0, tiled=True)
    smalls = [ln1_gain, ln1_bias, b_qkv, b_out, ln2_gain, ln2_bias, b_up, b_down]
    rows, third = w_qkv.shape
    first_unit = jnp.concatenate([w_qkv, pack_small(smalls, rows)], axis=1)
    firsts = gather_line(first_unit, line, sizes)
    tokens_in, cot, grad_b_down_local = sort_rows(tokens, cotangent)
    first = gather_joined(firsts, orders, core, sizes)
    seen = seen_frames(episode_offsets[0])
    hide = hidden_few(seen)
    cosine, sine = turn_tables(frame_ids)
    partner = partner_matrix()
    values_in = tokens_in.astype(f32)
    qkv_matrix, whole_small = assemble(
        first, me, [(0, rows, 0, third), (0, rows, third, first_unit.shape[1] - third)]
    )
    gain_one, bias_one, qkv_rows, *_ = unpack_small(whole_small, rows, smalls)
    stacked = [w_down[at : at + rows] for at in range(0, w_down.shape[0], rows)]
    second_unit = after(jnp.concatenate(stacked, axis=1), first[0][0], first[2][0])
    seconds = gather_line(second_unit, line, sizes)
    normed_one, unit_one, inv_one = normalize(values_in, gain_one, bias_one)
    normed_one = normed_one.astype(bf16)
    qkv = project(normed_one, qkv_matrix, qkv_rows.reshape(1, 3 * width), cosine, sine, partner)
    pairs = width // (2 * HEAD)
    seconds = [after_pieces(pieces, qkv_matrix) for pieces in seconds]
    seconds = [
        [pieces, moved(pieces, order[0], sizes) + moved(pieces, order[1], sizes)]
        for pieces, order in zip(seconds, orders)
    ]
    attended, lse_a, few_a = attend(seen, qkv, hide, 0, pairs // 2)
    seconds = [[near, after_pieces(far, attended)] for near, far in seconds]
    found = []
    for (near, far), order in zip(seconds, orders):
        pieces = near + far + moved(far[:1], order[1], sizes)
        for bit in order[2:]:
            pieces = pieces + moved(pieces, bit, sizes)
        found.append(pieces)
    attended, lse_b, few_b = attend(seen, qkv, hide, pairs // 2, pairs, attended)
    second = []
    for pieces in found:
        arrays, rels = zip(*pieces)
        pieces = [(after(jnp.concatenate(arrays, axis=0), attended), sum(rels, []))]
        second += pieces + moved(pieces, core, sizes)
    whole_small = after(whole_small, attended)
    *_, out_bias, gain_two, bias_two, up_bias, down_bias = unpack_small(whole_small, rows, smalls)
    hidden = w_up.shape[1]
    middle = values_in + jnp.dot(attended, out_matrix, preferred_element_type=f32) + out_bias
    normed_two, unit_two, inv_two = normalize(middle, gain_two, bias_two)
    normed_two = normed_two.astype(bf16)
    result, grad_normed_two, grad_b_up_local, feed_own, feed_other = feed(
        normed_two,
        cot,
        middle,
        up_bias[None],
        down_bias[None],
        up_matrix,
        second,
        line,
        orders,
        core,
        me,
    )
    feed_taken = swap(feed_other, 1 << core, sizes)
    grad_gain_two = jnp.sum(grad_normed_two * unit_two, axis=0)
    grad_bias_two = jnp.sum(grad_normed_two, axis=0)
    grad_middle = cot.astype(f32) + norm_back(grad_normed_two, unit_two, inv_two, gain_two)
    grad_branch = grad_middle.astype(bf16)
    grad_b_out_local = jnp.sum(grad_branch.astype(f32), axis=0)
    grad_attended = dot_t(grad_branch, out_matrix).astype(bf16)
    feed_own = after(feed_own, feed_taken, grad_attended)
    feed_sums = reduce_start(feed_own, feed_taken, orders, sizes)
    grad_attended = after(grad_attended, *[v for group in feed_sums for v in group[:1] + group[2:]])
    feed_sums = [group[:2] for group in feed_sums]
    back = (hide, cosine, sine, partner)
    grad_mixed = attend_back(
        seen, qkv, attended, grad_attended, lse_a, few_a, *back, 0, pairs // 2
    )
    grad_mixed = attend_back(
        seen, qkv, attended, grad_attended, lse_b, few_b, *back, pairs // 2, pairs, grad_mixed
    )
    steps = len(orders[0])
    for step in range(1, steps):
        feed_sums = together(feed_sums, grad_mixed)
        feed_sums = reduce_next(feed_sums, orders, step, sizes)
        grad_mixed = after(grad_mixed, *[v for group in feed_sums for v in group[:1] + group[2:]])
        feed_sums = [group[:2] for group in feed_sums]
    grads = weight_grad(normed_one, grad_mixed, where, 0, third + width, me)
    own, other = weight_grad(attended, grad_branch, where, third, third + width, me, grads)
    taken = swap(other, 1 << core, sizes)
    feed_parts = line_parts(together(feed_sums))
    feed_parts = feed_parts[:1] + [v.astype(bf16) for v in feed_parts[1:]]
    own = after(own, *feed_parts[1:])
    sums = reduce_start(own, taken, orders, sizes)
    going = [v for group in sums for v in group[:1] + group[2:]]
    sums = [group[:2] for group in sums]
    grad_mixed = after(grad_mixed, *going)
    grad_tokens, grad_gain_one, grad_bias_one, grad_b_qkv_local = last_step(
        grad_mixed, qkv_matrix, tokens_in, grad_middle, gain_one[None]
    )
    vectors = [
        grad_gain_one[0],
        grad_bias_one[0],
        grad_b_qkv_local[:, 0],
        grad_b_out_local,
        grad_gain_two,
        grad_bias_two,
        grad_b_up_local[0],
        grad_b_down_local[0],
    ]
    small_own, small_other = small_units(vectors, rows, where, me)
    small = jnp.concatenate([small_own, small_other], axis=2).astype(bf16)
    half = small.shape[0] // 2
    joined = []
    for (kept, came), at, order in zip(sums, (0, half), orders):
        here = small[at : at + half // 2]
        there = swap(small[at + half // 2 : at + half], 1 << order[-1], sizes)
        joined.append(
            (jnp.concatenate([kept, here], axis=2), jnp.concatenate([came, there], axis=2))
        )
    sums = joined
    for step in range(1, steps):
        sums = [group[:2] for group in reduce_next(sums, orders, step, sizes)]
    parts = line_parts(sums)
    parts = parts[:1] + [v.astype(bf16) for v in parts[1:]]
    feed_parts[0] = after(feed_parts[0], *parts[1:])
    output = unsort_rows(after(result, *parts[1:]))
    parts[0] = after(parts[0], output)
    feed_sum = reduce_line(feed_parts, line, sizes)
    sum_one = reduce_line(parts, line, sizes)
    small = sum_one[:, third + width :]
    small = small[:, :128] + swap(small[:, 128:], 1 << core, sizes)
    small = small_parts(small, vectors, count)
    sum_down = feed_sum[:, hidden:].reshape(rows, -1, width).swapaxes(0, 1).reshape(-1, width)
    return (
        output,
        grad_tokens,
        small[0],
        small[1],
        sum_one[:, :third],
        small[2],
        sum_one[:, third : third + width],
        small[3],
        small[4],
        small[5],
        feed_sum[:, :hidden],
        small[6],
        sum_down,
        small[7],
    )


def solution(mesh):
    placed = (
        P(("dp", "fsdp"), None),
        P(("dp", "fsdp")),
        P(("dp", "fsdp")),
        P(("dp", "fsdp"), None),
        P(("dp", "fsdp")),
        P(("dp", "fsdp")),
        P(("dp", "fsdp"), None),
        P(None, ("dp", "fsdp")),
        P(("dp", "fsdp"), None),
        P(("dp", "fsdp")),
        P(("dp", "fsdp")),
        P(("dp", "fsdp")),
        P(("dp", "fsdp"), None),
        P(("dp", "fsdp")),
        P(("dp", "fsdp"), None),
        P(("dp", "fsdp")),
        P(("dp", "fsdp"), None),
    )
    sizes = (mesh.shape["dp"], mesh.shape["fsdp"])
    return jax.shard_map(
        functools.partial(body, sizes),
        mesh=mesh,
        in_specs=placed,
        out_specs=(
            P(("dp", "fsdp"), None),
            P(("dp", "fsdp"), None),
            P(("dp", "fsdp")),
            P(("dp", "fsdp")),
            P(("dp", "fsdp"), None),
            P(None, ("dp", "fsdp")),
            P(("dp", "fsdp"), None),
            P(("dp", "fsdp")),
            P(("dp", "fsdp")),
            P(("dp", "fsdp")),
            P(("dp", "fsdp"), None),
            P(("dp", "fsdp")),
            P(("dp", "fsdp"), None),
            P(("dp", "fsdp")),
        ),
        check_vma=False,
    )
```

```python
import functools
import math

import jax
import jax.numpy as jnp
import numpy as np
from jax import lax
from jax.experimental import pallas as pl
from jax.experimental.pallas import tpu as pltpu
from jax.sharding import PartitionSpec as P

HEAD = 64
GRID = 16
FRAME_ROWS = 258
FRAMES = 4
PATCH = GRID * GRID
EXTRA = 16
FEW = 8
BODY = FRAMES * PATCH
ROWS = BODY + EXTRA
eps_norm = 1e-06
part_sizes = (24, 20, 20)
masked_value = -1e30
inv_sqrt_two = 1.0 / math.sqrt(2.0)
inv_sqrt_tau = 1.0 / math.sqrt(2.0 * math.pi)
f32 = jnp.float32
bf16 = jnp.bfloat16
vmem_most = 60 * 1024 * 1024


def cost(micros):
    return pl.CostEstimate(flops=int(micros * 1e9), bytes_accessed=0, transcendentals=0)


def log2(n):
    return n.bit_length() - 1


def swap(value, mask, sizes):
    count = sizes[0] * sizes[1]
    return lax.ppermute(value, ("dp", "fsdp"), [(i, i ^ mask) for i in range(count)])


def bit_orders(sizes):
    inner, outer = log2(sizes[1]), log2(sizes[0])
    line = list(range(1, inner))
    cross = [0]
    other = list(range(inner + 1, inner + outer))
    return inner, line, (cross + other, other + cross)


def spread(bits):
    rel = [0]
    for bit in bits:
        rel = rel + [p | (1 << bit) for p in rel]
    return rel


def gather_line(shard, line, sizes):
    rel = spread(line)
    held = [shard[None]] + [swap(shard[None], p, sizes) for p in rel[1:]]
    half = len(rel) // 2
    return [
        [(jnp.concatenate(held[at : at + half], axis=0), rel[at : at + half])]
        for at in (0, half)
    ]


def gather_doubling(shard, line, sizes):
    held, rel = shard[None], [0]
    for bit in line[:-1]:
        held = jnp.concatenate([held, swap(held, 1 << bit, sizes)], axis=0)
        rel = rel + [p | (1 << bit) for p in rel]
    return [[(held, rel)], moved([(held, rel)], line[-1], sizes)]


def moved(pieces, bit, sizes):
    return [(swap(v, 1 << bit, sizes), [p | (1 << bit) for p in q]) for v, q in pieces]


def relatives(line, orders, core):
    low, top = line[:-1], 1 << line[-1]
    rel = spread(low + orders[0]) + [p | top for p in spread(low + orders[1])]
    return rel, [p | (1 << core) for p in rel]


def reduce_start(own, taken, orders, sizes):
    half = own.shape[0] // 2
    return [
        reduce_step(own[at : at + half], taken[at : at + half], 1 << order[-1], sizes)
        for at, order in zip((0, half), orders)
    ]


def reduce_step(kept, taken, mask, sizes):
    kind = kept.dtype
    half = kept.shape[0] // 2
    sent = (kept[half:].astype(f32) + taken[half:].astype(f32)).astype(kind)
    held = (kept[:half].astype(f32) + taken[:half].astype(f32)).astype(kind)
    return held, swap(sent, mask, sizes), sent


def reduce_next(groups, orders, step, sizes):
    return [
        reduce_step(*group, 1 << order[-1 - step], sizes) for group, order in zip(groups, orders)
    ]


def together(groups, *others):
    came = [group[1] for group in groups]
    return [(after(kept, *came, *others), taken) for kept, taken in groups]


def after_pieces(pieces, *others):
    return [(after(v, *others), q) for v, q in pieces]


def line_parts(groups):
    return [
        kept[n].astype(f32) + taken[n].astype(f32)
        for kept, taken in groups
        for n in range(kept.shape[0])
    ]


def reduce_line(parts, line, sizes):
    total = parts[0]
    for part, p in zip(parts[1:], spread(line)[1:]):
        total = total + swap(part, p, sizes).astype(f32)
    return total


def after_kernel(*refs):
    del refs


def after(value, *others):
    anywhere = pl.BlockSpec(memory_space=pl.ANY)
    return pl.pallas_call(
        after_kernel,
        out_shape=jax.ShapeDtypeStruct(value.shape, value.dtype),
        in_specs=[anywhere] * (1 + len(others)),
        out_specs=anywhere,
        input_output_aliases={0: 0},
        cost_estimate=cost(0),
    )(value, *others)


def assemble_kernel(rels, parts, me_ref, *refs):
    pieces, refs = refs[: len(rels)], refs[len(rels) :]
    outs, sems = refs[: len(parts)], refs[-1]
    me = me_ref[0]
    for k, (top, height, left, cols) in enumerate(parts):
        for piece, rel in zip(pieces, rels):
            for at, p in enumerate(rel):
                start = pl.multiple_of(lax.bitwise_xor(me, p) * height, height)
                pltpu.make_async_copy(
                    piece.at[at, pl.ds(top, height), pl.ds(left, cols)],
                    outs[k].at[pl.ds(start, height)],
                    sems.at[k],
                ).start()
    for k, out in enumerate(outs):
        pltpu.make_async_copy(out, out, sems.at[k]).wait()


def assemble(pieces, me, parts):
    rels = [q for _, q in pieces]
    count = sum(len(q) for q in rels)
    total = sum(h * c for _, h, _, c in parts)
    return pl.pallas_call(
        functools.partial(assemble_kernel, rels, parts),
        out_shape=[jax.ShapeDtypeStruct((count * h, c), bf16) for _, h, _, c in parts],
        in_specs=[pl.BlockSpec(memory_space=pltpu.SMEM)]
        + [pl.BlockSpec(memory_space=pl.ANY)] * len(pieces),
        scratch_shapes=[pltpu.SemaphoreType.DMA((len(parts),))],
        compiler_params=pltpu.CompilerParams(vmem_limit_bytes=vmem_most),
        cost_estimate=cost(1.5),
    )(me, *[v for v, _ in pieces])


def pack_small(parts, rows):
    def fill(blocks):
        size = max(v.shape[1] for v in blocks)
        same = [v for v in blocks if v.shape[1] < size]
        rest = [v for v in blocks if v.shape[1] == size]
        if same:
            joined = jnp.concatenate(same, axis=0)
            rest = [jnp.pad(joined, ((0, 0), (0, size - joined.shape[1])))] + rest
        block = jnp.concatenate(rest, axis=0)
        return jnp.pad(block, ((0, rows - block.shape[0]), (0, 128 - size)))

    flat = sorted((v for v in parts if v.ndim == 1), key=lambda v: v.shape[0])
    flat = fill([v[None] for v in flat])
    return jnp.concatenate([flat] + [fill([v]) for v in parts if v.ndim == 2], axis=1)


def unpack_small(whole, rows, parts):
    whole = whole.reshape(-1, rows, whole.shape[1]).astype(f32)
    found, left = [], 128
    flat = sorted((i for i, v in enumerate(parts) if v.ndim == 1), key=lambda i: parts[i].shape[0])
    for i, v in enumerate(parts):
        size = v.shape[-1]
        if v.ndim == 2:
            block = whole[:, : v.shape[0], left : left + size].swapaxes(0, 1)
            found.append(block.reshape(v.shape[0], -1))
            left += 128
        else:
            found.append(whole[:, flat.index(i), :size].reshape(-1))
    return found


def small_units(parts, rows, where, me):
    count = sum(len(q) for q in where)
    blocks = [
        v.reshape(count, -1)
        if v.ndim == 1
        else v.reshape(v.shape[0], count, -1).swapaxes(0, 1).reshape(count, -1)
        for v in parts
    ]
    flat = jnp.concatenate(blocks, axis=1)
    flat = jnp.pad(flat, ((0, 0), (0, rows * 128 - flat.shape[1]))).reshape(count, rows, 128)
    index = lax.bitwise_xor(jnp.asarray(where[0] + where[1], jnp.int32), me[0])
    mixed = jnp.take(flat, index, axis=0)
    return mixed[: count // 2], mixed[count // 2 :]


def small_parts(unit, parts, count):
    flat = unit.reshape(-1)
    found, at = [], 0
    for v in parts:
        size = v.size // count
        block = flat[at : at + size]
        found.append(block if v.ndim == 1 else block.reshape(v.shape[0], -1))
        at = at + size
    return found


def dot_t(a, b):
    return lax.dot_general(a, b, (((1,), (1,)), ((), ())), preferred_element_type=f32)


def dot_n(a, b):
    return lax.dot_general(a, b, (((1,), (0,)), ((), ())), preferred_element_type=f32)


def dot_tl(a, b):
    return lax.dot_general(a, b, (((0,), (0,)), ((), ())), preferred_element_type=f32)


def head_lanes(a, rows):
    lane = lax.broadcasted_iota(jnp.int32, (rows, 2 * HEAD), 1)
    return (lane >= HEAD) if a else (lane < HEAD)


def keep_head(x, a):
    return jnp.where(head_lanes(a, x.shape[0]), x, jnp.zeros_like(x))


def stack_heads(x):
    head = lax.broadcasted_iota(jnp.int32, x.shape, 1) // HEAD
    heads = x.shape[1] // HEAD
    return jnp.concatenate([jnp.where(head == a, x, jnp.zeros_like(x)) for a in range(heads)], axis=0)


def join_heads(x):
    heads = x.shape[0] // FEW
    head = lax.broadcasted_iota(jnp.int32, (FEW, x.shape[1]), 1) // HEAD
    found = x[:FEW]
    for a in range(1, heads):
        found = jnp.where(head == a, x[a * FEW : (a + 1) * FEW], found)
    return found


def few_rows(x):
    return jnp.concatenate([x, jnp.zeros_like(x)], axis=0)


def hide_few(s, first, last):
    row = lax.broadcasted_iota(jnp.int32, (EXTRA, s.shape[1]), 0)
    frame = lax.shift_right_logical(row, 1)
    seen = (frame >= first) & (frame <= last)
    count = s.shape[0] - EXTRA
    return jnp.concatenate([s[:count], jnp.where(seen, s[count:], masked_value)], axis=0)


def seen_rows(ref, lanes, lo, n):
    return jnp.concatenate([ref[pl.ds(lo, n * PATCH), lanes], ref[BODY:ROWS, lanes]], axis=0)


def seen_lanes(ref, a, lo, n):
    rows = slice(a * HEAD, (a + 1) * HEAD)
    return jnp.concatenate([ref[rows, pl.ds(lo, n * PATCH)], ref[rows, BODY:ROWS]], axis=1)


def pair_lanes(a):
    at = a // 2 * 2 * HEAD
    return slice(at, at + 2 * HEAD)


def attend_kernel(seen_ref, q_ref, k_ref, v_ref, hide_ref, out_ref, lse_ref, few_ref, vt):
    f = pl.program_id(1)
    heads = q_ref.shape[1] // HEAD

    @pl.when(f == 0)
    def _():
        vt[...] = v_ref[...].T
        qs = stack_heads(q_ref[BODY:ROWS, :].astype(f32)[:FEW]).astype(bf16)
        s = dot_t(k_ref[...], qs) + hide_ref[...]
        top = jnp.max(s, axis=0, keepdims=True)
        p = jnp.exp(s - top)
        total = jnp.sum(p, axis=0, keepdims=True)
        o = dot_tl((p / total).astype(bf16), v_ref[...])
        out_ref[BODY:ROWS, :] = few_rows(join_heads(o)).astype(bf16)
        few_ref[0] = top + jnp.log(total)

    row = pl.multiple_of(f * PATCH, PATCH)
    seen = seen_ref[f]

    @pl.when(seen == 0)
    def _():
        out_ref[pl.ds(row, PATCH), :] = v_ref[pl.ds(row, PATCH), :]
        lse_ref[0, :, pl.ds(row, PATCH)] = jnp.zeros((heads, PATCH), f32)

    for n in range(1, FRAMES + 1):

        @pl.when(seen == n)
        def _(n=n):
            first = f - (n - 1)
            lo = pl.multiple_of(first * PATCH, PATCH)

            def score(a):
                lanes = pair_lanes(a)
                q = keep_head(q_ref[pl.ds(row, PATCH), lanes], a % 2)
                return hide_few(dot_t(seen_rows(k_ref, lanes, lo, n), q), first, f)

            ahead = 4
            scores = [score(a) for a in range(ahead)]
            outs, sums = [], []
            for a in range(heads):
                s = scores[a]
                top = jnp.max(s, axis=0, keepdims=True)
                p = jnp.exp(s - top)
                total = jnp.sum(p, axis=0, keepdims=True)
                if a + ahead < heads:
                    scores.append(score(a + ahead))
                o = dot_n(seen_lanes(vt, a, lo, n), p.astype(bf16))
                outs.append(o / total)
                sums.append(top + jnp.log(total))
            out_ref[pl.ds(row, PATCH), :] = jnp.concatenate(outs, axis=0).T.astype(bf16)
            lse_ref[0, :, pl.ds(row, PATCH)] = jnp.concatenate(sums, axis=0)


PAIRS = 4


def attend(seen, qkv, hide, pair_lo, pair_hi, kept=None):
    width = qkv.shape[1] // 3
    lanes = 2 * HEAD * PAIRS
    groups = width // lanes
    at = pair_lo // PAIRS
    some = (pair_hi - pair_lo) // PAIRS
    kernel = attend_kernel
    more, alias = [], {}
    if kept is not None:
        more, alias = [kept], {5: 0}

        def kernel(seen_ref, q_ref, k_ref, v_ref, hide_ref, kept_ref, *refs):
            attend_kernel(seen_ref, q_ref, k_ref, v_ref, hide_ref, *refs)

    return pl.pallas_call(
        kernel,
        grid_spec=pltpu.PrefetchScalarGridSpec(
            num_scalar_prefetch=1,
            grid=(some, FRAMES),
            in_specs=[
                pl.BlockSpec((ROWS, lanes), lambda h, f, s: (0, at + h)),
                pl.BlockSpec((ROWS, lanes), lambda h, f, s: (0, at + groups + h)),
                pl.BlockSpec((ROWS, lanes), lambda h, f, s: (0, at + 2 * groups + h)),
                pl.BlockSpec((ROWS, 2 * PAIRS * FEW), lambda h, f, s: (0, 0)),
            ]
            + [pl.BlockSpec(memory_space=pl.ANY)] * len(more),
            out_specs=[
                pl.BlockSpec((ROWS, lanes), lambda h, f, s: (0, at + h)),
                pl.BlockSpec((1, 2 * PAIRS, BODY), lambda h, f, s: (h, 0, 0)),
                pl.BlockSpec((1, 1, 2 * PAIRS * FEW), lambda h, f, s: (h, 0, 0)),
            ],
            scratch_shapes=[pltpu.VMEM((lanes, ROWS), bf16)],
        ),
        out_shape=(
            jax.ShapeDtypeStruct((ROWS, width), bf16),
            jax.ShapeDtypeStruct((some, 2 * PAIRS, BODY), f32),
            jax.ShapeDtypeStruct((some, 1, 2 * PAIRS * FEW), f32),
        ),
        input_output_aliases=alias,
        compiler_params=pltpu.CompilerParams(vmem_limit_bytes=vmem_most),
        cost_estimate=cost(6.4 * some),
    )(seen, qkv, qkv, qkv, hide, *more)


def unturn(x, cosine, sine, partner):
    return x * cosine - dot_n(x.astype(bf16), partner) * sine


def attend_back_kernel(
    scale, seen_ref, q_ref, k_ref, v_ref, o_ref, g_ref, lse_ref, few_ref, hide_ref, cos_ref, sin_ref,
    part_ref, out_ref, kt, dq, dk, dv,
):
    f = pl.program_id(1)
    heads = q_ref.shape[1] // HEAD
    pairs = [slice(p * 2 * HEAD, (p + 1) * 2 * HEAD) for p in range(heads // 2)]
    ones = jnp.where(
        (lax.broadcasted_iota(jnp.int32, (8, 2 * HEAD), 1) >= HEAD).astype(jnp.int32)
        == lax.broadcasted_iota(jnp.int32, (8, 2 * HEAD), 0),
        1.0,
        0.0,
    ).astype(bf16)

    @pl.when(f == 0)
    def _():
        kt[...] = k_ref[...].T
        qs = stack_heads(q_ref[BODY:ROWS, :].astype(f32)[:FEW]).astype(bf16)
        gs = stack_heads(g_ref[BODY:ROWS, :].astype(f32)[:FEW]).astype(bf16)
        p = jnp.exp(dot_t(k_ref[...], qs) + hide_ref[...] - few_ref[0])
        gp = dot_t(v_ref[...], gs)
        delta = jnp.sum(gp * p, axis=0, keepdims=True)
        ds = (p * (gp - delta)).astype(bf16)
        dv[...] = dot_n(p.astype(bf16), gs)
        dk[...] = dot_n(ds, qs)
        dq[BODY:ROWS, :] = few_rows(join_heads(dot_tl(ds, k_ref[...])))

    row = pl.multiple_of(f * PATCH, PATCH)
    seen = seen_ref[f]

    @pl.when(seen == 0)
    def _():
        dv[pl.ds(row, PATCH), :] += g_ref[pl.ds(row, PATCH), :].astype(f32)
        dq[pl.ds(row, PATCH), :] = jnp.zeros((PATCH, heads * HEAD), f32)

    for n in range(1, FRAMES + 1):

        @pl.when(seen == n)
        def _(n=n):
            first = f - (n - 1)
            lo = pl.multiple_of(first * PATCH, PATCH)
            count = n * PATCH

            def start(a):
                lanes = pair_lanes(a)
                q = keep_head(q_ref[pl.ds(row, PATCH), lanes], a % 2)
                g = keep_head(g_ref[pl.ds(row, PATCH), lanes], a % 2)
                s = hide_few(dot_t(seen_rows(k_ref, lanes, lo, n), q), first, f)
                return q, g, s, dot_t(seen_rows(v_ref, lanes, lo, n), g)

            deltas = []
            for lanes in pairs:
                g = g_ref[pl.ds(row, PATCH), lanes].astype(f32)
                product = g * o_ref[pl.ds(row, PATCH), lanes].astype(f32)
                upper = product.astype(bf16)
                lower = (product - upper.astype(f32)).astype(bf16)
                deltas.append(dot_t(ones, upper) + dot_t(ones, lower))
            ahead = 4
            started = [start(a) for a in range(ahead)]
            back, add_k, add_v = [], None, None
            for a in range(heads):
                q, g, s, gp = started[a]
                p = jnp.exp(s - lse_ref[0, a : a + 1, pl.ds(row, PATCH)])
                ds = (p * (gp - deltas[a // 2][a % 2 : a % 2 + 1])).astype(bf16)
                p = p.astype(bf16)
                if a + ahead < heads:
                    started.append(start(a + ahead))
                more_v, more_k = dot_n(p, g), dot_n(ds, q)
                back.append(dot_n(seen_lanes(kt, a, lo, n), ds))
                if a % 2 == 0:
                    add_v, add_k = more_v, more_k
                else:
                    lanes = pairs[a // 2]
                    add_v, add_k = add_v + more_v, add_k + more_k
                    dk[pl.ds(lo, count), lanes] += add_k[:count]
                    dk[BODY:ROWS, lanes] += add_k[count:]
                    dv[pl.ds(lo, count), lanes] += add_v[:count]
                    dv[BODY:ROWS, lanes] += add_v[count:]
            dq[pl.ds(row, PATCH), :] = jnp.concatenate(back, axis=0).T

    @pl.when(f == FRAMES - 1)
    def _():
        partner = part_ref[...]
        for lanes in pairs:
            out_ref[0, :, lanes] = unturn(
                dq[:, lanes] * scale, cos_ref[...], sin_ref[...], partner
            ).astype(bf16)
            out_ref[1, :, lanes] = unturn(
                dk[:, lanes], cos_ref[...], sin_ref[...], partner
            ).astype(bf16)
        out_ref[2] = dv[...].astype(bf16)


def attend_back(
    seen, qkv, attended, grad, lse, few, hide, cosine, sine, partner, pair_lo, pair_hi, kept=None
):
    width = qkv.shape[1] // 3
    pair = 2 * HEAD
    lanes = pair * PAIRS
    groups = width // lanes
    at = pair_lo // PAIRS
    some = (pair_hi - pair_lo) // PAIRS
    inner = functools.partial(attend_back_kernel, 1.0 / math.sqrt(HEAD))
    kernel = inner
    more, alias = [], {}
    if kept is not None:
        more, alias = [kept], {12: 0}

        def kernel(*refs):
            inner(*refs[:12], *refs[13:])

    def whole(h, f, s):
        return (0, 0)

    return pl.pallas_call(
        kernel,
        grid_spec=pltpu.PrefetchScalarGridSpec(
            num_scalar_prefetch=1,
            grid=(some, FRAMES),
            in_specs=[
                pl.BlockSpec((ROWS, lanes), lambda h, f, s: (0, at + h)),
                pl.BlockSpec((ROWS, lanes), lambda h, f, s: (0, at + groups + h)),
                pl.BlockSpec((ROWS, lanes), lambda h, f, s: (0, at + 2 * groups + h)),
                pl.BlockSpec((ROWS, lanes), lambda h, f, s: (0, at + h)),
                pl.BlockSpec((ROWS, lanes), lambda h, f, s: (0, at + h)),
                pl.BlockSpec((1, 2 * PAIRS, BODY), lambda h, f, s: (h, 0, 0)),
                pl.BlockSpec((1, 1, 2 * PAIRS * FEW), lambda h, f, s: (h, 0, 0)),
                pl.BlockSpec((ROWS, 2 * PAIRS * FEW), whole),
                pl.BlockSpec((ROWS, pair), whole),
                pl.BlockSpec((ROWS, pair), whole),
                pl.BlockSpec((pair, pair), whole),
            ]
            + [pl.BlockSpec(memory_space=pl.ANY)] * len(more),
            out_specs=pl.BlockSpec((3, ROWS, lanes), lambda h, f, s: (0, 0, at + h)),
            scratch_shapes=[
                pltpu.VMEM((lanes, ROWS), bf16),
                pltpu.VMEM((ROWS, lanes), f32),
                pltpu.VMEM((ROWS, lanes), f32),
                pltpu.VMEM((ROWS, lanes), f32),
            ],
        ),
        out_shape=jax.ShapeDtypeStruct((3, ROWS, width), bf16),
        input_output_aliases=alias,
        compiler_params=pltpu.CompilerParams(vmem_limit_bytes=vmem_most),
        cost_estimate=cost(7.6 * some),
    )(seen, qkv, qkv, qkv, attended, grad, lse, few, hide, cosine, sine, partner, *more)


def project_kernel(scale, x_ref, w_ref, b_ref, cos_ref, sin_ref, part_ref, out_ref):
    j = pl.program_id(0)
    third = pl.num_programs(0) // 3
    lanes = 2 * HEAD
    wide = part_ref.shape[0]
    w = w_ref[...]
    mixed = dot_n(x_ref[...], w) + b_ref[...]

    @pl.when(j < 2 * third)
    def _():
        by = jnp.where(j < third, scale, 1.0)
        for left in range(0, w.shape[1], wide):
            x = mixed[:, left : left + wide]
            upper = x.astype(bf16)
            lower = (x - upper.astype(f32)).astype(bf16)
            other = dot_n(upper, part_ref[...]) + dot_n(lower, part_ref[...])
            for at in range(0, wide, lanes):
                here = mixed[:, left + at : left + at + lanes] * cos_ref[...]
                there = other[:, at : at + lanes] * sin_ref[...]
                out_ref[:, left + at : left + at + lanes] = ((here + there) * by).astype(bf16)

    @pl.when(j >= 2 * third)
    def _():
        out_ref[...] = mixed.astype(bf16)


def project(x, w, bias, cosine, sine, partner):
    rows, width = x.shape
    cols = 512
    lanes = 2 * HEAD
    wide = 2 * lanes
    zero = jnp.zeros_like(partner)
    partner = jnp.block([[partner, zero], [zero, partner]])

    def whole(j):
        return (0, 0)

    return pl.pallas_call(
        functools.partial(project_kernel, 1.0 / math.sqrt(HEAD)),
        grid=(w.shape[1] // cols,),
        in_specs=[
            pl.BlockSpec((rows, width), whole),
            pl.BlockSpec((width, cols), lambda j: (0, j)),
            pl.BlockSpec((1, cols), lambda j: (0, j)),
            pl.BlockSpec((rows, lanes), whole),
            pl.BlockSpec((rows, lanes), whole),
            pl.BlockSpec((wide, wide), whole),
        ],
        out_specs=pl.BlockSpec((rows, cols), lambda j: (0, j)),
        out_shape=jax.ShapeDtypeStruct((rows, w.shape[1]), bf16),
        compiler_params=pltpu.CompilerParams(vmem_limit_bytes=vmem_most),
        cost_estimate=cost(4),
    )(x, w, bias, cosine, sine, partner)


def turn_tables(frame_ids):
    frequency, which, sign = [], [], []
    for kind, part in enumerate(part_sizes):
        half = part // 2
        frequency += [10000.0 ** (-i / half) for i in range(half)] * 2
        which += [kind] * part
        sign += [-1.0] * half + [1.0] * half
    frequency = jnp.asarray(np.tile(np.array(frequency, np.float32), 2))
    which = np.tile(np.array(which), 2)
    sign = np.tile(np.array(sign, np.float32), 2)
    time = frame_ids[:: FRAME_ROWS].astype(f32)[:, None] * frequency
    place = np.arange(GRID, dtype=np.float32)[:, None] * frequency

    def table(of, empty):
        by_time, by_place = of(time), of(place)
        still = jnp.full((FRAMES, 2, which.size), empty, f32)
        patches = jnp.where(which == 1, by_place[:, None], by_place[None]).reshape(1, PATCH, -1)
        patches = jnp.where(which == 0, by_time[:, None], patches).reshape(BODY, -1)
        few = jnp.where(which == 0, by_time[:, None], still).reshape(FEW, -1)
        return jnp.concatenate([patches, few, jnp.zeros_like(few)], axis=0)

    return table(jnp.cos, 1.0), table(lambda v: jnp.sin(v) * sign, 0.0)


def partner_matrix():
    lanes = 2 * HEAD
    matrix = np.zeros((lanes, lanes), np.float32)
    for head in range(2):
        at = head * HEAD
        for part in part_sizes:
            for i in range(part // 2):
                matrix[at + i, at + i + part // 2] = 1.0
                matrix[at + i + part // 2, at + i] = 1.0
            at += part
    return jnp.asarray(matrix, bf16)


def seen_frames(offset_row):
    frame = jnp.arange(FRAMES, dtype=jnp.int32)
    start = jnp.where(frame >= offset_row[1], offset_row[1], 0)
    return jnp.where(frame < offset_row[2], frame - start + 1, 0)


def hidden_few(seen):
    frame_of = np.concatenate([np.repeat(np.arange(FRAMES), PATCH), np.repeat(np.arange(FRAMES), 2), np.full(EXTRA - FEW, FRAMES)])
    own = np.zeros((ROWS, FEW), bool)
    own[BODY + np.arange(FEW), np.arange(FEW)] = True
    frame = jnp.asarray(frame_of, jnp.int32)[:, None]
    query = jnp.arange(FEW, dtype=jnp.int32)[None, :] // 2
    count = jnp.repeat(seen, 2)[None, :]
    allowed = ((frame <= query) & (frame > query - count)) | jnp.asarray(own)
    return jnp.tile(jnp.where(allowed, 0.0, masked_value), (1, 2 * PAIRS))


def place(p, line, orders, core):
    own, other = relatives(line, orders, core)
    return (1, other.index(p)) if p in other else (0, own.index(p))


def find_piece(rels, p):
    for c, rel in enumerate(rels):
        if p in rel:
            return c, rel.index(p)
    raise ValueError(p)


def feed_kernel(
    rels, where, me_ref, x_ref, g_ref, bias_ref, shift_ref, mid_ref, up_ref, *refs
):
    pieces, refs = refs[: len(rels)], refs[len(rels) :]
    out_ref, gx_ref, gb_ref = refs[:3]
    grads = refs[3:5]
    wu, wd, su, sd, acc, xt, act, gup, in_sem, out_sem, mid_sem = refs[5:]
    count = sum(len(q) for q in rels)
    blocks = FEED_BLOCKS
    each = count // blocks
    shift = each.bit_length() - 1
    i = pl.program_id(0)
    me = me_ref[0]
    width = x_ref.shape[1]
    cols = wu.shape[2]
    rows = width // count
    part = cols // each
    hidden = blocks * cols
    stacks = part // rows
    slot = lax.rem(i, 2)

    def group(j):
        return lax.bitwise_xor(lax.shift_right_logical(me, shift), j)

    def fetch(j, to):
        at = pl.multiple_of(group(j) * cols, cols)
        pltpu.make_async_copy(up_ref.at[:, pl.ds(at, cols)], wu.at[to], in_sem.at[0, to]).start()
        for k in range(blocks):

            @pl.when(j == k)
            def _():
                for p in range(each):
                    c, n = find_piece(rels, (k << shift) | p)
                    start = pl.multiple_of(lax.bitwise_xor(me & (each - 1), p) * part, part)
                    for q in range(stacks):
                        pltpu.make_async_copy(
                            pieces[c].at[n, :, pl.ds(q * width, width)],
                            wd.at[to, pl.ds(start + q * rows, rows), :],
                            in_sem.at[1, to],
                        ).start()

    middle = pltpu.make_async_copy(mid_ref, acc, mid_sem)

    @pl.when(i == 0)
    def _():
        fetch(i, slot)
        middle.start()
        xt[...] = x_ref[...].T
        gx_ref[...] = jnp.zeros_like(gx_ref)

    @pl.when(i + 1 < blocks)
    def _():
        fetch(i + 1, 1 - slot)

    pltpu.make_async_copy(wu.at[slot], wu.at[slot], in_sem.at[0, slot]).wait()
    pltpu.make_async_copy(wd.at[slot], wd.at[slot], in_sem.at[1, slot]).wait()
    half = cols // 2
    low, high = slice(0, half), slice(half, cols)

    def curves(u, ga):
        e = jnp.exp2(u * u * (-0.5 * math.log2(math.e)))
        d = 1.0 + jnp.abs(u) * (0.3275911 * inv_sqrt_two)
        t = pl.reciprocal(d, approx=True)
        t = t * (2.0 - d * t)
        poly = t * (0.127414796 + t * (-0.142248368 + t * (0.7107068705 + t * (-0.7265760135 + t * 0.5307027145))))
        tail = poly * e
        phi = jnp.where(u >= 0.0, 1.0 - tail, tail)
        gu = ga * (phi + u * (e * inv_sqrt_tau))
        return (u * phi).astype(bf16), gu.astype(bf16), jnp.sum(gu, axis=0, keepdims=True)

    u0 = dot_n(x_ref[...], wu[slot, :, low]) + bias_ref[:, low]
    g0 = dot_t(g_ref[...], wd[slot, low, :])
    u1 = dot_n(x_ref[...], wu[slot, :, high]) + bias_ref[:, high]
    g1 = dot_t(g_ref[...], wd[slot, high, :])
    a, g, total = curves(u0, g0)
    act[:, low] = a
    gup[:, low] = g
    gb_ref[:, low] = total

    @pl.when(i >= 2)
    def _():
        pltpu.make_async_copy(su.at[slot], su.at[slot], out_sem.at[0, slot]).wait()
        pltpu.make_async_copy(sd.at[slot], sd.at[slot], out_sem.at[1, slot]).wait()

    @pl.when(i == 0)
    def _():
        middle.wait()

    a, g, total = curves(u1, g1)
    act[:, high] = a
    gup[:, high] = g
    gb_ref[:, high] = total
    sd[slot] = dot_tl(act[...], g_ref[...]).astype(bf16)
    su[slot] = dot_n(xt[...], gup[...]).astype(bf16)
    acc[...] += dot_n(act[...], wd[slot])
    gx_ref[...] += dot_t(gup[...], wu[slot])
    at = pl.multiple_of(group(i) * cols, cols)
    for p in range(count):
        c, n = place(p, *where)
        start = pl.multiple_of(lax.bitwise_xor(me, p) * rows, rows)
        pltpu.make_async_copy(
            su.at[slot, pl.ds(start, rows), :],
            grads[c].at[n, :, pl.ds(at, cols)],
            out_sem.at[0, slot],
        ).start()
    for k in range(blocks):

        @pl.when(i == k)
        def _():
            for p in range(each):
                c, n = place((k << shift) | p, *where)
                start = pl.multiple_of(lax.bitwise_xor(me & (each - 1), p) * part, part)
                for q in range(stacks):
                    pltpu.make_async_copy(
                        sd.at[slot, pl.ds(start + q * rows, rows), :],
                        grads[c].at[n, :, pl.ds(hidden + q * width, width)],
                        out_sem.at[1, slot],
                    ).start()

    @pl.when(i == blocks - 1)
    def _():
        out_ref[...] = (acc[...] + shift_ref[...]).astype(bf16)
        for s in range(2):
            pltpu.make_async_copy(su.at[s], su.at[s], out_sem.at[0, s]).wait()
            pltpu.make_async_copy(sd.at[s], sd.at[s], out_sem.at[1, s]).wait()


FEED_BLOCKS = 4


def feed(x, grad, middle, bias, shift, up, pieces, line, orders, core, me):
    rels = [q for _, q in pieces]
    count = sum(len(q) for q in rels)
    tokens, width = x.shape
    hidden = bias.shape[1]
    cols = hidden // FEED_BLOCKS
    shift_by = (count // FEED_BLOCKS).bit_length() - 1

    def block(i, me_ref):
        return (0, lax.bitwise_xor(lax.shift_right_logical(me_ref[0], shift_by), i))

    def whole(i, me_ref):
        return (0, 0)

    once = pl.Buffered(1)
    anywhere = pl.BlockSpec(memory_space=pl.ANY)
    return pl.pallas_call(
        functools.partial(feed_kernel, rels, (line, orders, core)),
        grid_spec=pltpu.PrefetchScalarGridSpec(
            num_scalar_prefetch=1,
            grid=(FEED_BLOCKS,),
            in_specs=[
                pl.BlockSpec((tokens, width), whole, pipeline_mode=once),
                pl.BlockSpec((tokens, width), whole, pipeline_mode=once),
                pl.BlockSpec((1, cols), block),
                pl.BlockSpec((1, width), whole),
                anywhere,
                anywhere,
            ]
            + [anywhere] * len(pieces),
            out_specs=[
                pl.BlockSpec((tokens, width), whole, pipeline_mode=once),
                pl.BlockSpec((tokens, width), whole, pipeline_mode=once),
                pl.BlockSpec((1, cols), block),
            ]
            + [anywhere] * 2,
            scratch_shapes=[
                pltpu.VMEM((2, width, cols), bf16),
                pltpu.VMEM((2, cols, width), bf16),
                pltpu.VMEM((2, width, cols), bf16),
                pltpu.VMEM((2, cols, width), bf16),
                pltpu.VMEM((tokens, width), f32),
                pltpu.VMEM((width, tokens), bf16),
                pltpu.VMEM((tokens, cols), bf16),
                pltpu.VMEM((tokens, cols), bf16),
                pltpu.SemaphoreType.DMA((2, 2)),
                pltpu.SemaphoreType.DMA((2, 2)),
                pltpu.SemaphoreType.DMA,
            ],
        ),
        out_shape=[
            jax.ShapeDtypeStruct((tokens, width), bf16),
            jax.ShapeDtypeStruct((tokens, width), f32),
            jax.ShapeDtypeStruct((1, hidden), f32),
        ]
        + [jax.ShapeDtypeStruct((count // 2, width // count, 2 * hidden), bf16)] * 2,
        compiler_params=pltpu.CompilerParams(vmem_limit_bytes=vmem_most),
        cost_estimate=cost(20),
    )(me, x, grad, bias, shift, middle, up, *[v for v, _ in pieces])


def weight_kernel(where, left, count, me_ref, x_ref, g_ref, *refs):
    outs, (xt, staged, sem) = refs[-5:-3], refs[-3:]
    j = pl.program_id(0)
    me = me_ref[0]
    slot = lax.rem(j, 2)
    width, cols = staged.shape[1:]
    rows = width // count

    @pl.when(j == 0)
    def _():
        xt[...] = x_ref[...].T

    @pl.when(j >= 2)
    def _():
        pltpu.make_async_copy(staged.at[slot], staged.at[slot], sem.at[slot]).wait()

    staged[slot] = dot_n(xt[...], g_ref[...].reshape(g_ref.shape[-2:])).astype(bf16)
    at = pl.multiple_of(left + j * cols, cols)
    for out, rel in zip(outs, where):
        for n, p in enumerate(rel):
            start = pl.multiple_of(lax.bitwise_xor(me, p) * rows, rows)
            pltpu.make_async_copy(
                staged.at[slot, pl.ds(start, rows), :], out.at[n, :, pl.ds(at, cols)], sem.at[slot]
            ).start()

    @pl.when(j == pl.num_programs(0) - 1)
    def _():
        for s in range(2):
            pltpu.make_async_copy(staged.at[s], staged.at[s], sem.at[s]).wait()


def weight_grad(x, grad, where, left, total, me, into=()):
    tokens, width = x.shape
    count = sum(len(q) for q in where)
    cols = 512
    deep = grad.ndim == 3
    found = grad.shape[-1] * (grad.shape[0] if deep else 1)
    per = grad.shape[-1] // cols
    if deep:
        spec = pl.BlockSpec((1, tokens, cols), lambda j, m: (j // per, 0, j % per))
    else:
        spec = pl.BlockSpec((tokens, cols), lambda j, m: (0, j))
    anywhere = pl.BlockSpec(memory_space=pl.ANY)
    return pl.pallas_call(
        functools.partial(weight_kernel, where, left, count),
        grid_spec=pltpu.PrefetchScalarGridSpec(
            num_scalar_prefetch=1,
            grid=(found // cols,),
            in_specs=[pl.BlockSpec((tokens, width), lambda j, m: (0, 0)), spec]
            + [anywhere] * len(into),
            out_specs=[anywhere] * 2,
            scratch_shapes=[
                pltpu.VMEM((width, tokens), bf16),
                pltpu.VMEM((2, width, cols), bf16),
                pltpu.SemaphoreType.DMA((2,)),
            ],
        ),
        out_shape=[jax.ShapeDtypeStruct((count // 2, width // count, total), bf16)] * 2,
        input_output_aliases={3 + i: i for i in range(len(into))},
        compiler_params=pltpu.CompilerParams(vmem_limit_bytes=vmem_most),
        cost_estimate=cost(0.5 * found / 512),
    )(me, x, grad, *into)


def sort_kernel(x_ref, g_ref, x_out, g_out, sum_ref, wide):
    for source, target in ((x_ref, x_out), (g_ref, g_out)):
        wide[...] = source[...].astype(f32)
        for f in range(FRAMES):
            at = f * FRAME_ROWS + 2
            target[f * PATCH : (f + 1) * PATCH, :] = wide[at : at + PATCH, :].astype(bf16)
        few = [wide[f * FRAME_ROWS : f * FRAME_ROWS + 2, :] for f in range(FRAMES)]
        few = jnp.concatenate(few + [jnp.zeros((EXTRA - FEW, wide.shape[1]), f32)], axis=0)
        target[BODY:ROWS, :] = few.astype(bf16)
    sum_ref[...] = jnp.sum(wide[...], axis=0, keepdims=True)


def sort_rows(x, grad):
    tokens, width = x.shape
    return pl.pallas_call(
        sort_kernel,
        out_shape=[jax.ShapeDtypeStruct((ROWS, width), bf16)] * 2
        + [jax.ShapeDtypeStruct((1, width), f32)],
        scratch_shapes=[pltpu.VMEM((tokens, width), f32)],
        compiler_params=pltpu.CompilerParams(vmem_limit_bytes=vmem_most),
        cost_estimate=cost(1),
    )(x, grad)


def unsort_kernel(x_ref, out_ref, *scratch):
    wide = scratch[0] if scratch else out_ref
    for f in range(FRAMES):
        at = f * FRAME_ROWS
        wide[at + 2 : at + FRAME_ROWS, :] = x_ref[f * PATCH : (f + 1) * PATCH, :].astype(f32)
    few = x_ref[BODY:ROWS, :].astype(f32)
    for f in range(FRAMES):
        wide[f * FRAME_ROWS : f * FRAME_ROWS + 2, :] = few[2 * f : 2 * f + 2]
    if scratch:
        out_ref[...] = wide[...].astype(out_ref.dtype)


def unsort_rows(x):
    tokens, width = FRAMES * FRAME_ROWS, x.shape[1]
    return pl.pallas_call(
        unsort_kernel,
        out_shape=jax.ShapeDtypeStruct((tokens, width), x.dtype),
        scratch_shapes=[] if x.dtype == f32 else [pltpu.VMEM((tokens, width), f32)],
        compiler_params=pltpu.CompilerParams(vmem_limit_bytes=vmem_most),
        cost_estimate=cost(1),
    )(x)


def last_kernel(
    g_ref, w_ref, x_any, mid_any, gain_ref, out_ref, sum_ref, acc, x_ref, mid_ref, sems
):
    i = pl.program_id(0)
    copies = [
        pltpu.make_async_copy(x_any, x_ref, sems.at[0]),
        pltpu.make_async_copy(mid_any, mid_ref, sems.at[1]),
    ]

    @pl.when(i == 0)
    def _():
        for copy in copies:
            copy.start()

    g = g_ref[0]
    more = dot_t(g, w_ref[...])

    @pl.when(i == 0)
    def _():
        acc[...] = more

    @pl.when(i > 0)
    def _():
        acc[...] += more

    sum_ref[pl.ds(2 + i, 1), :] = jnp.sum(g.astype(f32), axis=0, keepdims=True)

    @pl.when(i == pl.num_programs(0) - 1)
    def _():
        for copy in copies:
            copy.wait()
        gain = gain_ref[...]
        gain_sum, bias_sum = 0.0, 0.0
        spans = [(f * PATCH, PATCH) for f in range(FRAMES)] + [(BODY, EXTRA)]
        for at, size in spans:
            rows = slice(at, at + size)
            x = x_ref[rows, :].astype(f32)
            center = x - jnp.mean(x, axis=-1, keepdims=True)
            inverse = lax.rsqrt(jnp.mean(center * center, axis=-1, keepdims=True) + eps_norm)
            unit = center * inverse
            grad = acc[rows, :]
            gain_sum += jnp.sum(grad * unit, axis=0, keepdims=True)
            bias_sum += jnp.sum(grad, axis=0, keepdims=True)
            scaled = grad * gain
            mean_grad = jnp.mean(scaled, axis=-1, keepdims=True)
            mean_cross = jnp.mean(scaled * unit, axis=-1, keepdims=True)
            found = mid_ref[rows, :] + inverse * (scaled - mean_grad - unit * mean_cross)
            if size == PATCH:
                start = at // PATCH * FRAME_ROWS + 2
                out_ref[start : start + PATCH, :] = found
            else:
                for f in range(FRAMES):
                    out_ref[f * FRAME_ROWS : f * FRAME_ROWS + 2, :] = found[2 * f : 2 * f + 2]
        sum_ref[0:1, :] = gain_sum
        sum_ref[1:2, :] = bias_sum


def last_step(grad_mixed, w, x, middle, gain):
    parts, rows, width = grad_mixed.shape

    def whole(i):
        return (0, 0)

    once = pl.Buffered(1)
    return pl.pallas_call(
        last_kernel,
        grid=(parts,),
        in_specs=[
            pl.BlockSpec((1, rows, width), lambda i: (i, 0, 0)),
            pl.BlockSpec((width, width), lambda i: (0, i)),
            pl.BlockSpec(memory_space=pl.ANY),
            pl.BlockSpec(memory_space=pl.ANY),
            pl.BlockSpec((1, width), whole),
        ],
        out_specs=[
            pl.BlockSpec((FRAMES * FRAME_ROWS, width), whole, pipeline_mode=once),
            pl.BlockSpec((8, width), whole),
        ],
        out_shape=[
            jax.ShapeDtypeStruct((FRAMES * FRAME_ROWS, width), f32),
            jax.ShapeDtypeStruct((8, width), f32),
        ],
        scratch_shapes=[
            pltpu.VMEM((rows, width), f32),
            pltpu.VMEM((rows, width), bf16),
            pltpu.VMEM((rows, width), f32),
            pltpu.SemaphoreType.DMA((2,)),
        ],
        compiler_params=pltpu.CompilerParams(vmem_limit_bytes=vmem_most),
        cost_estimate=cost(5),
    )(grad_mixed, w, x, middle, gain)


def normalize(values, gain, bias_add):
    center = values - jnp.mean(values, axis=-1, keepdims=True)
    scale_inv = lax.rsqrt(jnp.mean(center * center, axis=-1, keepdims=True) + eps_norm)
    unit_rows = center * scale_inv
    return (unit_rows * gain + bias_add, unit_rows, scale_inv)


def norm_back(grad_out, unit_rows, scale_inv, gain):
    scaled = grad_out * gain
    mean_grad = jnp.mean(scaled, axis=-1, keepdims=True)
    mean_cross = jnp.mean(scaled * unit_rows, axis=-1, keepdims=True)
    return scale_inv * (scaled - mean_grad - unit_rows * mean_cross)


def gather_joined(groups, orders, core, sizes):
    found = []
    for pieces, order in zip(groups, orders):
        for bit in order[:-1]:
            pieces = pieces + moved(pieces, bit, sizes)
        arrays, rels = zip(*pieces)
        pieces = [(jnp.concatenate(arrays, axis=0), sum(rels, []))]
        found += pieces + moved(pieces, order[-1], sizes)
    return found + moved(found, core, sizes)


def gather_rest(groups, orders, core, sizes):
    found = []
    for pieces, order in zip(groups, orders):
        for bit in order:
            pieces = pieces + moved(pieces, bit, sizes)
        found += pieces
    return found + moved(found, core, sizes)


def body(
    sizes,
    tokens,
    frame_ids,
    pad_mask,
    episode_offsets,
    ln1_gain,
    ln1_bias,
    w_qkv,
    b_qkv,
    w_out,
    b_out,
    ln2_gain,
    ln2_bias,
    w_up,
    b_up,
    w_down,
    b_down,
    cotangent,
):
    width = tokens.shape[1]
    count = sizes[0] * sizes[1]
    me = (lax.axis_index("dp") * sizes[1] + lax.axis_index("fsdp")).astype(jnp.int32)[None]
    core, line, orders = bit_orders(sizes)
    where = relatives(line, orders, core)
    out_matrix = lax.all_gather(w_out, ("dp", "fsdp"), axis=0, tiled=True)
    up_matrix = lax.all_gather(w_up, ("dp", "fsdp"), axis=0, tiled=True)
    smalls = [ln1_gain, ln1_bias, b_qkv, b_out, ln2_gain, ln2_bias, b_up, b_down]
    rows, third = w_qkv.shape
    first_unit = jnp.concatenate([w_qkv, pack_small(smalls, rows)], axis=1)
    firsts = gather_line(first_unit, line, sizes)
    tokens_in, cot, grad_b_down_local = sort_rows(tokens, cotangent)
    first = gather_joined(firsts, orders, core, sizes)
    seen = seen_frames(episode_offsets[0])
    hide = hidden_few(seen)
    cosine, sine = turn_tables(frame_ids)
    partner = partner_matrix()
    values_in = tokens_in.astype(f32)
    qkv_matrix, whole_small = assemble(
        first, me, [(0, rows, 0, third), (0, rows, third, first_unit.shape[1] - third)]
    )
    gain_one, bias_one, qkv_rows, *_ = unpack_small(whole_small, rows, smalls)
    stacked = [w_down[at : at + rows] for at in range(0, w_down.shape[0], rows)]
    second_unit = after(jnp.concatenate(stacked, axis=1), first[0][0], first[2][0])
    seconds = gather_line(second_unit, line, sizes)
    normed_one, unit_one, inv_one = normalize(values_in, gain_one, bias_one)
    normed_one = normed_one.astype(bf16)
    qkv = project(normed_one, qkv_matrix, qkv_rows.reshape(1, 3 * width), cosine, sine, partner)
    pairs = width // (2 * HEAD)
    seconds = [after_pieces(pieces, qkv_matrix) for pieces in seconds]
    seconds = [
        [pieces, moved(pieces, order[0], sizes) + moved(pieces, order[1], sizes)]
        for pieces, order in zip(seconds, orders)
    ]
    attended, lse_a, few_a = attend(seen, qkv, hide, 0, pairs // 2)
    seconds = [[near, after_pieces(far, attended)] for near, far in seconds]
    found = []
    for (near, far), order in zip(seconds, orders):
        pieces = near + far + moved(far[:1], order[1], sizes)
        for bit in order[2:]:
            pieces = pieces + moved(pieces, bit, sizes)
        found.append(pieces)
    attended, lse_b, few_b = attend(seen, qkv, hide, pairs // 2, pairs, attended)
    second = []
    for pieces in found:
        arrays, rels = zip(*pieces)
        pieces = [(after(jnp.concatenate(arrays, axis=0), attended), sum(rels, []))]
        second += pieces + moved(pieces, core, sizes)
    whole_small = after(whole_small, attended)
    *_, out_bias, gain_two, bias_two, up_bias, down_bias = unpack_small(whole_small, rows, smalls)
    hidden = w_up.shape[1]
    middle = values_in + jnp.dot(attended, out_matrix, preferred_element_type=f32) + out_bias
    normed_two, unit_two, inv_two = normalize(middle, gain_two, bias_two)
    normed_two = normed_two.astype(bf16)
    result, grad_normed_two, grad_b_up_local, feed_own, feed_other = feed(
        normed_two,
        cot,
        middle,
        up_bias[None],
        down_bias[None],
        up_matrix,
        second,
        line,
        orders,
        core,
        me,
    )
    feed_taken = swap(feed_other, 1 << core, sizes)
    grad_gain_two = jnp.sum(grad_normed_two * unit_two, axis=0)
    grad_bias_two = jnp.sum(grad_normed_two, axis=0)
    grad_middle = cot.astype(f32) + norm_back(grad_normed_two, unit_two, inv_two, gain_two)
    grad_branch = grad_middle.astype(bf16)
    grad_b_out_local = jnp.sum(grad_branch.astype(f32), axis=0)
    grad_attended = dot_t(grad_branch, out_matrix).astype(bf16)
    feed_own = after(feed_own, grad_attended)
    feed_sums = reduce_start(feed_own, feed_taken, orders, sizes)
    grad_attended = after(grad_attended, *[v for group in feed_sums for v in group[:1] + group[2:]])
    feed_sums = [group[:2] for group in feed_sums]
    back = (hide, cosine, sine, partner)
    grad_mixed = attend_back(
        seen, qkv, attended, grad_attended, lse_a, few_a, *back, 0, pairs // 2
    )
    grad_mixed = attend_back(
        seen, qkv, attended, grad_attended, lse_b, few_b, *back, pairs // 2, pairs, grad_mixed
    )
    steps = len(orders[0])
    for step in range(1, steps):
        feed_sums = together(feed_sums, grad_mixed)
        feed_sums = reduce_next(feed_sums, orders, step, sizes)
        grad_mixed = after(grad_mixed, *[v for group in feed_sums for v in group[:1] + group[2:]])
        feed_sums = [group[:2] for group in feed_sums]
    grads = weight_grad(normed_one, grad_mixed, where, 0, third + width, me)
    own, other = weight_grad(attended, grad_branch, where, third, third + width, me, grads)
    taken = swap(other, 1 << core, sizes)
    feed_parts = line_parts(together(feed_sums))
    feed_parts = feed_parts[:1] + [v.astype(bf16) for v in feed_parts[1:]]
    own = after(own, *feed_parts[1:])
    sums = reduce_start(own, taken, orders, sizes)
    going = [v for group in sums for v in group[:1] + group[2:]]
    sums = [group[:2] for group in sums]
    grad_mixed = after(grad_mixed, *going)
    grad_tokens, late_sums = last_step(
        grad_mixed, qkv_matrix, tokens_in, grad_middle, gain_one[None]
    )
    vectors = [
        late_sums[:5],
        jnp.stack([grad_b_out_local, grad_gain_two, grad_bias_two, grad_b_down_local[0]]),
        grad_b_up_local[0],
    ]
    small_own, small_other = small_units(vectors, rows, where, me)
    small = jnp.concatenate([small_own, small_other], axis=2).astype(bf16)
    half = small.shape[0] // 2
    joined = []
    for (kept, came), at, order in zip(sums, (0, half), orders):
        here = small[at : at + half // 2]
        there = swap(small[at + half // 2 : at + half], 1 << order[-1], sizes)
        joined.append(
            (jnp.concatenate([kept, here], axis=2), jnp.concatenate([came, there], axis=2))
        )
    sums = joined
    for step in range(1, steps):
        sums = [group[:2] for group in reduce_next(sums, orders, step, sizes)]
    parts = line_parts(sums)
    parts = parts[:1] + [v.astype(bf16) for v in parts[1:]]
    feed_parts[0] = after(feed_parts[0], *parts[1:])
    output = unsort_rows(after(result, *parts[1:]))
    parts[0] = after(parts[0], output)
    feed_sum = reduce_line(feed_parts, line, sizes)
    sum_one = reduce_line(parts, line, sizes)
    small = sum_one[:, third + width :]
    small = small[:, :128] + swap(small[:, 128:], 1 << core, sizes)
    small = small_parts(small, vectors, count)
    sum_down = feed_sum[:, hidden:].reshape(rows, -1, width).swapaxes(0, 1).reshape(-1, width)
    return (
        output,
        grad_tokens,
        small[0][0],
        small[0][1],
        sum_one[:, :third],
        small[0][2:],
        sum_one[:, third : third + width],
        small[1][0],
        small[1][1],
        small[1][2],
        feed_sum[:, :hidden],
        small[2],
        sum_down,
        small[1][3],
    )


def solution(mesh):
    placed = (
        P(("dp", "fsdp"), None),
        P(("dp", "fsdp")),
        P(("dp", "fsdp")),
        P(("dp", "fsdp"), None),
        P(("dp", "fsdp")),
        P(("dp", "fsdp")),
        P(("dp", "fsdp"), None),
        P(None, ("dp", "fsdp")),
        P(("dp", "fsdp"), None),
        P(("dp", "fsdp")),
        P(("dp", "fsdp")),
        P(("dp", "fsdp")),
        P(("dp", "fsdp"), None),
        P(("dp", "fsdp")),
        P(("dp", "fsdp"), None),
        P(("dp", "fsdp")),
        P(("dp", "fsdp"), None),
    )
    sizes = (mesh.shape["dp"], mesh.shape["fsdp"])
    return jax.shard_map(
        functools.partial(body, sizes),
        mesh=mesh,
        in_specs=placed,
        out_specs=(
            P(("dp", "fsdp"), None),
            P(("dp", "fsdp"), None),
            P(("dp", "fsdp")),
            P(("dp", "fsdp")),
            P(("dp", "fsdp"), None),
            P(None, ("dp", "fsdp")),
            P(("dp", "fsdp"), None),
            P(("dp", "fsdp")),
            P(("dp", "fsdp")),
            P(("dp", "fsdp")),
            P(("dp", "fsdp"), None),
            P(("dp", "fsdp")),
            P(("dp", "fsdp"), None),
            P(("dp", "fsdp")),
        ),
        check_vma=False,
    )
```
